512 devices in a mesh: lat: 16 (over z_hi, x), lon: 32 (over y, z_lo, core).
Axes of the slice: x: 4, y: 8, z: 8 (z_hi: 4, z_lo: 2; z = z_hi * 2 + z_lo), core: 2. Of those that a mesh axis runs over, the one named last changes fastest.
Arguments:
- tokens: bfloat16 [2, 96, 768, 192], P(None, 'lat', 'lon'), may hold values from -30 to 30
- cotangent: bfloat16 [2, 96, 768, 192], P(None, 'lat', 'lon'), may hold values from -6 to 6
- norm_gain_vector: float32 [192], replicated, may hold values from 0.1 to 1.9
- norm_bias_vector: float32 [192], replicated, may hold values from -3 to 3
- qkv_weight: bfloat16 [192, 576], replicated, may hold values from -0.4375 to 0.4375
- qkv_bias: float32 [576], replicated, may hold values from -3 to 3
- proj_weight: bfloat16 [192, 192], replicated, may hold values from -0.4375 to 0.4375
- proj_bias: float32 [192], replicated, may hold values from -3 to 3
- earth_bias: float32 [1, 16, 6, 3312], P(None, 'lat'), may hold values from -2.5 to 300, as said below
- lat_valid: int32 [96], replicated, may hold values from 0 to 1, as said below
Outputs:
- block_out: float32 [2, 96, 768, 192], P(None, 'lat', 'lon')
- token_grad: float32 [2, 96, 768, 192], P(None, 'lat', 'lon')
- norm_gain_grad: float32 [192], replicated
- norm_shift_grad: float32 [192], replicated
- qkv_weight_grad: float32 [192, 576], replicated
- qkv_bias_grad: float32 [576], replicated
- proj_weight_grad: float32 [192, 192], replicated
- proj_bias_grad: float32 [192], replicated
- earth_bias_grad: float32 [1, 16, 6, 3312], P(None, 'lat')
The draws below stay inside these ranges and needn't reach their ends.
Inputs may be any that keep to these rules, and one draw needn't show every extreme that they name: `earth_bias`: bias tables of window types. `lat_valid`: 1 on every latitude row except the last 1 to 5 rows of the grid, which are 0.
All inputs are finite; a program needn't handle non-finite values.
Results may differ from the reference program's by a relative error of at most 0.0094.
Values may be sent and summed in bfloat16 or wider, within the bound.
No kernel may reach another device: no remote copies, remote signals or barrier semaphores. Data moves between devices by JAX's collectives and lax.ppermute only.
A program may use at most 128 MiB of HBM per device.

```python
import math
import jax
import jax.numpy as jnp
import numpy as np
from jax import lax

C = 192
HEADS = 6
WZ = 2
WLAT = 6
WLON = 12
Z = 2
NLAT = 96
NLON = 768
ZW = 1
NLATW = 16
PAIRS = 3312
TOKENS = 147456


def draw_tokens(key, part):
    key = jax.random.fold_in(key, 11)
    key_base, key_chan, key_tok = jax.random.split(key, 3)
    chan = jnp.exp(jax.random.uniform(key_chan, (C,), jnp.float32, -1.15, 1.15))
    tok = jnp.exp(jax.random.uniform(key_tok, (Z, NLAT, NLON, 1), jnp.float32, -1.15, 1.15))
    base = jnp.clip(jax.random.normal(key_base, (Z, NLAT, NLON, C), jnp.float32), -4.0, 4.0)
    return jnp.clip(base * chan * tok, -30.0, 30.0).astype(jnp.bfloat16)


def draw_earth_bias(key, part):
    key = jax.random.fold_in(key, 23)
    key_base = jax.random.fold_in(key, 0)
    shape = (ZW, NLATW, HEADS, WZ * WZ * WLAT * WLAT, 2 * WLON - 1)
    value = jnp.clip(0.5 * jax.random.normal(key_base, shape, jnp.float32), -2.5, 2.5)
    return value.reshape(ZW, NLATW, HEADS, PAIRS)


def draw_lat_valid(key, part):
    key = jax.random.fold_in(key, 37)
    padded = jax.random.randint(key, (), 1, WLAT)
    return (jnp.arange(NLAT, dtype=jnp.int32) < NLAT - padded).astype(jnp.int32)


def block_scale(own_key, shape, pieces, smallest, largest):
    level = 1.0
    for axis_at, parts in pieces:
        heights = jax.random.uniform(jax.random.fold_in(jax.random.fold_in(own_key, 6), axis_at), (parts,), jnp.float32, smallest / len(pieces), largest / len(pieces))
        level = level * jnp.repeat(jnp.exp(heights), shape[axis_at] // parts).reshape((-1,) + (1,) * (len(shape) - 1 - axis_at))
    return level


def gaussian(own_key, extent, deviation, reach, shards=(), kind=jnp.bfloat16):
    array = jax.random.normal(own_key, extent, jnp.float32) * deviation
    if len(shards) > 0:
        array = block_scale(own_key, extent, shards, -0.22, 0.18) * array
    return jnp.clip(array, min=-reach, max=reach).astype(kind)


def setup_inputs(seed: int = 0) -> dict:
    key_list = jax.random.split(jax.random.key(seed), 11)
    tokens = draw_tokens(jax.random.fold_in(key_list[10], 71), 0)
    cotangent = gaussian(key_list[1], (Z, NLAT, NLON, C), 1.0, 6.0, ((1, 16), (2, 32)))
    norm_gain_vector = jnp.clip(1.0 + 0.18 * jax.random.normal(key_list[2], (C,), jnp.float32), 0.1, 1.9)
    norm_bias_vector = gaussian(key_list[3], (C,), 0.5, 3.0, (), jnp.float32)
    qkv_weight = gaussian(key_list[4], (C, 3 * C), C ** -0.5, 0.4375)
    qkv_bias = gaussian(key_list[5], (3 * C,), 0.5, 3.0, (), jnp.float32)
    proj_weight = gaussian(key_list[6], (C, C), C ** -0.5, 0.4375)
    proj_bias = gaussian(key_list[7], (C,), 0.5, 3.0, (), jnp.float32)
    earth_bias = draw_earth_bias(jax.random.fold_in(key_list[10], 71), 0)
    lat_valid = draw_lat_valid(jax.random.fold_in(key_list[10], 71), 0)
    return dict(tokens=tokens, cotangent=cotangent, norm_gain_vector=norm_gain_vector, norm_bias_vector=norm_bias_vector, qkv_weight=qkv_weight, qkv_bias=qkv_bias, proj_weight=proj_weight, proj_bias=proj_bias, earth_bias=earth_bias, lat_valid=lat_valid)


mask_fill = -10000.0
epsilon = 1e-05
bias_factor = 8.0

def pair_index():
    position = np.arange(WZ * WLAT * WLON)
    level = position // (WLAT * WLON)
    row = position // WLON % WLAT
    column = position % WLON
    first = (level[:, None] * WZ + level[None, :]) * WLAT + row[:, None]
    second = (first * WLAT + row[None, :]) * (2 * WLON - 1)
    return (second + column[:, None] - column[None, :] + WLON - 1).astype(np.int32)

def to_windows(tile):
    levels, rows, cols, width = tile.shape
    grid = tile.reshape(levels // WZ, WZ, rows // WLAT, WLAT, cols // WLON, WLON, width)
    grid = grid.transpose(0, 2, 4, 1, 3, 5, 6)
    return grid.reshape(levels // WZ * (rows // WLAT), cols // WLON, WZ * WLAT * WLON, width)

def from_windows(blocks, levels, rows, cols):
    width = blocks.shape[-1]
    grid = blocks.reshape(levels // WZ, rows // WLAT, cols // WLON, WZ, WLAT, WLON, width)
    return grid.transpose(0, 3, 1, 4, 2, 5, 6).reshape(levels, rows, cols, width)

def attend(xw, dyw, add, norm_gain_vector, norm_bias_vector, qkv_weight, qkv_bias, proj_weight, proj_bias):
    f32 = jnp.float32
    half_width = jnp.bfloat16
    groups, across, count, width = xw.shape
    head_dim = width // HEADS
    scale = 1.0 / math.sqrt(head_dim)
    xf = xw.astype(f32)
    mean_value = lax.optimization_barrier(jnp.mean(xf, axis=-1, keepdims=True))
    centered_input = xf - mean_value
    inverse_deviation = lax.rsqrt(lax.optimization_barrier(jnp.mean(centered_input * centered_input, axis=-1, keepdims=True)) + epsilon)
    standardized_input = centered_input * inverse_deviation
    normalized_input = (standardized_input * norm_gain_vector + norm_bias_vector).astype(half_width)
    qkv = (jnp.einsum('aonc,cd->aond', normalized_input.astype(f32), qkv_weight.astype(f32)) + qkv_bias).astype(half_width)
    split = qkv.reshape(groups, across, count, 3, HEADS, head_dim)
    query_rows = split[:, :, :, 0]
    key_rows = split[:, :, :, 1]
    value_rows = split[:, :, :, 2]
    scores = jnp.einsum('aonhd,aomhd->aohnm', query_rows.astype(f32), key_rows.astype(f32)) * scale + add[:, None]
    probabilities_wide = jax.nn.softmax(scores, axis=-1)
    attention_probabilities = probabilities_wide.astype(half_width)
    attention_rows = jnp.einsum('aohnm,aomhd->aonhd', attention_probabilities.astype(f32), value_rows.astype(f32))
    attention_rows = attention_rows.reshape(groups, across, count, width).astype(half_width)
    output_rows = xf + jnp.einsum('aonc,ce->aone', attention_rows.astype(f32), proj_weight.astype(f32)) + proj_bias
    dyf = dyw.astype(f32)
    proj_bias_grad = lax.optimization_barrier(jnp.sum(dyf, axis=(0, 1, 2)))
    proj_weight_grad = jnp.einsum('aonc,aone->ce', attention_rows.astype(f32), dyf)
    d_attn = jnp.einsum('aone,ce->aonc', dyf, proj_weight.astype(f32)).astype(half_width)
    d_attn = d_attn.reshape(groups, across, count, HEADS, head_dim)
    d_values = jnp.einsum('aohnm,aonhd->aomhd', attention_probabilities.astype(f32), d_attn.astype(f32))
    d_probs = jnp.einsum('aonhd,aomhd->aohnm', d_attn.astype(f32), value_rows.astype(f32))
    d_scores = probabilities_wide * (d_probs - lax.optimization_barrier(jnp.sum(probabilities_wide * d_probs, axis=-1, keepdims=True)))
    bias_part = lax.optimization_barrier(jnp.sum(d_scores, axis=1))
    d_scores_b = d_scores.astype(half_width)
    d_query = jnp.einsum('aohnm,aomhd->aonhd', d_scores_b.astype(f32), key_rows.astype(f32)) * scale
    d_keys = jnp.einsum('aohnm,aonhd->aomhd', d_scores_b.astype(f32), query_rows.astype(f32)) * scale
    d_qkv = jnp.stack([d_query, d_keys, d_values], axis=3).reshape(groups, across, count, 3 * width).astype(half_width)
    qkv_bias_grad = lax.optimization_barrier(jnp.sum(d_qkv.astype(f32), axis=(0, 1, 2)))
    qkv_weight_grad = jnp.einsum('aonc,aond->cd', normalized_input.astype(f32), d_qkv.astype(f32))
    normalized_gradient = jnp.einsum('aond,cd->aonc', d_qkv.astype(f32), qkv_weight.astype(f32))
    gain_gradient = lax.optimization_barrier(jnp.sum(normalized_gradient * standardized_input, axis=(0, 1, 2)))
    shift_grad = lax.optimization_barrier(jnp.sum(normalized_gradient, axis=(0, 1, 2)))
    standardized_gradient = normalized_gradient * norm_gain_vector
    input_gradient = inverse_deviation * (standardized_gradient - lax.optimization_barrier(jnp.mean(standardized_gradient, axis=-1, keepdims=True)) - standardized_input * lax.optimization_barrier(jnp.mean(standardized_gradient * standardized_input, axis=-1, keepdims=True)))
    grad = dyf + input_gradient
    return (output_rows, grad, bias_part, (gain_gradient, shift_grad, qkv_weight_grad, qkv_bias_grad, proj_weight_grad, proj_bias_grad))

def reference(tokens, cotangent, norm_gain_vector, norm_bias_vector, qkv_weight, qkv_bias, proj_weight, proj_bias, earth_bias, lat_valid):
    half_z, half_lat, half_lon = (WZ // 2, WLAT // 2, WLON // 2)
    shifted = jnp.roll(tokens, (-half_z, -half_lat, -half_lon), (0, 1, 2))
    shifted_cot = jnp.roll(cotangent, (-half_z, -half_lat, -half_lon), (0, 1, 2))
    key_valid = jnp.roll(lat_valid, -half_lat)
    count = WZ * WLAT * WLON
    pair = jnp.asarray(pair_index())
    position = jnp.arange(count, dtype=jnp.int32)
    level_in = position // (WLAT * WLON)
    row_in = position // WLON % WLAT
    level = jnp.arange(ZW, dtype=jnp.int32)[:, None] * WZ + level_in[None, :]
    level_region = (level >= Z - WZ).astype(jnp.int32) + (level >= Z - half_z).astype(jnp.int32)

    def band(index):
        start = (index * WLAT).astype(jnp.int32)
        xw = to_windows(lax.dynamic_slice_in_dim(shifted, start, WLAT, 1))
        dyw = to_windows(lax.dynamic_slice_in_dim(shifted_cot, start, WLAT, 1))
        table = lax.dynamic_index_in_dim(earth_bias, index, 1, keepdims=False)
        row = start + row_in
        row_region = (row >= NLAT - WLAT).astype(jnp.int32) + (row >= NLAT - half_lat).astype(jnp.int32)
        key_ok = lax.dynamic_slice_in_dim(key_valid, start, WLAT)[row_in]
        allowed = (level_region[:, :, None] == level_region[:, None, :]) & (row_region[None, :, None] == row_region[None, None, :]) & (key_ok[None, None, :] == 1)
        add = table[:, :, pair] + jnp.where(allowed, jnp.float32(0.0), jnp.float32(mask_fill))[:, None]
        output_rows, grad, bias_part, grads = attend(xw, dyw, add, norm_gain_vector, norm_bias_vector, qkv_weight, qkv_bias, proj_weight, proj_bias)
        table_grad = jnp.zeros((ZW, HEADS, PAIRS), jnp.float32).at[:, :, pair.reshape(-1)].add(bias_part.reshape(ZW, HEADS, count * count))
        return (from_windows(output_rows, Z, WLAT, NLON), from_windows(grad, Z, WLAT, NLON), table_grad * bias_factor, grads)
    outs, grads, tables, partials = lax.map(band, jnp.arange(NLATW, dtype=jnp.int32))
    out_shifted = outs.transpose(1, 0, 2, 3, 4).reshape(Z, NLAT, NLON, C)
    grad_shifted = grads.transpose(1, 0, 2, 3, 4).reshape(Z, NLAT, NLON, C)
    block_out = jnp.roll(out_shifted, (half_z, half_lat, half_lon), (0, 1, 2))
    token_grad = jnp.roll(grad_shifted, (half_z, half_lat, half_lon), (0, 1, 2))
    norm_by = 1.0 / math.sqrt(TOKENS)
    sums = [lax.optimization_barrier(jnp.sum(p, axis=0)) * norm_by for p in partials]
    earth_bias_grad = tables.transpose(1, 0, 2, 3)
    return (block_out, token_grad, sums[0], sums[1], sums[2], sums[3], sums[4], sums[5], earth_bias_grad)
```

```python
import math

import jax
import jax.numpy as jnp
from jax import lax
from jax.sharding import PartitionSpec as P

HEADS = 6
WZ = 2
WLAT = 6
WLON = 12


mask_fill = -10000.0
epsilon = 1e-05
bias_factor = 8.0


def shifted(array, axis, by):
    count = lax.axis_size(axis)
    return lax.ppermute(array, axis, [(i, (i + by) % count) for i in range(count)])


def toeplitz():
    diffs = 2 * WLON - 1
    place = jnp.arange(WLON * WLON, dtype=jnp.int32)
    offset = place // WLON - place % WLON + WLON - 1
    return (jnp.arange(diffs, dtype=jnp.int32)[:, None] == offset[None, :]).astype(jnp.float32)


def to_windows(tile):
    levels, rows, cols, width = tile.shape
    grid = tile.reshape(levels // WZ, WZ, rows // WLAT, WLAT, cols // WLON, WLON, width)
    grid = grid.transpose(0, 2, 4, 1, 3, 5, 6)
    return grid.reshape(levels // WZ * (rows // WLAT), cols // WLON, WZ * WLAT * WLON, width)


def from_windows(blocks, levels, rows, cols):
    width = blocks.shape[-1]
    grid = blocks.reshape(levels // WZ, rows // WLAT, cols // WLON, WZ, WLAT, WLON, width)
    return grid.transpose(0, 3, 1, 4, 2, 5, 6).reshape(levels, rows, cols, width)


def into_shifted(stacked):
    kinds, levels, rows, cols, width = stacked.shape
    half_lat = WLAT // 2
    half_lon = WLON // 2
    stacked = jnp.roll(stacked, -(WZ // 2), axis=1)
    upper = stacked[:, :, :half_lat].reshape(kinds, levels, half_lat, cols * width)
    below = shifted(upper, "lat", -1).reshape(kinds, levels, half_lat, cols, width)
    stacked = jnp.concatenate([stacked[:, :, half_lat:], below], axis=2)
    left = stacked[:, :, :, :half_lon].reshape(kinds, levels, rows, half_lon * width)
    right = shifted(left, "lon", -1).reshape(kinds, levels, rows, half_lon, width)
    return jnp.concatenate([stacked[:, :, :, half_lon:], right], axis=3)


def to_owners(stacked):
    kinds, levels, rows, cols, width = stacked.shape
    half_lat = WLAT // 2
    half_lon = WLON // 2
    tail = stacked[:, :, :, cols - half_lon :].reshape(kinds, levels, rows, half_lon * width)
    front = shifted(tail, "lon", 1).reshape(kinds, levels, rows, half_lon, width)
    stacked = jnp.concatenate([front, stacked[:, :, :, : cols - half_lon]], axis=3)
    bottom = stacked[:, :, rows - half_lat :].reshape(kinds, levels, half_lat, cols * width)
    top = shifted(bottom, "lat", 1).reshape(kinds, levels, half_lat, cols, width)
    stacked = jnp.concatenate([top, stacked[:, :, : rows - half_lat]], axis=2)
    return jnp.roll(stacked, WZ // 2, axis=1)


def window_bias(table_bands, lat_valid, first_band, levels):
    zones, bands, heads, pairs = table_bands.shape
    total_rows = lat_valid.shape[0]
    band_count = total_rows // WLAT
    count = WZ * WLAT * WLON
    table = table_bands.reshape(zones, bands, heads, WZ * WZ * WLAT * WLAT, 2 * WLON - 1)
    spread = jnp.einsum("abhpd,dq->abhpq", table, toeplitz(), precision=lax.Precision.HIGHEST)
    spread = spread.reshape(zones, bands, heads, WZ, WZ, WLAT, WLAT, WLON, WLON)
    spread = spread.transpose(0, 1, 2, 3, 5, 7, 4, 6, 8).reshape(zones, bands, heads, count, count)
    position = jnp.arange(count, dtype=jnp.int32)
    level_in = position // (WLAT * WLON)
    row_in = position // WLON % WLAT
    level = jnp.arange(zones, dtype=jnp.int32)[:, None] * WZ + level_in[None, :]
    level_region = (level >= levels - WZ).astype(jnp.int32) + (level >= levels - WZ // 2).astype(
        jnp.int32
    )
    band_at = (first_band + jnp.arange(bands, dtype=jnp.int32)) % band_count
    row = band_at[:, None] * WLAT + row_in[None, :]
    row_region = (row >= total_rows - WLAT).astype(jnp.int32) + (
        row >= total_rows - WLAT // 2
    ).astype(jnp.int32)
    rolled = jnp.roll(lat_valid, -(WLAT // 2))
    doubled = jnp.concatenate([rolled, rolled])
    tile_valid = lax.dynamic_slice_in_dim(doubled, band_at[0] * WLAT, bands * WLAT)
    key_ok = jnp.broadcast_to(
        tile_valid.reshape(bands, 1, WLAT, 1), (bands, WZ, WLAT, WLON)
    ).reshape(bands, count)
    same_level = level_region[:, None, :, None] == level_region[:, None, None, :]
    same_row = row_region[None, :, :, None] == row_region[None, :, None, :]
    allowed = same_level & same_row & (key_ok[None, :, None, :] == 1)
    masked = jnp.where(allowed, jnp.float32(0.0), jnp.float32(mask_fill))
    return (spread + masked[:, :, None]).reshape(zones * bands, heads, count, count)


def bias_table_grad(bias_part, zones, bands):
    heads = bias_part.shape[1]
    grid = bias_part.reshape(zones, bands, heads, WZ, WLAT, WLON, WZ, WLAT, WLON)
    grid = grid.transpose(0, 1, 2, 3, 6, 4, 7, 5, 8).reshape(
        zones, bands, heads, WZ * WZ * WLAT * WLAT, WLON * WLON
    )
    table = jnp.einsum("abhpq,dq->abhpd", grid, toeplitz(), precision=lax.Precision.HIGHEST)
    return table.reshape(zones, bands, heads, -1) * bias_factor


def forward(xw, add, params):
    norm_gain_vector, norm_bias_vector, qkv_weight, qkv_bias, proj_weight, proj_bias = params
    f32 = jnp.float32
    groups, across, count, width = xw.shape
    head_dim = width // HEADS
    scale = 1.0 / math.sqrt(head_dim)
    xf = xw.astype(f32)
    mean_value = jnp.mean(xf, axis=-1, keepdims=True)
    centered_input = xf - mean_value
    inverse_deviation = lax.rsqrt(
        jnp.mean(centered_input * centered_input, axis=-1, keepdims=True) + epsilon
    )
    standardized_input = centered_input * inverse_deviation
    normalized_input = (standardized_input * norm_gain_vector + norm_bias_vector).astype(
        jnp.bfloat16
    )
    qkv = (
        jnp.einsum("aonc,cd->aond", normalized_input, qkv_weight, preferred_element_type=f32)
        + qkv_bias
    )
    split = qkv.astype(jnp.bfloat16).reshape(groups, across, count, 3, HEADS, head_dim)
    query_rows = split[:, :, :, 0]
    key_rows = split[:, :, :, 1]
    value_rows = split[:, :, :, 2]
    scores = (
        jnp.einsum("aonhd,aomhd->aohnm", query_rows, key_rows, preferred_element_type=f32) * scale
        + add[:, None]
    )
    probabilities_wide = jax.nn.softmax(scores, axis=-1)
    attention_probabilities = probabilities_wide.astype(jnp.bfloat16)
    attention_rows = jnp.einsum(
        "aohnm,aomhd->aonhd", attention_probabilities, value_rows, preferred_element_type=f32
    )
    attention_rows = attention_rows.reshape(groups, across, count, width).astype(jnp.bfloat16)
    output_rows = (
        xf
        + jnp.einsum("aonc,ce->aone", attention_rows, proj_weight, preferred_element_type=f32)
        + proj_bias
    )
    return (
        output_rows,
        (
            standardized_input,
            inverse_deviation,
            normalized_input,
            query_rows,
            key_rows,
            value_rows,
            probabilities_wide,
            attention_probabilities,
            attention_rows,
        ),
    )


def backward(saved_residuals, dyw, params, counted):
    norm_gain_vector, norm_bias_vector, qkv_weight, qkv_bias, proj_weight, proj_bias = params
    (
        standardized_input,
        inverse_deviation,
        normalized_input,
        query_rows,
        key_rows,
        value_rows,
        probabilities_wide,
        attention_probabilities,
        attention_rows,
    ) = saved_residuals
    f32 = jnp.float32
    groups, across, count, width = dyw.shape
    head_dim = width // HEADS
    scale = 1.0 / math.sqrt(head_dim)
    keep = counted[:, :, None, None]
    kept_dy = jnp.where(keep, dyw, jnp.zeros_like(dyw))
    proj_bias_grad = jnp.sum(kept_dy, axis=(0, 1, 2), dtype=f32)
    proj_weight_grad = jnp.einsum(
        "aonc,aone->ce", attention_rows, kept_dy, preferred_element_type=f32
    )
    d_attn = jnp.einsum("aone,ce->aonc", dyw, proj_weight, preferred_element_type=f32).astype(
        jnp.bfloat16
    )
    d_attn = d_attn.reshape(groups, across, count, HEADS, head_dim)
    d_values = jnp.einsum(
        "aohnm,aonhd->aomhd", attention_probabilities, d_attn, preferred_element_type=f32
    )
    d_probs = jnp.einsum("aonhd,aomhd->aohnm", d_attn, value_rows, preferred_element_type=f32)
    d_scores = probabilities_wide * (
        d_probs - jnp.sum(probabilities_wide * d_probs, axis=-1, keepdims=True)
    )
    bias_part = jnp.sum(
        jnp.where(counted[:, :, None, None, None], d_scores, jnp.float32(0.0)), axis=1
    )
    d_scores_b = d_scores.astype(jnp.bfloat16)
    d_query = (
        jnp.einsum("aohnm,aomhd->aonhd", d_scores_b, key_rows, preferred_element_type=f32) * scale
    )
    d_keys = (
        jnp.einsum("aohnm,aonhd->aomhd", d_scores_b, query_rows, preferred_element_type=f32) * scale
    )
    d_qkv = (
        jnp.stack([d_query, d_keys, d_values], axis=3)
        .reshape(groups, across, count, 3 * width)
        .astype(jnp.bfloat16)
    )
    kept_qkv = jnp.where(keep, d_qkv, jnp.zeros_like(d_qkv))
    qkv_bias_grad = jnp.sum(kept_qkv, axis=(0, 1, 2), dtype=f32)
    qkv_weight_grad = jnp.einsum(
        "aonc,aond->cd", normalized_input, kept_qkv, preferred_element_type=f32
    )
    normalized_gradient = jnp.einsum("aond,cd->aonc", d_qkv, qkv_weight, preferred_element_type=f32)
    retained_normalized = jnp.where(keep, normalized_gradient, jnp.float32(0.0))
    gain_gradient = jnp.sum(retained_normalized * standardized_input, axis=(0, 1, 2))
    shift_grad = jnp.sum(retained_normalized, axis=(0, 1, 2))
    standardized_gradient = normalized_gradient * norm_gain_vector
    input_gradient = inverse_deviation * (
        standardized_gradient
        - jnp.mean(standardized_gradient, axis=-1, keepdims=True)
        - standardized_input
        * jnp.mean(standardized_gradient * standardized_input, axis=-1, keepdims=True)
    )
    grad = dyw.astype(f32) + input_gradient
    return (
        grad,
        bias_part,
        (
            gain_gradient,
            shift_grad,
            qkv_weight_grad,
            qkv_bias_grad,
            proj_weight_grad,
            proj_bias_grad,
        ),
    )


def spread_to_all(piece, axis):
    count = lax.axis_size(axis)
    return lax.all_to_all(jnp.broadcast_to(piece[None], (count,) + piece.shape), axis, 0, 0)


def reduce_all(qkv_weight_grad, proj_weight_grad, vectors, table):
    f32 = jnp.float32
    lon_count = lax.axis_size("lon")
    width, wide = qkv_weight_grad.shape
    across = wide + width
    vector = jnp.concatenate(vectors)
    vector_rows = vector.shape[0] // 128
    entries = across - 128
    matrix = jnp.concatenate([qkv_weight_grad, proj_weight_grad], axis=1)
    matrix = matrix.reshape(lon_count, width // lon_count, across)
    flat = table.reshape(-1)
    flat = jnp.pad(flat, (0, lon_count * entries - flat.shape[0])).reshape(lon_count, 1, entries)
    vector = jnp.pad(vector.reshape(vector_rows, 1, 128), ((0, lon_count - vector_rows), (0, 0), (0, 0)))
    last = jnp.concatenate([flat, vector], axis=2)
    parts = jnp.concatenate([matrix, last, jnp.zeros_like(last)], axis=1).astype(jnp.bfloat16)
    by_lon = jnp.sum(lax.all_to_all(parts, "lon", 0, 0).astype(f32), axis=0)
    by_lat = jnp.sum(spread_to_all(by_lon.astype(jnp.bfloat16), "lat").astype(f32), axis=0)
    row = lax.broadcasted_iota(jnp.int32, by_lat.shape, 0)
    column = lax.broadcasted_iota(jnp.int32, by_lat.shape, 1)
    is_table = (row == width // lon_count) & (column < entries)
    done = jnp.where(is_table, by_lon, by_lat).astype(jnp.bfloat16)
    full = spread_to_all(done, "lon").astype(f32)
    rows = width // lon_count
    matrix = full[:, :rows].reshape(width, across)
    flat = full[:, rows, :entries].reshape(-1)[: table.size].reshape(table.shape)
    vector = full[:vector_rows, rows, entries:].reshape(-1)
    pieces = []
    start = 0
    for v in vectors:
        pieces.append(vector[start : start + v.shape[0]])
        start += v.shape[0]
    return (matrix[:, :wide], matrix[:, wide:], tuple(pieces)), flat


def local(
    tokens,
    cotangent,
    norm_gain_vector,
    norm_bias_vector,
    qkv_weight,
    qkv_bias,
    proj_weight,
    proj_bias,
    earth_bias,
    lat_valid,
):
    levels, rows, cols, width = tokens.shape
    lat_count = lax.axis_size("lat")
    lon_count = lax.axis_size("lon")
    lat_at = lax.axis_index("lat")
    zones = levels // WZ
    bands = rows // WLAT
    params = (norm_gain_vector, norm_bias_vector, qkv_weight, qkv_bias, proj_weight, proj_bias)
    add = window_bias(earth_bias, lat_valid, lat_at * bands, levels)
    counted = jnp.ones((zones * bands, cols // WLON), bool)
    moved = into_shifted(jnp.stack([tokens, cotangent]))
    out_w, saved_residuals = forward(to_windows(moved[0]), add, params)
    grad_w, bias_part, grads = backward(saved_residuals, to_windows(moved[1]), params, counted)
    results = jnp.stack(
        [from_windows(out_w, levels, rows, cols), from_windows(grad_w, levels, rows, cols)]
    )
    back = to_owners(results)
    block_out = back[0]
    token_grad = back[1]
    table_part = bias_table_grad(bias_part, zones, bands)
    gain_gradient, shift_grad, qkv_weight_grad, qkv_bias_grad, proj_weight_grad, proj_bias_grad = (
        grads
    )
    norm_by = 1.0 / math.sqrt(levels * rows * cols * lat_count * lon_count)
    summed, earth_bias_grad = reduce_all(
        qkv_weight_grad,
        proj_weight_grad,
        (gain_gradient, shift_grad, qkv_bias_grad, proj_bias_grad),
        table_part,
    )
    qkv_weight_grad, proj_weight_grad, (gain_gradient, shift_grad, qkv_bias_grad, proj_bias_grad) = summed
    summed = (
        gain_gradient,
        shift_grad,
        qkv_weight_grad,
        qkv_bias_grad,
        proj_weight_grad,
        proj_bias_grad,
    )
    return (
        block_out,
        token_grad,
        summed[0] * norm_by,
        summed[1] * norm_by,
        summed[2] * norm_by,
        summed[3] * norm_by,
        summed[4] * norm_by,
        summed[5] * norm_by,
        earth_bias_grad,
    )


def solution(mesh):
    placed = (
        P(None, "lat", "lon", None),
        P(None, "lat", "lon", None),
        P(),
        P(),
        P(),
        P(),
        P(),
        P(),
        P(None, "lat", None, None),
        P(),
    )
    return jax.shard_map(
        local,
        mesh=mesh,
        in_specs=placed,
        out_specs=(
            P(None, "lat", "lon", None),
            P(None, "lat", "lon", None),
            P(),
            P(),
            P(),
            P(),
            P(),
            P(),
            P(None, "lat", None, None),
        ),
        check_vma=False,
    )
```

```python
import math

import jax
import jax.numpy as jnp
import numpy as np
from jax import lax
from jax.experimental import pallas as pl
from jax.experimental.pallas import tpu as pltpu
from jax.sharding import PartitionSpec as P

HEADS = 6
WZ = 2
WLAT = 6
WLON = 12

HALF_LAT = WLAT // 2
HALF_LON = WLON // 2
GROUP = WZ * WLAT
COUNT = GROUP * WLON
DIFFS = 2 * WLON - 1
SKEW = DIFFS * GROUP
LANES = 128
SPREAD = 3 * LANES

mask_fill = -10000.0
epsilon = 1e-05
bias_factor = 8.0

f32 = jnp.float32
bf16 = jnp.bfloat16


def matmul(a, b, dims=((1,), (0,)), precision=None):
    return lax.dot_general(a, b, (dims, ((), ())), preferred_element_type=f32, precision=precision)


def order_of_skew():
    place = np.zeros((SKEW, SPREAD), np.float32)
    for z in range(WZ):
        for r in range(WLAT):
            for d in range(DIFFS):
                place[(z * WLAT + r) * DIFFS + d, (DIFFS - 1 - d) * GROUP + z * WLAT + r] = 1.0
    return place


def bias_kernel(table_ref, place_ref, masked_ref, add_ref):
    skewed = matmul(table_ref[...], place_ref[...], precision=lax.Precision.HIGHEST)
    for i in range(WLON):
        shift = (GROUP * (i - WLON + 1)) % SPREAD
        rolled = skewed if shift == 0 else pltpu.roll(skewed, shift, 1)
        rows = slice(i * GROUP, (i + 1) * GROUP)
        masked = masked_ref[rows, :]
        for h in range(HEADS):
            add_ref[h * COUNT + i * GROUP : h * COUNT + (i + 1) * GROUP, :] = (
                rolled[h * GROUP : (h + 1) * GROUP, :COUNT] + masked
            )


def head_lanes(width, h):
    lane = lax.broadcasted_iota(jnp.int32, (1, width), 1)
    return (lane // 32 == h).astype(f32)


def attention_kernel(
    x_ref,
    dy_ref,
    gain_ref,
    shift_ref,
    qkv_weight_ref,
    qkv_bias_ref,
    proj_weight_ref,
    proj_bias_ref,
    add_ref,
    out_ref,
    grad_ref,
    parts_ref,
    d_bias_ref,
):
    tokens, width = x_ref.shape
    windows = tokens // COUNT
    head_dim = width // HEADS
    scale = 1.0 / math.sqrt(head_dim)
    xf = x_ref[...].astype(f32)
    mean_value = jnp.mean(xf, axis=-1, keepdims=True)
    centered = xf - mean_value
    inverse = lax.rsqrt(jnp.mean(centered * centered, axis=-1, keepdims=True) + epsilon)
    xhat = centered * inverse
    gain = gain_ref[...]
    normed = (xhat * gain + shift_ref[...]).astype(bf16)
    weights = [qkv_weight_ref[:, k * width : (k + 1) * width] for k in range(3)]
    q, k, v = [
        (matmul(normed, weights[i]) + qkv_bias_ref[:, i * width : (i + 1) * width]).astype(bf16)
        for i in range(3)
    ]
    dy = dy_ref[...]
    proj_weight = proj_weight_ref[...]
    d_attn = matmul(dy, proj_weight, ((1,), (1,))).astype(bf16)
    tiles = [(0, 4), (4, 2)]
    whole = []
    for w in range(windows):
        rows = slice(w * COUNT, (w + 1) * COUNT)
        per_tile = []
        for first, heads in tiles:
            lanes = slice(first * head_dim, (first + heads) * head_dim)
            masks = [head_lanes(heads * head_dim, h) for h in range(heads)]
            masks_b = [m.astype(bf16) for m in masks]
            qt, kt, vt, at = q[rows, lanes], k[rows, lanes], v[rows, lanes], d_attn[rows, lanes]
            q_stack = jnp.concatenate([qt * m for m in masks_b], axis=0)
            a_stack = jnp.concatenate([at * m for m in masks_b], axis=0)

            def by_head(stacked):
                total = stacked[:COUNT] * masks[0]
                for h in range(1, heads):
                    total = total + stacked[h * COUNT : (h + 1) * COUNT] * masks[h]
                return total

            at_rows = slice(first * COUNT, (first + heads) * COUNT)
            scores = matmul(q_stack, kt, ((1,), (1,))) * scale + add_ref[at_rows, :]
            top = jnp.max(scores, axis=-1, keepdims=True)
            e = jnp.exp(scores - top)
            probs_f = e * (1.0 / jnp.sum(e, axis=-1, keepdims=True))
            probs = probs_f.astype(bf16)
            attn = by_head(matmul(probs, vt)).astype(bf16)
            d_probs = matmul(a_stack, vt, ((1,), (1,)))
            d_scores = probs_f * (d_probs - jnp.sum(probs_f * d_probs, axis=-1, keepdims=True))
            if w == 0:
                d_bias_ref[at_rows, :] = d_scores
            else:
                d_bias_ref[at_rows, :] += d_scores
            d_scores_b = d_scores.astype(bf16)
            d_v = matmul(probs, a_stack, ((0,), (0,))).astype(bf16)
            d_q = (by_head(matmul(d_scores_b, kt)) * scale).astype(bf16)
            d_k = (matmul(d_scores_b, q_stack, ((0,), (0,))) * scale).astype(bf16)
            per_tile.append((attn, d_q, d_k, d_v))
        whole.append([jnp.concatenate([t[i] for t in per_tile], axis=1) for i in range(4)])
    attn, d_q, d_k, d_v = [jnp.concatenate([t[i] for t in whole], axis=0) for i in range(4)]
    out_ref[...] = xf + matmul(attn, proj_weight) + proj_bias_ref[...]
    d_parts = (d_q, d_k, d_v)
    d_normed = sum(matmul(d_parts[i], weights[i], ((1,), (1,))) for i in range(3))
    d_xhat = d_normed * gain
    grad_ref[...] = dy.astype(f32) + inverse * (
        d_xhat
        - jnp.mean(d_xhat, axis=-1, keepdims=True)
        - xhat * jnp.mean(d_xhat * xhat, axis=-1, keepdims=True)
    )
    d_qkv = jnp.concatenate(d_parts, axis=1)
    qkv_weight_grad = matmul(normed, d_qkv, ((0,), (0,)))
    proj_weight_grad = matmul(attn, dy, ((0,), (0,)))
    matrix = jnp.concatenate([qkv_weight_grad, proj_weight_grad], axis=1)
    vector = jnp.concatenate(
        [
            jnp.sum(d_normed * xhat, axis=0, keepdims=True),
            jnp.sum(d_normed, axis=0, keepdims=True),
            jnp.sum(d_qkv.astype(f32), axis=0, keepdims=True),
            jnp.sum(dy.astype(f32), axis=0, keepdims=True),
        ],
        axis=1,
    )
    skewed = jnp.zeros((HEADS * GROUP, SPREAD), f32)
    for i in range(WLON):
        part = jnp.concatenate(
            [
                d_bias_ref[h * COUNT + i * GROUP : h * COUNT + (i + 1) * GROUP, :]
                for h in range(HEADS)
            ],
            axis=0,
        )
        part = jnp.concatenate([part, jnp.zeros((HEADS * GROUP, SPREAD - COUNT), f32)], axis=1)
        shift = GROUP * (WLON - 1 - i)
        skewed = skewed + (part if shift == 0 else pltpu.roll(part, shift, 1))
    pack(parts_ref, matrix, vector, skewed)


def table_slots(pieces, pairs):
    slots = []
    for p in range(pairs):
        if p < pieces:
            slots.append((p, 0, p, 4 * LANES))
        else:
            slots.append((p - pieces, 2 * LANES, p - pieces + (pairs - pieces), 2 * LANES))
    return slots


def pack(parts_ref, matrix, vector, skewed):
    pieces = parts_ref.shape[0]
    rows = matrix.shape[0] // pieces
    for d in range(pieces):
        parts_ref[d, 0:rows, :] = matrix[d * rows : (d + 1) * rows, :]
        parts_ref[d, rows:8, :] = jnp.zeros((8 - rows, matrix.shape[1]), f32)
    for p, (d, at, d2, at2) in enumerate(table_slots(pieces, skewed.shape[0] // 2)):
        pair = slice(2 * p, 2 * p + 2)
        parts_ref[d, rows : rows + 2, at : at + 2 * LANES] = skewed[pair, : 2 * LANES]
        parts_ref[d2, rows : rows + 2, at2 : at2 + LANES] = skewed[pair, 2 * LANES :]
    for d in range(vector.shape[1] // LANES):
        parts_ref[d, rows : rows + 1, 5 * LANES :] = vector[:, d * LANES : (d + 1) * LANES]


def unpack_kernel(norm_by, full_ref, place_ref, qkv_ref, proj_ref, table_ref, gain_ref, shift_ref, qkv_bias_ref, proj_bias_ref, wide_ref, skewed_ref):
    pieces = full_ref.shape[0]
    width, wide = qkv_ref.shape
    rows = width // pieces
    wide_ref[...] = full_ref[...].astype(f32)
    for d in range(pieces):
        piece = wide_ref[d, 0:rows, :] * norm_by
        qkv_ref[d * rows : (d + 1) * rows, :] = piece[:, :wide]
        proj_ref[d * rows : (d + 1) * rows, :] = piece[:, wide:]
    for p, (d, at, d2, at2) in enumerate(table_slots(pieces, skewed_ref.shape[0] // 2)):
        skewed_ref[2 * p : 2 * p + 2, : 2 * LANES] = wide_ref[d, rows : rows + 2, at : at + 2 * LANES]
        skewed_ref[2 * p : 2 * p + 2, 2 * LANES :] = wide_ref[d2, rows : rows + 2, at2 : at2 + LANES]
    table_ref[...] = matmul(
        skewed_ref[...] * bias_factor, place_ref[...], ((1,), (1,)), lax.Precision.HIGHEST
    )
    count = (3 * width + wide) // LANES
    vector = jnp.concatenate(
        [wide_ref[d, rows : rows + 1, 5 * LANES :] for d in range(count)], axis=1
    )
    vector = vector * norm_by
    gain_ref[...] = vector[:, :width]
    shift_ref[...] = vector[:, width : 2 * width]
    qkv_bias_ref[...] = vector[:, 2 * width : 2 * width + wide]
    proj_bias_ref[...] = vector[:, 2 * width + wide :]


VMEM_LIMIT = 48 * 1024 * 1024


def call(kernel, out_shape, name, scratch=()):
    return pl.pallas_call(
        kernel,
        out_shape=out_shape,
        scratch_shapes=scratch,
        compiler_params=pltpu.CompilerParams(vmem_limit_bytes=VMEM_LIMIT),
        name=name,
    )


def struct(shape, dtype=f32):
    return jax.ShapeDtypeStruct(shape, dtype)


def spread_to_all(piece, axis):
    count = lax.axis_size(axis)
    return lax.all_to_all(jnp.broadcast_to(piece[None], (count,) + piece.shape), axis, 0, 0)


def reduce_all(parts, rows):
    by_lon = jnp.sum(lax.all_to_all(parts.astype(bf16), "lon", 0, 0).astype(f32), axis=0)
    by_lat = jnp.sum(spread_to_all(by_lon.astype(bf16), "lat").astype(f32), axis=0)
    row = lax.broadcasted_iota(jnp.int32, by_lat.shape, 0)
    column = lax.broadcasted_iota(jnp.int32, by_lat.shape, 1)
    is_table = (row >= rows) & (column < 5 * LANES)
    done = jnp.where(is_table, by_lon, by_lat).astype(bf16)
    return spread_to_all(done, "lon")


def mask_of_windows(lat_valid, band, levels):
    total_rows = lat_valid.shape[0]
    position = jnp.arange(COUNT, dtype=jnp.int32)
    level = position % GROUP // WLAT
    row_in = position % WLAT
    level_region = (level >= levels - WZ).astype(jnp.int32) + (level >= levels - WZ // 2).astype(jnp.int32)
    row = band * WLAT + row_in
    row_region = (row >= total_rows - WLAT).astype(jnp.int32) + (row >= total_rows - HALF_LAT).astype(jnp.int32)
    rolled = jnp.roll(lat_valid, -HALF_LAT)
    valid = lax.dynamic_slice_in_dim(rolled, band * WLAT, WLAT)
    key_ok = jnp.tile(valid, WZ * WLON)
    allowed = (
        (level_region[:, None] == level_region[None, :])
        & (row_region[:, None] == row_region[None, :])
        & (key_ok[None, :] == 1)
    )
    return jnp.where(allowed, f32(0.0), f32(mask_fill))


def to_neighbour(value, axes, steps):
    counts = [lax.axis_size(a) for a in axes]
    if len(axes) == 1:
        n = counts[0]
        return lax.ppermute(value, axes[0], [(i, (i + steps[0]) % n) for i in range(n)])
    na, nb = counts
    pairs = [
        (a * nb + b, (a + steps[0]) % na * nb + (b + steps[1]) % nb)
        for a in range(na)
        for b in range(nb)
    ]
    return lax.ppermute(value, axes, pairs)


def local(
    tokens,
    cotangent,
    norm_gain_vector,
    norm_bias_vector,
    qkv_weight,
    qkv_bias,
    proj_weight,
    proj_bias,
    earth_bias,
    lat_valid,
):
    levels, rows, cols, width = tokens.shape
    wide = qkv_weight.shape[1]
    lat_count = lax.axis_size("lat")
    lon_count = lax.axis_size("lon")
    total = levels * rows * cols
    lat_halo = jnp.stack([a[:, :HALF_LAT, HALF_LON:] for a in (tokens, cotangent)])
    lon_halo = jnp.stack([a[:, HALF_LAT:, :HALF_LON] for a in (tokens, cotangent)])
    corner = jnp.stack([a[:, :HALF_LAT, :HALF_LON] for a in (tokens, cotangent)])
    lat_halo = to_neighbour(lat_halo, ("lat",), (-1,))
    corner = to_neighbour(corner, ("lat", "lon"), (-1, -1))
    lon_halo = to_neighbour(lon_halo, ("lon",), (-1,))

    place = jnp.asarray(order_of_skew())
    table = earth_bias.reshape(HEADS, WZ, WZ, WLAT, WLAT * DIFFS).transpose(0, 1, 3, 2, 4)
    masked = mask_of_windows(lat_valid, lax.axis_index("lat"), levels)
    add = call(bias_kernel, struct((HEADS * COUNT, COUNT)), "bias")(
        table.reshape(HEADS * GROUP, SKEW), place, masked
    )

    def windows_of(kind, array):
        own = jnp.concatenate([array[:, HALF_LAT:, HALF_LON:], lat_halo[kind]], axis=1)
        side = jnp.concatenate([lon_halo[kind], corner[kind]], axis=1)
        moved = jnp.roll(jnp.concatenate([own, side], axis=2), -(WZ // 2), axis=0)
        return moved.transpose(2, 0, 1, 3).reshape(total, width)

    out, grad, parts = call(
        attention_kernel,
        (struct((total, width)), struct((total, width)), struct((lon_count, 8, wide + width))),
        "attention",
        [pltpu.VMEM((HEADS * COUNT, COUNT), f32)],
    )(
        windows_of(0, tokens),
        windows_of(1, cotangent),
        norm_gain_vector[None],
        norm_bias_vector[None],
        qkv_weight,
        qkv_bias[None],
        proj_weight,
        proj_bias[None],
        add,
    )
    full = reduce_all(parts, width // lon_count)

    both = jnp.stack([out, grad]).reshape(2, cols, levels, rows, width)
    both = jnp.roll(both, WZ // 2, axis=2).transpose(0, 2, 3, 1, 4)
    half = both.astype(bf16)
    inner = rows - HALF_LAT
    edge = cols - HALF_LON
    lat_back = to_neighbour(half[:, :, inner:, :edge], ("lat",), (1,))
    corner_back = to_neighbour(half[:, :, inner:, edge:], ("lat", "lon"), (1, 1))
    lon_back = to_neighbour(half[:, :, :inner, edge:], ("lon",), (1,))
    top = jnp.concatenate([corner_back, lat_back], axis=3).astype(f32)
    bottom = jnp.concatenate([lon_back.astype(f32), both[:, :, :inner, :edge]], axis=3)
    back = jnp.concatenate([top, bottom], axis=2)

    norm_by = 1.0 / math.sqrt(total * lat_count * lon_count)

    def unpack(*refs):
        unpack_kernel(norm_by, *refs)

    qkv_weight_grad, proj_weight_grad, table, gain, shift, qkv_bias_grad, proj_bias_grad = call(
        unpack,
        (
            struct((width, wide)),
            struct((width, width)),
            struct((HEADS * GROUP, SKEW)),
            struct((1, width)),
            struct((1, width)),
            struct((1, wide)),
            struct((1, width)),
        ),
        "unpack",
        [pltpu.VMEM((lon_count, 8, wide + width), f32), pltpu.VMEM((HEADS * GROUP, SPREAD), f32)],
    )(full, place)
    table = table.reshape(HEADS, WZ, WLAT, WZ, WLAT * DIFFS).transpose(0, 1, 3, 2, 4)
    return (
        back[0],
        back[1],
        gain[0],
        shift[0],
        qkv_weight_grad,
        qkv_bias_grad[0],
        proj_weight_grad,
        proj_bias_grad[0],
        table.reshape(earth_bias.shape),
    )


def solution(mesh):
    placed = (
        P(None, "lat", "lon", None),
        P(None, "lat", "lon", None),
        P(),
        P(),
        P(),
        P(),
        P(),
        P(),
        P(None, "lat", None, None),
        P(),
    )
    return jax.shard_map(
        local,
        mesh=mesh,
        in_specs=placed,
        out_specs=(
            P(None, "lat", "lon", None),
            P(None, "lat", "lon", None),
            P(),
            P(),
            P(),
            P(),
            P(),
            P(),
            P(None, "lat", None, None),
        ),
        check_vma=False,
    )
```

```python
import math

import jax
import jax.numpy as jnp
from jax import lax
from jax.experimental import pallas as pl
from jax.experimental.pallas import tpu as pltpu
from jax.sharding import PartitionSpec as P

HEADS = 6
WZ = 2
WLAT = 6
WLON = 12

HALF_LAT = WLAT // 2
HALF_LON = WLON // 2
GROUP = WZ * WLAT
COUNT = GROUP * WLON
DIFFS = 2 * WLON - 1
SIDE = WLAT * DIFFS
LANES = 128
SPREAD = 3 * LANES

mask_fill = -10000.0
epsilon = 1e-05
bias_factor = 8.0

f32 = jnp.float32
bf16 = jnp.bfloat16


def matmul(a, b, dims=((1,), (0,)), precision=None):
    return lax.dot_general(a, b, (dims, ((), ())), preferred_element_type=f32, precision=precision)


def order_of_skew(z):
    row = lax.broadcasted_iota(jnp.int32, (SIDE, 1), 0)
    lat = sum((row >= k * DIFFS).astype(jnp.int32) for k in range(1, WLAT))
    diff = row - DIFFS * lat
    target = (DIFFS - 1 - diff) * GROUP + z * WLAT + lat
    return (lax.broadcasted_iota(jnp.int32, (SIDE, SPREAD), 1) == target).astype(f32)


def to_tiles(tiles_ref, value):
    for t in range(tiles_ref.shape[0]):
        part = value[:, t * LANES : (t + 1) * LANES]
        tiles_ref[t, :, : part.shape[1]] = part


def strided_rows(tiles_ref, start, count, stride):
    tiles = [tiles_ref[t, pl.ds(start, count, stride=stride), :] for t in range(tiles_ref.shape[0])]
    return jnp.concatenate(tiles, axis=1)


def bias_kernel(place_ref, valid_ref, table_ref, add_ref, sides_ref, skewed_ref):
    for zn in range(WZ):
        for zm in range(WZ):
            for ln in range(WLAT):
                at = ((zn * WZ + zm) * WLAT + ln) * SIDE
                row = (zn * WLAT + ln) * HEADS
                for h in range(HEADS):
                    sides_ref[zm, row + h : row + h + 1, :] = table_ref[h, :, at : at + SIDE]
    skewed = sum(
        matmul(sides_ref[z], order_of_skew(z), precision=lax.Precision.HIGHEST) for z in range(WZ)
    )
    to_tiles(skewed_ref, skewed)
    skewed = jnp.concatenate(
        [strided_rows(skewed_ref, h, GROUP, HEADS) for h in range(HEADS)], axis=0
    )
    masked = mask_of_windows(place_ref[0], valid_ref)
    for i in range(WLON):
        shift = (GROUP * (i - WLON + 1)) % SPREAD
        rolled = skewed if shift == 0 else pltpu.roll(skewed, shift, 1)
        for h in range(HEADS):
            add_ref[h * COUNT + i * GROUP : h * COUNT + (i + 1) * GROUP, :] = (
                rolled[h * GROUP : (h + 1) * GROUP, :COUNT] + masked
            )


def mask_of_windows(band, valid_ref):
    total_rows = valid_ref.shape[0]

    def place_of(shape, axis):
        position = lax.broadcasted_iota(jnp.int32, shape, axis)
        group = position - GROUP * sum(
            (position >= GROUP * k).astype(jnp.int32) for k in range(1, shape[axis] // GROUP)
        )
        level = (group >= WLAT).astype(jnp.int32)
        row_in = group - WLAT * level
        row = band * WLAT + row_in
        region = (row >= total_rows - WLAT).astype(jnp.int32) + (
            row >= total_rows - HALF_LAT
        ).astype(jnp.int32)
        return level, row_in, region

    level_n, _, region_n = place_of((GROUP, COUNT), 0)
    level_m, row_m, region_m = place_of((GROUP, COUNT), 1)
    key_ok = jnp.zeros((GROUP, COUNT), jnp.int32)
    for r in range(WLAT):
        at = lax.rem(band * WLAT + r + HALF_LAT, total_rows)
        key_ok = jnp.where(row_m == r, valid_ref[at], key_ok)
    allowed = (level_n == level_m) & (region_n == region_m) & (key_ok == 1)
    return jnp.where(allowed, f32(0.0), f32(mask_fill))


def head_lanes(width, h):
    lane = lax.broadcasted_iota(jnp.int32, (1, width), 1)
    return (lane // 32 == h).astype(f32)


def attention_kernel(
    place_ref,
    x_ref,
    dy_ref,
    gain_ref,
    shift_ref,
    qkv_weight_ref,
    qkv_bias_ref,
    proj_weight_ref,
    proj_bias_ref,
    add_ref,
    out_ref,
    grad_ref,
    bottom_ref,
    mine_ref,
    other_ref,
    d_bias_ref,
    parts_ref,
    result_ref,
):
    tokens, width = x_ref.shape
    windows = tokens // COUNT
    head_dim = width // HEADS
    scale = 1.0 / math.sqrt(head_dim)
    xf = x_ref[...].astype(f32)
    mean_value = jnp.mean(xf, axis=-1, keepdims=True)
    centered = xf - mean_value
    inverse = lax.rsqrt(jnp.mean(centered * centered, axis=-1, keepdims=True) + epsilon)
    xhat = centered * inverse
    gain = gain_ref[...]
    normed = (xhat * gain + shift_ref[...]).astype(bf16)
    weights = [qkv_weight_ref[:, k * width : (k + 1) * width] for k in range(3)]
    q, k, v = [
        (matmul(normed, weights[i]) + qkv_bias_ref[:, i * width : (i + 1) * width]).astype(bf16)
        for i in range(3)
    ]
    dy = dy_ref[...]
    proj_weight = proj_weight_ref[...]
    d_attn = matmul(dy, proj_weight, ((1,), (1,))).astype(bf16)
    tiles = [(0, 4), (4, 2)]
    whole = []
    for w in range(windows):
        rows = slice(w * COUNT, (w + 1) * COUNT)
        per_tile = []
        for first, heads in tiles:
            lanes = slice(first * head_dim, (first + heads) * head_dim)
            masks = [head_lanes(heads * head_dim, h) for h in range(heads)]
            masks_b = [m.astype(bf16) for m in masks]
            qt, kt, vt, at = q[rows, lanes], k[rows, lanes], v[rows, lanes], d_attn[rows, lanes]
            q_stack = jnp.concatenate([qt * m for m in masks_b], axis=0)
            a_stack = jnp.concatenate([at * m for m in masks_b], axis=0)

            def by_head(stacked):
                total = stacked[:COUNT] * masks[0]
                for h in range(1, heads):
                    total = total + stacked[h * COUNT : (h + 1) * COUNT] * masks[h]
                return total

            at_rows = slice(first * COUNT, (first + heads) * COUNT)
            scores = matmul(q_stack, kt, ((1,), (1,))) * scale + add_ref[at_rows, :]
            top = jnp.max(scores, axis=-1, keepdims=True)
            e = jnp.exp(scores - top)
            probs_f = e * (1.0 / jnp.sum(e, axis=-1, keepdims=True))
            probs = probs_f.astype(bf16)
            attn = by_head(matmul(probs, vt)).astype(bf16)
            d_probs = matmul(a_stack, vt, ((1,), (1,)))
            d_scores = probs_f * (d_probs - jnp.sum(probs_f * d_probs, axis=-1, keepdims=True))
            if w == 0:
                d_bias_ref[at_rows, :] = d_scores
            else:
                d_bias_ref[at_rows, :] += d_scores
            d_scores_b = d_scores.astype(bf16)
            d_v = matmul(probs, a_stack, ((0,), (0,))).astype(bf16)
            d_q = (by_head(matmul(d_scores_b, kt)) * scale).astype(bf16)
            d_k = (matmul(d_scores_b, q_stack, ((0,), (0,))) * scale).astype(bf16)
            per_tile.append((attn, d_q, d_k, d_v))
        whole.append([jnp.concatenate([t[i] for t in per_tile], axis=1) for i in range(4)])
    attn, d_q, d_k, d_v = [jnp.concatenate([t[i] for t in whole], axis=0) for i in range(4)]
    to_tiles(result_ref, xf + matmul(attn, proj_weight) + proj_bias_ref[...])
    to_grid(result_ref, out_ref, bottom_ref, 0)
    d_parts = (d_q, d_k, d_v)
    d_normed = sum(matmul(d_parts[i], weights[i], ((1,), (1,))) for i in range(3))
    d_xhat = d_normed * gain
    d_centered = inverse * (
        d_xhat
        - jnp.mean(d_xhat, axis=-1, keepdims=True)
        - xhat * jnp.mean(d_xhat * xhat, axis=-1, keepdims=True)
    )
    to_tiles(result_ref, dy.astype(f32) + d_centered)
    to_grid(result_ref, grad_ref, bottom_ref, 1)
    d_qkv = jnp.concatenate(d_parts, axis=1)
    qkv_weight_grad = matmul(normed, d_qkv, ((0,), (0,)))
    proj_weight_grad = matmul(attn, dy, ((0,), (0,)))
    matrix = jnp.concatenate([qkv_weight_grad, proj_weight_grad], axis=1)
    vector = jnp.concatenate(
        [
            jnp.sum(d_normed * xhat, axis=0, keepdims=True),
            jnp.sum(d_normed, axis=0, keepdims=True),
            jnp.sum(d_qkv.astype(f32), axis=0, keepdims=True),
            jnp.sum(dy.astype(f32), axis=0, keepdims=True),
        ],
        axis=1,
    )
    skewed = jnp.zeros((HEADS * GROUP, SPREAD), f32)
    for i in range(WLON):
        part = jnp.concatenate(
            [
                d_bias_ref[h * COUNT + i * GROUP : h * COUNT + (i + 1) * GROUP, :]
                for h in range(HEADS)
            ],
            axis=0,
        )
        part = jnp.concatenate([part, jnp.zeros((HEADS * GROUP, SPREAD - COUNT), f32)], axis=1)
        shift = GROUP * (WLON - 1 - i)
        skewed = skewed + (part if shift == 0 else pltpu.roll(part, shift, 1))
    pack(parts_ref, matrix, vector, skewed)
    core = place_ref[1]
    mine_ref[...] = parts_ref[core]
    other_ref[...] = parts_ref[1 - core].astype(bf16)


def to_grid(result_ref, grid_ref, bottom_ref, kind):
    levels, rows, cols, width = grid_ref.shape
    for z in range(levels):
        for r in range(rows):
            line = strided_rows(result_ref, z * rows + r, cols, levels * rows)[:, :width]
            to = (z + WZ // 2) % levels
            if r < rows - HALF_LAT:
                grid_ref[to, r + HALF_LAT] = line
            else:
                bottom_ref[kind, to, r - rows + HALF_LAT] = line.astype(bf16)
                grid_ref[to, r - rows + HALF_LAT] = jnp.zeros_like(line)


def table_slots(pieces, pairs):
    slots = []
    for p in range(pairs):
        if p < pieces:
            slots.append((p, 0, p, 4 * LANES))
        else:
            slots.append((p - pieces, 2 * LANES, p - pieces + (pairs - pieces), 2 * LANES))
    return slots


def pack(parts_ref, matrix, vector, skewed):
    cores, half = parts_ref.shape[:2]
    pieces = cores * half
    rows = matrix.shape[0] // pieces
    for d in range(pieces):
        parts_ref[d % cores, d // cores, 0:rows, :] = matrix[d * rows : (d + 1) * rows, :]
        parts_ref[d % cores, d // cores, rows:8, :] = jnp.zeros((8 - rows, matrix.shape[1]), f32)
    for p, (d, at, d2, at2) in enumerate(table_slots(pieces, skewed.shape[0] // 2)):
        pair = slice(2 * p, 2 * p + 2)
        parts_ref[d % cores, d // cores, rows : rows + 2, at : at + 2 * LANES] = skewed[pair, : 2 * LANES]
        parts_ref[d2 % cores, d2 // cores, rows : rows + 2, at2 : at2 + LANES] = skewed[pair, 2 * LANES :]
    for d in range(vector.shape[1] // LANES):
        parts_ref[d % cores, d // cores, rows : rows + 1, 5 * LANES :] = vector[
            :, d * LANES : (d + 1) * LANES
        ]


def unpack_kernel(
    norm_by,
    place_ref,
    mine_ref,
    other_ref,
    qkv_ref,
    proj_ref,
    table_ref,
    gain_ref,
    shift_ref,
    qkv_bias_ref,
    proj_bias_ref,
    wide_ref,
    skewed_ref,
):
    core = place_ref[1]
    wide_ref[core] = mine_ref[...].astype(f32)
    wide_ref[1 - core] = other_ref[...].astype(f32)
    cores, half = wide_ref.shape[:2]
    pieces = cores * half
    width, wide = qkv_ref.shape
    rows = width // pieces
    for d in range(pieces):
        piece = wide_ref[d % cores, d // cores, 0:rows, :] * norm_by
        qkv_ref[d * rows : (d + 1) * rows, :] = piece[:, :wide]
        proj_ref[d * rows : (d + 1) * rows, :] = piece[:, wide:]
    for p, (d, at, d2, at2) in enumerate(table_slots(pieces, skewed_ref.shape[1] // 2)):
        for t in range(2):
            lanes = slice(at + t * LANES, at + (t + 1) * LANES)
            skewed_ref[t, 2 * p : 2 * p + 2, :] = wide_ref[
                d % cores, d // cores, rows : rows + 2, lanes
            ]
        skewed_ref[2, 2 * p : 2 * p + 2, :] = wide_ref[
            d2 % cores, d2 // cores, rows : rows + 2, at2 : at2 + LANES
        ]
    skewed = bias_factor * jnp.concatenate(
        [strided_rows(skewed_ref, a, HEADS, GROUP) for a in range(GROUP)], axis=0
    )
    sides = [
        matmul(skewed, order_of_skew(z), ((1,), (1,)), lax.Precision.HIGHEST) for z in range(WZ)
    ]
    table = jnp.concatenate(
        [
            sides[zm][(zn * WLAT + ln) * HEADS : (zn * WLAT + ln + 1) * HEADS]
            for zn in range(WZ)
            for zm in range(WZ)
            for ln in range(WLAT)
        ],
        axis=1,
    )
    for h in range(HEADS):
        table_ref[h] = table[h : h + 1]
    count = (3 * width + wide) // LANES
    vector = jnp.concatenate(
        [wide_ref[d % cores, d // cores, rows : rows + 1, 5 * LANES :] for d in range(count)], axis=1
    )
    vector = vector * norm_by
    gain_ref[...] = vector[:, :width]
    shift_ref[...] = vector[:, width : 2 * width]
    qkv_bias_ref[...] = vector[:, 2 * width : 2 * width + wide]
    proj_bias_ref[...] = vector[:, 2 * width + wide :]


VMEM_LIMIT = 48 * 1024 * 1024


def call(kernel, out_shape, name, scalars, arrays, scratch=()):
    smem = pl.BlockSpec(memory_space=pltpu.SMEM)
    vmem = pl.BlockSpec(memory_space=pltpu.VMEM)
    return pl.pallas_call(
        kernel,
        out_shape=out_shape,
        in_specs=[smem] * len(scalars) + [vmem] * len(arrays),
        scratch_shapes=scratch,
        compiler_params=pltpu.CompilerParams(vmem_limit_bytes=VMEM_LIMIT),
        name=name,
    )(*scalars, *arrays)


def struct(shape, dtype=f32):
    return jax.ShapeDtypeStruct(shape, dtype)


CORES = 2


def swap_cores(value):
    count = lax.axis_size("lon")
    return lax.ppermute(value, "lon", [(i, i ^ 1) for i in range(count)])


def same_core():
    count = lax.axis_size("lon")
    return [list(range(c, count, CORES)) for c in range(CORES)]


def spread_to_all(piece, axis, count, groups=None):
    wide = jnp.broadcast_to(piece[None], (count,) + piece.shape)
    return lax.all_to_all(wide, axis, 0, 0, axis_index_groups=groups)


def to_neighbour(value, axes, steps):
    counts = [lax.axis_size(a) for a in axes]
    if len(axes) == 1:
        n = counts[0]
        return lax.ppermute(value, axes[0], [(i, (i + steps[0]) % n) for i in range(n)])
    na, nb = counts
    pairs = [
        (a * nb + b, (a + steps[0]) % na * nb + (b + steps[1]) % nb)
        for a in range(na)
        for b in range(nb)
    ]
    return lax.ppermute(value, axes, pairs)


def local(
    tokens,
    cotangent,
    norm_gain_vector,
    norm_bias_vector,
    qkv_weight,
    qkv_bias,
    proj_weight,
    proj_bias,
    earth_bias,
    lat_valid,
):
    levels, rows, cols, width = tokens.shape
    wide = qkv_weight.shape[1]
    lat_count = lax.axis_size("lat")
    lon_count = lax.axis_size("lon")
    total = levels * rows * cols
    place = jnp.stack([lax.axis_index("lat"), lax.axis_index("lon") % CORES]).astype(jnp.int32)
    lat_halo = jnp.stack([a[:, :HALF_LAT, HALF_LON:] for a in (tokens, cotangent)])
    lon_halo = jnp.stack([a[:, HALF_LAT:, :HALF_LON] for a in (tokens, cotangent)])
    corner = jnp.stack([a[:, :HALF_LAT, :HALF_LON] for a in (tokens, cotangent)])
    lat_halo = to_neighbour(lat_halo, ("lat",), (-1,))
    corner = to_neighbour(corner, ("lat", "lon"), (-1, -1))
    lon_halo = to_neighbour(lon_halo, ("lon",), (-1,))

    add = call(
        bias_kernel,
        struct((HEADS * COUNT, COUNT)),
        "bias",
        [place, lat_valid],
        [earth_bias.reshape(HEADS, 1, -1)],
        [pltpu.VMEM((WZ, HEADS * GROUP, SIDE), f32), pltpu.VMEM((SPREAD // LANES, HEADS * GROUP, LANES), f32)],
    )

    def windows_of(kind, array):
        own = jnp.concatenate([array[:, HALF_LAT:, HALF_LON:], lat_halo[kind]], axis=1)
        side = jnp.concatenate([lon_halo[kind], corner[kind]], axis=1)
        moved = jnp.roll(jnp.concatenate([own, side], axis=2), -(WZ // 2), axis=0)
        return moved.transpose(2, 0, 1, 3).reshape(total, width)

    half = lon_count // CORES
    across = wide + width
    out, grad, bottom, mine, other = call(
        attention_kernel,
        (
            struct(tokens.shape),
            struct(tokens.shape),
            struct((2, levels, HALF_LAT, cols, width), bf16),
            struct((half, 8, across)),
            struct((half, 8, across), bf16),
        ),
        "attention",
        [place],
        [
            windows_of(0, tokens),
            windows_of(1, cotangent),
            norm_gain_vector[None],
            norm_bias_vector[None],
            qkv_weight,
            qkv_bias[None],
            proj_weight,
            proj_bias[None],
            add,
        ],
        [
            pltpu.VMEM((HEADS * COUNT, COUNT), f32),
            pltpu.VMEM((CORES, half, 8, across), f32),
            pltpu.VMEM((pl.cdiv(width, LANES), total, LANES), f32),
        ],
    )

    pair = (mine + swap_cores(other).astype(f32)).astype(bf16)
    by_lon = jnp.sum(lax.all_to_all(pair, "lon", 0, 0, axis_index_groups=same_core()).astype(f32), axis=0)
    top = to_neighbour(bottom, ("lat",), (1,))
    by_lon, top = lax.optimization_barrier((by_lon, top))
    by_lat = spread_to_all(by_lon.astype(bf16), "lat", lat_count)
    edge = cols - HALF_LON
    right = jnp.concatenate(
        [top[:, :, :, edge:], jnp.stack([a[:, HALF_LAT:, edge:] for a in (out, grad)]).astype(bf16)],
        axis=2,
    )
    left = to_neighbour(right, ("lon",), (1,))
    by_lat, left = lax.optimization_barrier((by_lat, left))
    by_lat = jnp.sum(by_lat.astype(f32), axis=0)
    row = lax.broadcasted_iota(jnp.int32, by_lat.shape, 0)
    column = lax.broadcasted_iota(jnp.int32, by_lat.shape, 1)
    is_table = (row >= width // lon_count) & (column < 5 * LANES)
    done = jnp.where(is_table, by_lon, by_lat).astype(bf16)
    mine = spread_to_all(done, "lon", half, same_core())
    other = swap_cores(mine)

    def owned(kind, array):
        upper = jnp.concatenate([left[kind, :, :HALF_LAT], top[kind, :, :, :edge]], axis=2)
        lower = jnp.concatenate(
            [left[kind, :, HALF_LAT:].astype(f32), array[:, HALF_LAT:, :edge]], axis=2
        )
        return jnp.concatenate([upper.astype(f32), lower], axis=1)

    norm_by = 1.0 / math.sqrt(total * lat_count * lon_count)

    def unpack(*refs):
        unpack_kernel(norm_by, *refs)

    qkv_weight_grad, proj_weight_grad, table, gain, shift, qkv_bias_grad, proj_bias_grad = call(
        unpack,
        (
            struct((width, wide)),
            struct((width, width)),
            struct((HEADS, 1, earth_bias.shape[-1])),
            struct((1, width)),
            struct((1, width)),
            struct((1, wide)),
            struct((1, width)),
        ),
        "unpack",
        [place],
        [mine, other],
        [pltpu.VMEM((CORES, half, 8, across), f32), pltpu.VMEM((SPREAD // LANES, HEADS * GROUP, LANES), f32)],
    )
    return (
        owned(0, out),
        owned(1, grad),
        gain[0],
        shift[0],
        qkv_weight_grad,
        qkv_bias_grad[0],
        proj_weight_grad,
        proj_bias_grad[0],
        table.reshape(earth_bias.shape),
    )


def solution(mesh):
    placed = (
        P(None, "lat", "lon", None),
        P(None, "lat", "lon", None),
        P(),
        P(),
        P(),
        P(),
        P(),
        P(),
        P(None, "lat", None, None),
        P(),
    )
    return jax.shard_map(
        local,
        mesh=mesh,
        in_specs=placed,
        out_specs=(
            P(None, "lat", "lon", None),
            P(None, "lat", "lon", None),
            P(),
            P(),
            P(),
            P(),
            P(),
            P(),
            P(None, "lat", None, None),
        ),
        check_vma=False,
    )
```

```python
import math

import jax
import jax.numpy as jnp
from jax import lax
from jax.experimental import pallas as pl
from jax.experimental.pallas import tpu as pltpu
from jax.sharding import PartitionSpec as P

HEADS = 6
WZ = 2
WLAT = 6
WLON = 12

HALF_LAT = WLAT // 2
HALF_LON = WLON // 2
GROUP = WZ * WLAT
COUNT = GROUP * WLON
DIFFS = 2 * WLON - 1
SIDE = WLAT * DIFFS
LANES = 128
SPREAD = 3 * LANES

mask_fill = -10000.0
epsilon = 1e-05
bias_factor = 8.0

f32 = jnp.float32
bf16 = jnp.bfloat16


def matmul(a, b, dims=((1,), (0,)), precision=None):
    return lax.dot_general(a, b, (dims, ((), ())), preferred_element_type=f32, precision=precision)


def order_of_skew(z):
    row = lax.broadcasted_iota(jnp.int32, (SIDE, 1), 0)
    lat = sum((row >= k * DIFFS).astype(jnp.int32) for k in range(1, WLAT))
    diff = row - DIFFS * lat
    target = (DIFFS - 1 - diff) * GROUP + z * WLAT + lat
    return (lax.broadcasted_iota(jnp.int32, (SIDE, SPREAD), 1) == target).astype(f32)


def to_tiles(tiles_ref, value):
    for t in range(tiles_ref.shape[0]):
        part = value[:, t * LANES : (t + 1) * LANES]
        tiles_ref[t, :, : part.shape[1]] = part


def strided_rows(tiles_ref, start, count, stride):
    tiles = [tiles_ref[t, pl.ds(start, count, stride=stride), :] for t in range(tiles_ref.shape[0])]
    return jnp.concatenate(tiles, axis=1)


def bias_kernel(
    place_ref,
    valid_ref,
    table_ref,
    qkv_weight_ref,
    proj_weight_ref,
    add_ref,
    qkv_out_ref,
    proj_out_ref,
    sides_ref,
    skewed_ref,
):
    qkv_out_ref[...] = qkv_weight_ref[...]
    proj_out_ref[...] = proj_weight_ref[...]
    for zn in range(WZ):
        for zm in range(WZ):
            for ln in range(WLAT):
                at = ((zn * WZ + zm) * WLAT + ln) * SIDE
                row = (zn * WLAT + ln) * HEADS
                for h in range(HEADS):
                    sides_ref[zm, row + h : row + h + 1, :] = table_ref[0, h, :, at : at + SIDE]
    skewed = sum(
        matmul(sides_ref[z], order_of_skew(z), precision=lax.Precision.HIGHEST) for z in range(WZ)
    )
    to_tiles(skewed_ref, skewed)
    skewed = jnp.concatenate(
        [strided_rows(skewed_ref, h, GROUP, HEADS) for h in range(HEADS)], axis=0
    )
    masked = mask_of_windows(place_ref[0], valid_ref)
    for i in range(WLON):
        shift = (GROUP * (i - WLON + 1)) % SPREAD
        rolled = skewed if shift == 0 else pltpu.roll(skewed, shift, 1)
        for h in range(HEADS):
            add_ref[h * COUNT + i * GROUP : h * COUNT + (i + 1) * GROUP, :] = (
                rolled[h * GROUP : (h + 1) * GROUP, :COUNT] + masked
            )


def mask_of_windows(band, valid_ref):
    total_rows = valid_ref.shape[0]

    def place_of(shape, axis):
        position = lax.broadcasted_iota(jnp.int32, shape, axis)
        group = position - GROUP * sum(
            (position >= GROUP * k).astype(jnp.int32) for k in range(1, shape[axis] // GROUP)
        )
        level = (group >= WLAT).astype(jnp.int32)
        row_in = group - WLAT * level
        row = band * WLAT + row_in
        region = (row >= total_rows - WLAT).astype(jnp.int32) + (
            row >= total_rows - HALF_LAT
        ).astype(jnp.int32)
        return level, row_in, region

    level_n, _, region_n = place_of((GROUP, COUNT), 0)
    level_m, row_m, region_m = place_of((GROUP, COUNT), 1)
    key_ok = jnp.zeros((GROUP, COUNT), jnp.int32)
    for r in range(WLAT):
        at = lax.rem(band * WLAT + r + HALF_LAT, total_rows)
        key_ok = jnp.where(row_m == r, valid_ref[at], key_ok)
    allowed = (level_n == level_m) & (region_n == region_m) & (key_ok == 1)
    return jnp.where(allowed, f32(0.0), f32(mask_fill))


def head_lanes(width, h):
    lane = lax.broadcasted_iota(jnp.int32, (1, width), 1)
    return (lane // 32 == h).astype(f32)


def gather_window(kind, first, own_ref, lat_ref, right_ref, tiles_ref):
    levels, rows, cols, width = own_ref.shape
    inner = rows - HALF_LAT
    for z in range(levels):
        src = (z + WZ // 2) % levels
        for r in range(rows):
            line = own_ref[src, HALF_LAT + r] if r < inner else lat_ref[kind, src, r - inner]
            line = line.astype(f32)[first:]
            if right_ref is None:
                line = line[:WLON]
            else:
                line = jnp.concatenate([line, right_ref[kind, src, r].astype(f32)], axis=0)
            line = jnp.concatenate([line, jnp.zeros((WLON, -width % LANES), f32)], axis=1)
            for t in range(tiles_ref.shape[0]):
                tiles_ref[t, pl.ds(z * rows + r, WLON, stride=GROUP), :] = line[
                    :, t * LANES : (t + 1) * LANES
                ]
    return jnp.concatenate([tiles_ref[t] for t in range(tiles_ref.shape[0])], axis=1)[:, :width]


def scatter_window(kind, result, tiles_ref, upper_ref, bottom_ref):
    levels, inner = upper_ref.shape[1:3]
    width = result.shape[1]
    to_tiles(tiles_ref, result)
    for z in range(levels):
        to = (z + WZ // 2) % levels
        for r in range(WLAT):
            line = strided_rows(tiles_ref, z * WLAT + r, WLON, GROUP)[:, :width]
            if r < inner:
                upper_ref[kind, to, r] = line
            else:
                bottom_ref[kind, to, r - inner] = line.astype(bf16)


def attend(
    x_tiles, dy_tiles, own, cot, lat, right, first, params, add_ref, d_bias_ref, prior, upper, bottom
):
    gain_ref, shift_ref, qkv_weight_ref, qkv_bias_ref, proj_weight_ref, proj_bias_ref = params
    width = own.shape[-1]
    head_dim = width // HEADS
    scale = 1.0 / math.sqrt(head_dim)
    xf = gather_window(0, first, own, lat, right, x_tiles)
    dyf = gather_window(1, first, cot, lat, right, dy_tiles)
    dy = dyf.astype(bf16)
    mean_value = jnp.mean(xf, axis=-1, keepdims=True)
    centered = xf - mean_value
    inverse = lax.rsqrt(jnp.mean(centered * centered, axis=-1, keepdims=True) + epsilon)
    xhat = centered * inverse
    gain = gain_ref[...]
    normed = (xhat * gain + shift_ref[...]).astype(bf16)
    weights = [qkv_weight_ref[:, k * width : (k + 1) * width] for k in range(3)]
    q, k, v = [
        (matmul(normed, weights[i]) + qkv_bias_ref[:, i * width : (i + 1) * width]).astype(bf16)
        for i in range(3)
    ]
    proj_weight = proj_weight_ref[...]
    d_attn = matmul(dy, proj_weight, ((1,), (1,))).astype(bf16)
    per_tile = []
    for head, heads in ((0, 4), (4, 2)):
        lanes = slice(head * head_dim, (head + heads) * head_dim)
        masks = [head_lanes(heads * head_dim, h) for h in range(heads)]
        masks_b = [m.astype(bf16) for m in masks]
        qt, kt, vt, at = q[:, lanes], k[:, lanes], v[:, lanes], d_attn[:, lanes]
        q_stack = jnp.concatenate([qt * m for m in masks_b], axis=0)
        a_stack = jnp.concatenate([at * m for m in masks_b], axis=0)

        def by_head(stacked):
            total = stacked[:COUNT] * masks[0]
            for h in range(1, heads):
                total = total + stacked[h * COUNT : (h + 1) * COUNT] * masks[h]
            return total

        rows = slice(head * COUNT, (head + heads) * COUNT)
        scores = matmul(q_stack, kt, ((1,), (1,))) * scale + add_ref[rows, :]
        top = jnp.max(scores, axis=-1, keepdims=True)
        e = jnp.exp(scores - top)
        probs_f = e * (1.0 / jnp.sum(e, axis=-1, keepdims=True))
        probs = probs_f.astype(bf16)
        attn = by_head(matmul(probs, vt)).astype(bf16)
        d_probs = matmul(a_stack, vt, ((1,), (1,)))
        d_scores = probs_f * (d_probs - jnp.sum(probs_f * d_probs, axis=-1, keepdims=True))
        d_bias_ref[rows, :] = d_scores if prior is None else d_scores + prior[rows, :]
        d_scores_b = d_scores.astype(bf16)
        d_v = matmul(probs, a_stack, ((0,), (0,))).astype(bf16)
        d_q = (by_head(matmul(d_scores_b, kt)) * scale).astype(bf16)
        d_k = (matmul(d_scores_b, q_stack, ((0,), (0,))) * scale).astype(bf16)
        per_tile.append((attn, d_q, d_k, d_v))
    attn, d_q, d_k, d_v = [jnp.concatenate([t[i] for t in per_tile], axis=1) for i in range(4)]
    out = xf + matmul(attn, proj_weight) + proj_bias_ref[...]
    scatter_window(0, out, x_tiles, upper, bottom)
    d_parts = (d_q, d_k, d_v)
    d_normed = sum(matmul(d_parts[i], weights[i], ((1,), (1,))) for i in range(3))
    d_xhat = d_normed * gain
    d_centered = inverse * (
        d_xhat
        - jnp.mean(d_xhat, axis=-1, keepdims=True)
        - xhat * jnp.mean(d_xhat * xhat, axis=-1, keepdims=True)
    )
    scatter_window(1, dyf + d_centered, dy_tiles, upper, bottom)
    d_qkv = jnp.concatenate(d_parts, axis=1)
    qkv_weight_grad = matmul(normed, d_qkv, ((0,), (0,)))
    proj_weight_grad = matmul(attn, dy, ((0,), (0,)))
    matrix = jnp.concatenate([qkv_weight_grad, proj_weight_grad], axis=1)
    vector = jnp.concatenate(
        [
            jnp.sum(d_normed * xhat, axis=0, keepdims=True),
            jnp.sum(d_normed, axis=0, keepdims=True),
            jnp.sum(d_qkv.astype(f32), axis=0, keepdims=True),
            jnp.sum(dyf, axis=0, keepdims=True),
        ],
        axis=1,
    )
    return matrix, vector


def first_kernel(own, cot, lat, *rest):
    params, (add, upper, bottom, d_bias, matrix_ref, vector_ref, x_tiles, dy_tiles) = rest[:6], rest[6:]
    matrix_ref[...], vector_ref[...] = attend(
        x_tiles, dy_tiles, own, cot, lat, None, HALF_LON, params, add, d_bias, None, upper, bottom
    )


def second_kernel(place_ref, own, cot, lat, right, *rest):
    params, (add, prior, prior_matrix, prior_vector) = rest[:6], rest[6:10]
    upper, bottom, mine_ref, other_ref, x_tiles, dy_tiles, d_bias, parts_ref = rest[10:]
    first = own.shape[2] - HALF_LON
    matrix, vector = attend(
        x_tiles, dy_tiles, own, cot, lat, right, first, params, add, d_bias, prior, upper, bottom
    )
    skewed = jnp.zeros((HEADS * GROUP, SPREAD), f32)
    for i in range(WLON):
        part = jnp.concatenate(
            [d_bias[h * COUNT + i * GROUP : h * COUNT + (i + 1) * GROUP, :] for h in range(HEADS)],
            axis=0,
        )
        part = jnp.concatenate([part, jnp.zeros((HEADS * GROUP, SPREAD - COUNT), f32)], axis=1)
        shift = GROUP * (WLON - 1 - i)
        skewed = skewed + (part if shift == 0 else pltpu.roll(part, shift, 1))
    pack(parts_ref, matrix + prior_matrix[...], vector + prior_vector[...], skewed)
    core = place_ref[1]
    mine_ref[...] = parts_ref[core]
    other_ref[...] = parts_ref[1 - core].astype(bf16)


def table_slots(pieces, pairs):
    slots = []
    for p in range(pairs):
        if p < pieces:
            slots.append((p, 0, p, 4 * LANES))
        else:
            slots.append((p - pieces, 2 * LANES, p - pieces + (pairs - pieces), 2 * LANES))
    return slots


def pack(parts_ref, matrix, vector, skewed):
    cores, half = parts_ref.shape[:2]
    pieces = cores * half
    rows = matrix.shape[0] // pieces
    for d in range(pieces):
        parts_ref[d % cores, d // cores, 0:rows, :] = matrix[d * rows : (d + 1) * rows, :]
        parts_ref[d % cores, d // cores, rows:8, :] = jnp.zeros((8 - rows, matrix.shape[1]), f32)
    for p, (d, at, d2, at2) in enumerate(table_slots(pieces, skewed.shape[0] // 2)):
        pair = slice(2 * p, 2 * p + 2)
        parts_ref[d % cores, d // cores, rows : rows + 2, at : at + 2 * LANES] = skewed[pair, : 2 * LANES]
        parts_ref[d2 % cores, d2 // cores, rows : rows + 2, at2 : at2 + LANES] = skewed[pair, 2 * LANES :]
    for d in range(vector.shape[1] // LANES):
        parts_ref[d % cores, d // cores, rows : rows + 1, 5 * LANES :] = vector[
            :, d * LANES : (d + 1) * LANES
        ]


def unpack_kernel(
    norm_by,
    place_ref,
    mine_ref,
    other_ref,
    qkv_ref,
    proj_ref,
    table_ref,
    gain_ref,
    shift_ref,
    qkv_bias_ref,
    proj_bias_ref,
    wide_ref,
    skewed_ref,
):
    core = place_ref[1]
    wide_ref[core] = mine_ref[...].astype(f32)
    wide_ref[1 - core] = other_ref[...].astype(f32)
    cores, half = wide_ref.shape[:2]
    pieces = cores * half
    width, wide = qkv_ref.shape
    rows = width // pieces
    for d in range(pieces):
        piece = wide_ref[d % cores, d // cores, 0:rows, :] * norm_by
        qkv_ref[d * rows : (d + 1) * rows, :] = piece[:, :wide]
        proj_ref[d * rows : (d + 1) * rows, :] = piece[:, wide:]
    for p, (d, at, d2, at2) in enumerate(table_slots(pieces, skewed_ref.shape[1] // 2)):
        for t in range(2):
            lanes = slice(at + t * LANES, at + (t + 1) * LANES)
            skewed_ref[t, 2 * p : 2 * p + 2, :] = wide_ref[
                d % cores, d // cores, rows : rows + 2, lanes
            ]
        skewed_ref[2, 2 * p : 2 * p + 2, :] = wide_ref[
            d2 % cores, d2 // cores, rows : rows + 2, at2 : at2 + LANES
        ]
    skewed = jnp.concatenate(
        [strided_rows(skewed_ref, a, HEADS, GROUP) for a in range(GROUP)], axis=0
    )
    skewed = (skewed * bias_factor).astype(bf16)
    sides = [matmul(skewed, order_of_skew(z).astype(bf16), ((1,), (1,))) for z in range(WZ)]
    table = jnp.concatenate(
        [
            sides[zm][(zn * WLAT + ln) * HEADS : (zn * WLAT + ln + 1) * HEADS]
            for zn in range(WZ)
            for zm in range(WZ)
            for ln in range(WLAT)
        ],
        axis=1,
    )
    for h in range(HEADS):
        table_ref[0, h] = table[h : h + 1]
    count = (3 * width + wide) // LANES
    vector = jnp.concatenate(
        [wide_ref[d % cores, d // cores, rows : rows + 1, 5 * LANES :] for d in range(count)], axis=1
    )
    vector = vector * norm_by
    gain_ref[...] = vector[:, :width]
    shift_ref[...] = vector[:, width : 2 * width]
    qkv_bias_ref[...] = vector[:, 2 * width : 2 * width + wide]
    proj_bias_ref[...] = vector[:, 2 * width + wide :]


VMEM_LIMIT = 48 * 1024 * 1024


def call(kernel, out_shape, name, scalars, arrays, scratch=()):
    smem = pl.BlockSpec(memory_space=pltpu.SMEM)
    vmem = pl.BlockSpec(memory_space=pltpu.VMEM)
    return pl.pallas_call(
        kernel,
        out_shape=out_shape,
        in_specs=[smem] * len(scalars) + [vmem] * len(arrays),
        scratch_shapes=scratch,
        compiler_params=pltpu.CompilerParams(vmem_limit_bytes=VMEM_LIMIT),
        name=name,
    )(*scalars, *arrays)


def struct(shape, dtype=f32):
    return jax.ShapeDtypeStruct(shape, dtype)


CORES = 2


def swap_cores(value):
    count = lax.axis_size("lon")
    return lax.ppermute(value, "lon", [(i, i ^ 1) for i in range(count)])


def same_core():
    count = lax.axis_size("lon")
    return [list(range(c, count, CORES)) for c in range(CORES)]


def spread_to_all(piece, axis, count, groups=None):
    wide = jnp.broadcast_to(piece[None], (count,) + piece.shape)
    return lax.all_to_all(wide, axis, 0, 0, axis_index_groups=groups)


def to_neighbour(value, axes, steps):
    counts = [lax.axis_size(a) for a in axes]
    if len(axes) == 1:
        n = counts[0]
        return lax.ppermute(value, axes[0], [(i, (i + steps[0]) % n) for i in range(n)])
    na, nb = counts
    pairs = [
        (a * nb + b, (a + steps[0]) % na * nb + (b + steps[1]) % nb)
        for a in range(na)
        for b in range(nb)
    ]
    return lax.ppermute(value, axes, pairs)


def local(
    tokens,
    cotangent,
    norm_gain_vector,
    norm_bias_vector,
    qkv_weight,
    qkv_bias,
    proj_weight,
    proj_bias,
    earth_bias,
    lat_valid,
):
    levels, rows, cols, width = tokens.shape
    wide = qkv_weight.shape[1]
    lat_count = lax.axis_size("lat")
    lon_count = lax.axis_size("lon")
    total = levels * rows * cols
    place = jnp.stack([lax.axis_index("lat"), lax.axis_index("lon") % CORES]).astype(jnp.int32)
    lat_halo = to_neighbour(
        jnp.stack([a[:, :HALF_LAT] for a in (tokens, cotangent)]), ("lat",), (-1,)
    )
    table = earth_bias.transpose(0, 2, 1, 3)
    add, qkv_weight, proj_weight = call(
        bias_kernel,
        (
            struct((HEADS * COUNT, COUNT)),
            struct(qkv_weight.shape, bf16),
            struct(proj_weight.shape, bf16),
        ),
        "bias",
        [place, lat_valid],
        [table, qkv_weight, proj_weight],
        [
            pltpu.VMEM((WZ, HEADS * GROUP, SIDE), f32),
            pltpu.VMEM((SPREAD // LANES, HEADS * GROUP, LANES), f32),
        ],
    )
    lat_halo, add, qkv_weight, proj_weight = lax.optimization_barrier(
        (lat_halo, add, qkv_weight, proj_weight)
    )
    own_side = jnp.stack([a[:, HALF_LAT:, :HALF_LON] for a in (tokens, cotangent)])
    right_halo = to_neighbour(
        jnp.concatenate([own_side, lat_halo[:, :, :, :HALF_LON]], axis=2), ("lon",), (-1,)
    )

    half = lon_count // CORES
    across = wide + width
    params = [
        norm_gain_vector[None],
        norm_bias_vector[None],
        qkv_weight,
        qkv_bias[None],
        proj_weight,
        proj_bias[None],
    ]
    upper = struct((2, levels, rows - HALF_LAT, WLON, width))
    bottom = struct((2, levels, HALF_LAT, WLON, width), bf16)
    tiles = pltpu.VMEM((pl.cdiv(width, LANES), COUNT, LANES), f32)
    d_bias = (HEADS * COUNT, COUNT)
    upper_a, bottom_a, *prior = call(
        first_kernel,
        (upper, bottom, struct(d_bias), struct((width, across)), struct((1, 3 * width + wide))),
        "first",
        [],
        [tokens, cotangent, lat_halo, *params, add],
        [tiles, tiles],
    )
    upper_b, bottom_b, mine, other = call(
        second_kernel,
        (upper, bottom, struct((half, 8, across)), struct((half, 8, across), bf16)),
        "second",
        [place],
        [tokens, cotangent, lat_halo, right_halo, *params, add, *prior],
        [tiles, tiles, pltpu.VMEM(d_bias, f32), pltpu.VMEM((CORES, half, 8, across), f32)],
    )

    pair = (mine + swap_cores(other).astype(f32)).astype(bf16)
    by_lon = jnp.sum(lax.all_to_all(pair, "lon", 0, 0, axis_index_groups=same_core()).astype(f32), axis=0)
    by_lat = spread_to_all(by_lon.astype(bf16), "lat", lat_count)
    top = to_neighbour(jnp.concatenate([bottom_a, bottom_b], axis=3), ("lat",), (1,))
    by_lat, top = lax.optimization_barrier((by_lat, top))
    edge = cols - HALF_LON
    right = jnp.concatenate([top[:, :, :, edge:], upper_b[:, :, :, HALF_LON:].astype(bf16)], axis=2)
    left = to_neighbour(right, ("lon",), (1,))
    by_lat = jnp.sum(by_lat.astype(f32), axis=0)
    row = lax.broadcasted_iota(jnp.int32, by_lat.shape, 0)
    column = lax.broadcasted_iota(jnp.int32, by_lat.shape, 1)
    is_table = (row >= width // lon_count) & (column < 5 * LANES)
    done = jnp.where(is_table, by_lon, by_lat).astype(bf16)
    mine = spread_to_all(done, "lon", half, same_core())
    mine, left = lax.optimization_barrier((mine, left))
    other = swap_cores(mine)

    def owned(kind):
        above = jnp.concatenate([left[kind, :, :HALF_LAT], top[kind, :, :, :edge]], axis=2)
        below = jnp.concatenate(
            [
                left[kind, :, HALF_LAT:].astype(f32),
                upper_a[kind],
                upper_b[kind, :, :, :HALF_LON],
            ],
            axis=2,
        )
        return jnp.concatenate([above.astype(f32), below], axis=1)

    norm_by = 1.0 / math.sqrt(total * lat_count * lon_count)

    def unpack(*refs):
        unpack_kernel(norm_by, *refs)

    qkv_weight_grad, proj_weight_grad, table, gain, shift, qkv_bias_grad, proj_bias_grad = call(
        unpack,
        (
            struct((width, wide)),
            struct((width, width)),
            struct(table.shape),
            struct((1, width)),
            struct((1, width)),
            struct((1, wide)),
            struct((1, width)),
        ),
        "unpack",
        [place],
        [mine, other],
        [pltpu.VMEM((CORES, half, 8, across), f32), pltpu.VMEM((SPREAD // LANES, HEADS * GROUP, LANES), f32)],
    )
    return (
        owned(0),
        owned(1),
        gain[0],
        shift[0],
        qkv_weight_grad,
        qkv_bias_grad[0],
        proj_weight_grad,
        proj_bias_grad[0],
        table.transpose(0, 2, 1, 3),
    )


def solution(mesh):
    placed = (
        P(None, "lat", "lon", None),
        P(None, "lat", "lon", None),
        P(),
        P(),
        P(),
        P(),
        P(),
        P(),
        P(None, "lat", None, None),
        P(),
    )
    return jax.shard_map(
        local,
        mesh=mesh,
        in_specs=placed,
        out_specs=(
            P(None, "lat", "lon", None),
            P(None, "lat", "lon", None),
            P(),
            P(),
            P(),
            P(),
            P(),
            P(),
            P(None, "lat", None, None),
        ),
        check_vma=False,
    )
```

```python
import math

import jax
import jax.numpy as jnp
from jax import lax
from jax.experimental import pallas as pl
from jax.experimental.pallas import tpu as pltpu
from jax.sharding import PartitionSpec as P

HEADS = 6
WZ = 2
WLAT = 6
WLON = 12

HALF_LAT = WLAT // 2
HALF_LON = WLON // 2
GROUP = WZ * WLAT
COUNT = GROUP * WLON
DIFFS = 2 * WLON - 1
SIDE = WLAT * DIFFS
LANES = 128
SPREAD = 3 * LANES

mask_fill = -10000.0
epsilon = 1e-05
bias_factor = 8.0

f32 = jnp.float32
bf16 = jnp.bfloat16


def matmul(a, b, dims=((1,), (0,)), precision=None):
    return lax.dot_general(a, b, (dims, ((), ())), preferred_element_type=f32, precision=precision)


def order_of_skew(z):
    row = lax.broadcasted_iota(jnp.int32, (SIDE, 1), 0)
    lat = sum((row >= k * DIFFS).astype(jnp.int32) for k in range(1, WLAT))
    diff = row - DIFFS * lat
    target = (DIFFS - 1 - diff) * GROUP + z * WLAT + lat
    return (lax.broadcasted_iota(jnp.int32, (SIDE, SPREAD), 1) == target).astype(f32)


def to_tiles(tiles_ref, value):
    for t in range(tiles_ref.shape[0]):
        part = value[:, t * LANES : (t + 1) * LANES]
        tiles_ref[t, :, : part.shape[1]] = part


def strided_rows(tiles_ref, start, count, stride):
    tiles = [tiles_ref[t, pl.ds(start, count, stride=stride), :] for t in range(tiles_ref.shape[0])]
    return jnp.concatenate(tiles, axis=1)


def bias_kernel(
    place_ref,
    valid_ref,
    table_ref,
    *rest,
):
    params, add_ref, params_out, (sides_ref, skewed_ref) = rest[:6], rest[6], rest[7:13], rest[13:]
    for ref, to in zip(params, params_out):
        to[...] = ref[...]
    for zn in range(WZ):
        for zm in range(WZ):
            for ln in range(WLAT):
                at = ((zn * WZ + zm) * WLAT + ln) * SIDE
                row = (zn * WLAT + ln) * HEADS
                for h in range(HEADS):
                    sides_ref[zm, row + h : row + h + 1, :] = table_ref[0, h, :, at : at + SIDE]
    skewed = sum(
        matmul(sides_ref[z], order_of_skew(z), precision=lax.Precision.HIGHEST) for z in range(WZ)
    )
    to_tiles(skewed_ref, skewed)
    skewed = jnp.concatenate(
        [strided_rows(skewed_ref, h, GROUP, HEADS) for h in range(HEADS)], axis=0
    )
    masked = mask_of_windows(place_ref[0], valid_ref)
    for i in range(WLON):
        shift = (GROUP * (i - WLON + 1)) % SPREAD
        rolled = skewed if shift == 0 else pltpu.roll(skewed, shift, 1)
        for h in range(HEADS):
            add_ref[h * COUNT + i * GROUP : h * COUNT + (i + 1) * GROUP, :] = (
                rolled[h * GROUP : (h + 1) * GROUP, :COUNT] + masked
            )


def mask_of_windows(band, valid_ref):
    total_rows = valid_ref.shape[0]

    def place_of(shape, axis):
        position = lax.broadcasted_iota(jnp.int32, shape, axis)
        group = position - GROUP * sum(
            (position >= GROUP * k).astype(jnp.int32) for k in range(1, shape[axis] // GROUP)
        )
        level = (group >= WLAT).astype(jnp.int32)
        row_in = group - WLAT * level
        row = band * WLAT + row_in
        region = (row >= total_rows - WLAT).astype(jnp.int32) + (
            row >= total_rows - HALF_LAT
        ).astype(jnp.int32)
        return level, row_in, region

    level_n, _, region_n = place_of((GROUP, COUNT), 0)
    level_m, row_m, region_m = place_of((GROUP, COUNT), 1)
    key_ok = jnp.zeros((GROUP, COUNT), jnp.int32)
    for r in range(WLAT):
        at = lax.rem(band * WLAT + r + HALF_LAT, total_rows)
        key_ok = jnp.where(row_m == r, valid_ref[at], key_ok)
    allowed = (level_n == level_m) & (region_n == region_m) & (key_ok == 1)
    return jnp.where(allowed, f32(0.0), f32(mask_fill))


def head_lanes(width, h):
    lane = lax.broadcasted_iota(jnp.int32, (1, width), 1)
    return (lane // 32 == h).astype(f32)


def unpacked(packed_ref, at, kind):
    low = packed_ref[(*at, kind)].astype(f32)
    high = packed_ref[(*at, 2)].astype(f32)
    return [low, high if kind == 0 else pltpu.roll(high, LANES // 2, 1)]


def gather_window(kind, first, own_ref, lat_ref, right_ref, tiles_ref):
    levels, rows, cols, width = own_ref.shape
    inner = rows - HALF_LAT
    for z in range(levels):
        src = (z + WZ // 2) % levels
        for r in range(rows):
            if r < inner:
                line = own_ref[src, HALF_LAT + r].astype(f32)
                high = jnp.concatenate(
                    [line[:, LANES:], jnp.zeros((cols, -width % LANES), f32)], axis=1
                )
                line = [line[:, :LANES], high]
            else:
                line = unpacked(lat_ref, (src, r - inner), kind)
            if right_ref is None:
                line = [part[first : first + WLON] for part in line]
            else:
                ends = unpacked(right_ref, (src, r), kind)
                line = [jnp.concatenate([p[first:], e], axis=0) for p, e in zip(line, ends)]
            for t, part in enumerate(line):
                tiles_ref[t, pl.ds(z * rows + r, WLON, stride=GROUP), :] = part
    return jnp.concatenate([tiles_ref[0], tiles_ref[1]], axis=1)[:, :width]


def pack_line(packed_ref, at, kind, low, high):
    packed_ref[(*at, kind)] = low.astype(bf16)
    half = LANES // 2
    if kind == 0:
        packed_ref[(*at, 2, slice(None), slice(0, half))] = high[:, :half].astype(bf16)
    else:
        moved = pltpu.roll(high, half, 1)
        packed_ref[(*at, 2, slice(None), slice(half, LANES))] = moved[:, half:].astype(bf16)


def scatter_window(kind, result, tiles_ref, upper_ref, bottom_ref, side_ref):
    levels, inner = upper_ref.shape[1:3]
    width = result.shape[1]
    to_tiles(tiles_ref, result)
    for z in range(levels):
        to = (z + WZ // 2) % levels
        for r in range(WLAT):
            low, high = [
                tiles_ref[t, pl.ds(z * WLAT + r, WLON, stride=GROUP), :] for t in range(2)
            ]
            if side_ref is not None:
                pack_line(side_ref, (to, r), kind, low[HALF_LON:], high[HALF_LON:])
            if r < inner:
                upper_ref[kind, to, r] = jnp.concatenate([low, high], axis=1)[:, :width]
            else:
                pack_line(bottom_ref, (to, r - inner), kind, low, high)


def packed_lines(tokens, cotangent):
    high = jnp.concatenate([tokens[..., LANES:], cotangent[..., LANES:]], axis=-1)
    return jnp.stack([tokens[..., :LANES], cotangent[..., :LANES], high], axis=2)


def cut_kernel(tokens_ref, cot_ref, packed_ref):
    for z in range(packed_ref.shape[0]):
        for r in range(packed_ref.shape[1]):
            lines = [ref[z, r] for ref in (tokens_ref, cot_ref)]
            for k in range(2):
                packed_ref[z, r, k] = lines[k][:, :LANES]
            packed_ref[z, r, 2] = jnp.concatenate([line[:, LANES:] for line in lines], axis=1)


def owned_kernel(top_ref, left_ref, upper_a_ref, upper_b_ref, out_ref, grad_ref):
    levels, rows, cols, width = out_ref.shape
    for kind, ref in enumerate((out_ref, grad_ref)):
        for z in range(levels):
            for r in range(rows):
                if r < HALF_LAT:
                    ref[z, r] = jnp.concatenate(unpacked(top_ref, (z, r), kind), axis=1)[:, :width]
                else:
                    line = unpacked(left_ref, (z, r - HALF_LAT), kind)
                    own = [u[kind, z, r - HALF_LAT] for u in (upper_a_ref, upper_b_ref)]
                    parts = [jnp.concatenate(line, axis=1)[:, :width], own[0], own[1][:HALF_LON]]
                    ref[z, r] = jnp.concatenate(parts, axis=0)


def pair_kernel(mine_ref, other_ref, sum_ref):
    sum_ref[...] = (mine_ref[...] + other_ref[...].astype(f32)).astype(bf16)


def spread(piece_ref, out_ref, sem):
    copies = [pltpu.make_async_copy(piece_ref, out_ref.at[d], sem.at[d]) for d in range(out_ref.shape[0])]
    for copy in copies:
        copy.start()
    for copy in copies:
        copy.wait()


def sum_pieces(pieces_ref):
    total = pieces_ref[0].astype(f32)
    for d in range(1, pieces_ref.shape[0]):
        total = total + pieces_ref[d].astype(f32)
    return total


def lon_kernel(pieces_ref, piece_ref, out_ref, sem):
    piece_ref[...] = sum_pieces(pieces_ref).astype(bf16)
    spread(piece_ref, out_ref, sem)


def lat_kernel(rows, pieces_ref, by_lon_ref, out_ref, piece_ref, sem):
    shape = piece_ref.shape
    row = lax.broadcasted_iota(jnp.int32, shape, 0)
    column = lax.broadcasted_iota(jnp.int32, shape, 1)
    is_table = (row >= rows) & (column < 5 * LANES)
    total = jnp.where(is_table, by_lon_ref[...].astype(f32), sum_pieces(pieces_ref))
    piece_ref[...] = total.astype(bf16)
    spread(piece_ref, out_ref, sem)


def attend(
    x_tiles, dy_tiles, own, cot, lat, right, first, params, add_ref, d_bias_ref, prior, *grids
):
    gain_ref, shift_ref, qkv_weight_ref, qkv_bias_ref, proj_weight_ref, proj_bias_ref = params
    width = own.shape[-1]
    head_dim = width // HEADS
    scale = 1.0 / math.sqrt(head_dim)
    xf = gather_window(0, first, own, lat, right, x_tiles)
    dyf = gather_window(1, first, cot, lat, right, dy_tiles)
    dy = dyf.astype(bf16)
    mean_value = jnp.mean(xf, axis=-1, keepdims=True)
    centered = xf - mean_value
    inverse = lax.rsqrt(jnp.mean(centered * centered, axis=-1, keepdims=True) + epsilon)
    xhat = centered * inverse
    gain = gain_ref[...]
    normed = (xhat * gain + shift_ref[...]).astype(bf16)
    weights = [qkv_weight_ref[:, k * width : (k + 1) * width] for k in range(3)]
    q, k, v = [
        (matmul(normed, weights[i]) + qkv_bias_ref[:, i * width : (i + 1) * width]).astype(bf16)
        for i in range(3)
    ]
    proj_weight = proj_weight_ref[...]
    d_attn = matmul(dy, proj_weight, ((1,), (1,))).astype(bf16)
    per_tile = []
    for head, heads in ((0, 4), (4, 2)):
        lanes = slice(head * head_dim, (head + heads) * head_dim)
        masks = [head_lanes(heads * head_dim, h) for h in range(heads)]
        masks_b = [m.astype(bf16) for m in masks]
        qt, kt, vt, at = q[:, lanes], k[:, lanes], v[:, lanes], d_attn[:, lanes]
        q_stack = jnp.concatenate([qt * m for m in masks_b], axis=0)
        a_stack = jnp.concatenate([at * m for m in masks_b], axis=0)

        def by_head(stacked):
            total = stacked[:COUNT] * masks[0]
            for h in range(1, heads):
                total = total + stacked[h * COUNT : (h + 1) * COUNT] * masks[h]
            return total

        rows = slice(head * COUNT, (head + heads) * COUNT)
        scores = matmul(q_stack, kt, ((1,), (1,))) * scale + add_ref[rows, :]
        top = jnp.max(scores, axis=-1, keepdims=True)
        e = jnp.exp(scores - top)
        probs_f = e * (1.0 / jnp.sum(e, axis=-1, keepdims=True))
        probs = probs_f.astype(bf16)
        attn = by_head(matmul(probs, vt)).astype(bf16)
        d_probs = matmul(a_stack, vt, ((1,), (1,)))
        d_scores = probs_f * (d_probs - jnp.sum(probs_f * d_probs, axis=-1, keepdims=True))
        d_bias_ref[rows, :] = d_scores if prior is None else d_scores + prior[rows, :]
        d_scores_b = d_scores.astype(bf16)
        d_v = matmul(probs, a_stack, ((0,), (0,))).astype(bf16)
        d_q = (by_head(matmul(d_scores_b, kt)) * scale).astype(bf16)
        d_k = (matmul(d_scores_b, q_stack, ((0,), (0,))) * scale).astype(bf16)
        per_tile.append((attn, d_q, d_k, d_v))
    attn, d_q, d_k, d_v = [jnp.concatenate([t[i] for t in per_tile], axis=1) for i in range(4)]
    out = xf + matmul(attn, proj_weight) + proj_bias_ref[...]
    scatter_window(0, out, x_tiles, *grids)
    d_parts = (d_q, d_k, d_v)
    d_normed = sum(matmul(d_parts[i], weights[i], ((1,), (1,))) for i in range(3))
    d_xhat = d_normed * gain
    d_centered = inverse * (
        d_xhat
        - jnp.mean(d_xhat, axis=-1, keepdims=True)
        - xhat * jnp.mean(d_xhat * xhat, axis=-1, keepdims=True)
    )
    scatter_window(1, dyf + d_centered, dy_tiles, *grids)
    d_qkv = jnp.concatenate(d_parts, axis=1)
    qkv_weight_grad = matmul(normed, d_qkv, ((0,), (0,)))
    proj_weight_grad = matmul(attn, dy, ((0,), (0,)))
    matrix = jnp.concatenate([qkv_weight_grad, proj_weight_grad], axis=1)
    vector = jnp.concatenate(
        [
            jnp.sum(d_normed * xhat, axis=0, keepdims=True),
            jnp.sum(d_normed, axis=0, keepdims=True),
            jnp.sum(d_qkv.astype(f32), axis=0, keepdims=True),
            jnp.sum(dyf, axis=0, keepdims=True),
        ],
        axis=1,
    )
    return matrix, vector


def first_kernel(own, cot, lat, *rest):
    params, (add, upper, bottom, d_bias, matrix_ref, vector_ref, x_tiles, dy_tiles) = rest[:6], rest[6:]
    matrix_ref[...], vector_ref[...] = attend(
        x_tiles, dy_tiles, own, cot, lat, None, HALF_LON, params, add, d_bias, None, upper, bottom, None
    )


def second_kernel(place_ref, own, cot, lat, right, *rest):
    params, (add, prior, prior_matrix, prior_vector) = rest[:6], rest[6:10]
    upper, bottom, side, mine_ref, other_ref, x_tiles, dy_tiles, d_bias, parts_ref = rest[10:]
    first = own.shape[2] - HALF_LON
    matrix, vector = attend(
        x_tiles, dy_tiles, own, cot, lat, right, first, params, add, d_bias, prior, upper, bottom, side
    )
    skewed = jnp.zeros((HEADS * GROUP, SPREAD), f32)
    for i in range(WLON):
        part = jnp.concatenate(
            [d_bias[h * COUNT + i * GROUP : h * COUNT + (i + 1) * GROUP, :] for h in range(HEADS)],
            axis=0,
        )
        part = jnp.concatenate([part, jnp.zeros((HEADS * GROUP, SPREAD - COUNT), f32)], axis=1)
        shift = GROUP * (WLON - 1 - i)
        skewed = skewed + (part if shift == 0 else pltpu.roll(part, shift, 1))
    pack(parts_ref, matrix + prior_matrix[...], vector + prior_vector[...], skewed)
    core = place_ref[1]
    mine_ref[...] = parts_ref[core]
    other_ref[...] = parts_ref[1 - core].astype(bf16)


def table_slots(pieces, pairs):
    slots = []
    for p in range(pairs):
        if p < pieces:
            slots.append((p, 0, p, 4 * LANES))
        else:
            slots.append((p - pieces, 2 * LANES, p - pieces + (pairs - pieces), 2 * LANES))
    return slots


def pack(parts_ref, matrix, vector, skewed):
    cores, half = parts_ref.shape[:2]
    pieces = cores * half
    rows = matrix.shape[0] // pieces
    for d in range(pieces):
        parts_ref[d % cores, d // cores, 0:rows, :] = matrix[d * rows : (d + 1) * rows, :]
        parts_ref[d % cores, d // cores, rows:8, :] = jnp.zeros((8 - rows, matrix.shape[1]), f32)
    for p, (d, at, d2, at2) in enumerate(table_slots(pieces, skewed.shape[0] // 2)):
        pair = slice(2 * p, 2 * p + 2)
        parts_ref[d % cores, d // cores, rows : rows + 2, at : at + 2 * LANES] = skewed[pair, : 2 * LANES]
        parts_ref[d2 % cores, d2 // cores, rows : rows + 2, at2 : at2 + LANES] = skewed[pair, 2 * LANES :]
    for d in range(vector.shape[1] // LANES):
        parts_ref[d % cores, d // cores, rows : rows + 1, 5 * LANES :] = vector[
            :, d * LANES : (d + 1) * LANES
        ]


def unpack_kernel(
    norm_by,
    place_ref,
    mine_ref,
    other_ref,
    qkv_ref,
    proj_ref,
    table_ref,
    gain_ref,
    shift_ref,
    qkv_bias_ref,
    proj_bias_ref,
    wide_ref,
    skewed_ref,
):
    core = place_ref[1]
    wide_ref[core] = mine_ref[...].astype(f32)
    wide_ref[1 - core] = other_ref[...].astype(f32)
    cores, half = wide_ref.shape[:2]
    pieces = cores * half
    width, wide = qkv_ref.shape
    rows = width // pieces
    for d in range(pieces):
        piece = wide_ref[d % cores, d // cores, 0:rows, :] * norm_by
        qkv_ref[d * rows : (d + 1) * rows, :] = piece[:, :wide]
        proj_ref[d * rows : (d + 1) * rows, :] = piece[:, wide:]
    for p, (d, at, d2, at2) in enumerate(table_slots(pieces, skewed_ref.shape[1] // 2)):
        for t in range(2):
            lanes = slice(at + t * LANES, at + (t + 1) * LANES)
            skewed_ref[t, 2 * p : 2 * p + 2, :] = wide_ref[
                d % cores, d // cores, rows : rows + 2, lanes
            ]
        skewed_ref[2, 2 * p : 2 * p + 2, :] = wide_ref[
            d2 % cores, d2 // cores, rows : rows + 2, at2 : at2 + LANES
        ]
    skewed = jnp.concatenate(
        [strided_rows(skewed_ref, a, HEADS, GROUP) for a in range(GROUP)], axis=0
    )
    skewed = (skewed * bias_factor).astype(bf16)
    sides = [matmul(skewed, order_of_skew(z).astype(bf16), ((1,), (1,))) for z in range(WZ)]
    table = jnp.concatenate(
        [
            sides[zm][(zn * WLAT + ln) * HEADS : (zn * WLAT + ln + 1) * HEADS]
            for zn in range(WZ)
            for zm in range(WZ)
            for ln in range(WLAT)
        ],
        axis=1,
    )
    for h in range(HEADS):
        table_ref[0, h] = table[h : h + 1]
    count = (3 * width + wide) // LANES
    vector = jnp.concatenate(
        [wide_ref[d % cores, d // cores, rows : rows + 1, 5 * LANES :] for d in range(count)], axis=1
    )
    vector = vector * norm_by
    gain_ref[...] = vector[:, :width]
    shift_ref[...] = vector[:, width : 2 * width]
    qkv_bias_ref[...] = vector[0, 2 * width : 2 * width + wide]
    proj_bias_ref[...] = vector[:, 2 * width + wide :]


VMEM_LIMIT = 48 * 1024 * 1024


def call(kernel, out_shape, name, scalars, arrays, scratch=(), in_space=pltpu.VMEM, out_spaces=None):
    smem = pl.BlockSpec(memory_space=pltpu.SMEM)
    vmem = pl.BlockSpec(memory_space=in_space)
    if out_spaces is None:
        out_specs = jax.tree.map(lambda _: pl.BlockSpec(memory_space=pltpu.VMEM), out_shape)
    else:
        out_specs = jax.tree.map(lambda space: pl.BlockSpec(memory_space=space), out_spaces)
    return pl.pallas_call(
        kernel,
        out_shape=out_shape,
        in_specs=[smem] * len(scalars) + [vmem] * len(arrays),
        out_specs=out_specs,
        scratch_shapes=scratch,
        compiler_params=pltpu.CompilerParams(vmem_limit_bytes=VMEM_LIMIT),
        name=name,
    )(*scalars, *arrays)


def struct(shape, dtype=f32):
    return jax.ShapeDtypeStruct(shape, dtype)


CORES = 2


def swap_cores(value):
    count = lax.axis_size("lon")
    return lax.ppermute(value, "lon", [(i, i ^ 1) for i in range(count)])


def same_core():
    count = lax.axis_size("lon")
    return [list(range(c, count, CORES)) for c in range(CORES)]


def to_neighbour(value, axes, steps):
    counts = [lax.axis_size(a) for a in axes]
    if len(axes) == 1:
        n = counts[0]
        return lax.ppermute(value, axes[0], [(i, (i + steps[0]) % n) for i in range(n)])
    na, nb = counts
    pairs = [
        (a * nb + b, (a + steps[0]) % na * nb + (b + steps[1]) % nb)
        for a in range(na)
        for b in range(nb)
    ]
    return lax.ppermute(value, axes, pairs)


def local(
    tokens,
    cotangent,
    norm_gain_vector,
    norm_bias_vector,
    qkv_weight,
    qkv_bias,
    proj_weight,
    proj_bias,
    earth_bias,
    lat_valid,
):
    levels, rows, cols, width = tokens.shape
    wide = qkv_weight.shape[1]
    lat_count = lax.axis_size("lat")
    lon_count = lax.axis_size("lon")
    total = levels * rows * cols
    place = jnp.stack([lax.axis_index("lat"), lax.axis_index("lon") % CORES]).astype(jnp.int32)
    def packed(count, columns):
        return struct((levels, count, 3, columns, LANES), bf16)

    cuts = lax.optimization_barrier(tuple(a[:, :HALF_LAT] for a in (tokens, cotangent)))
    lat_halo = to_neighbour(
        call(cut_kernel, packed(HALF_LAT, cols), "cut", [], list(cuts)), ("lat",), (-1,)
    )
    table = earth_bias.transpose(0, 2, 1, 3)
    params = [
        norm_gain_vector[None],
        norm_bias_vector[None],
        qkv_weight,
        qkv_bias[None],
        proj_weight,
        proj_bias[None],
    ]
    add, *params = call(
        bias_kernel,
        (struct((HEADS * COUNT, COUNT)), *[struct(p.shape, p.dtype) for p in params]),
        "bias",
        [place, lat_valid],
        [table, *params],
        [
            pltpu.VMEM((WZ, HEADS * GROUP, SIDE), f32),
            pltpu.VMEM((SPREAD // LANES, HEADS * GROUP, LANES), f32),
        ],
    )
    lat_halo, add = lax.optimization_barrier((lat_halo, add))
    own_side = packed_lines(*[a[:, HALF_LAT:, :HALF_LON] for a in (tokens, cotangent)])
    right_halo = to_neighbour(
        jnp.concatenate([own_side, lat_halo[:, :, :, :HALF_LON]], axis=1), ("lon",), (-1,)
    )

    half = lon_count // CORES
    across = wide + width
    upper = struct((2, levels, rows - HALF_LAT, WLON, width))
    bottom = packed(HALF_LAT, WLON)
    side = packed(rows, WLON - HALF_LON)
    tiles = pltpu.VMEM((pl.cdiv(width, LANES), COUNT, LANES), f32)
    d_bias = (HEADS * COUNT, COUNT)
    upper_a, bottom_a, *prior = call(
        first_kernel,
        (upper, bottom, struct(d_bias), struct((width, across)), struct((1, 3 * width + wide))),
        "first",
        [],
        [tokens, cotangent, lat_halo, *params, add],
        [tiles, tiles],
    )
    upper_b, bottom_b, side_b, mine, other = call(
        second_kernel,
        (upper, bottom, side, struct((half, 8, across)), struct((half, 8, across), bf16)),
        "second",
        [place],
        [tokens, cotangent, lat_halo, right_halo, *params, add, *prior],
        [tiles, tiles, pltpu.VMEM(d_bias, f32), pltpu.VMEM((CORES, half, 8, across), f32)],
    )

    pieces = struct((half, 8, across), bf16)
    piece = struct((8, across), bf16)
    pair = call(pair_kernel, pieces, "pair", [], [mine, swap_cores(other)])
    pair = lax.all_to_all(pair, "lon", 0, 0, axis_index_groups=same_core())
    left = to_neighbour(side_b, ("lon",), (1,))
    pair, left = lax.optimization_barrier((pair, left))
    by_lon, pair = call(
        lon_kernel,
        (piece, struct((lat_count, 8, across), bf16)),
        "lon",
        [],
        [pair],
        [pltpu.SemaphoreType.DMA((lat_count,))],
        out_spaces=(pltpu.VMEM, pl.ANY),
    )
    by_lat = lax.all_to_all(pair, "lat", 0, 0)
    inner = rows - HALF_LAT
    bottom = [left[:, inner:], bottom_a, bottom_b[:, :, :, :HALF_LON]]
    top = to_neighbour(jnp.concatenate(bottom, axis=3), ("lat",), (1,))
    by_lat, top = lax.optimization_barrier((by_lat, top))

    def lat_sum(*refs):
        lat_kernel(width // lon_count, *refs)

    mine = call(
        lat_sum,
        pieces,
        "lat",
        [],
        [by_lat, by_lon],
        [pltpu.VMEM((8, across), bf16), pltpu.SemaphoreType.DMA((half,))],
        out_spaces=pl.ANY,
    )
    mine = lax.all_to_all(mine, "lon", 0, 0, axis_index_groups=same_core())
    block_out, token_grad = call(
        owned_kernel,
        (struct(tokens.shape), struct(tokens.shape)),
        "owned",
        [],
        [top, left, upper_a, upper_b],
    )
    mine, block_out, token_grad = lax.optimization_barrier((mine, block_out, token_grad))
    other = swap_cores(mine)

    norm_by = 1.0 / math.sqrt(total * lat_count * lon_count)

    def unpack(*refs):
        unpack_kernel(norm_by, *refs)

    qkv_weight_grad, proj_weight_grad, table, gain, shift, qkv_bias_grad, proj_bias_grad = call(
        unpack,
        (
            struct((width, wide)),
            struct((width, width)),
            struct(table.shape),
            struct((1, width)),
            struct((1, width)),
            struct((wide,)),
            struct((1, width)),
        ),
        "unpack",
        [place],
        [mine, other],
        [pltpu.VMEM((CORES, half, 8, across), f32), pltpu.VMEM((SPREAD // LANES, HEADS * GROUP, LANES), f32)],
    )
    return (
        block_out,
        token_grad,
        gain[0],
        shift[0],
        qkv_weight_grad,
        qkv_bias_grad,
        proj_weight_grad,
        proj_bias_grad[0],
        table.transpose(0, 2, 1, 3),
    )


def solution(mesh):
    placed = (
        P(None, "lat", "lon", None),
        P(None, "lat", "lon", None),
        P(),
        P(),
        P(),
        P(),
        P(),
        P(),
        P(None, "lat", None, None),
        P(),
    )
    return jax.shard_map(
        local,
        mesh=mesh,
        in_specs=placed,
        out_specs=(
            P(None, "lat", "lon", None),
            P(None, "lat", "lon", None),
            P(),
            P(),
            P(),
            P(),
            P(),
            P(),
            P(None, "lat", None, None),
        ),
        check_vma=False,
    )
```

```python
import math

import jax
import jax.numpy as jnp
from jax import lax
from jax.experimental import pallas as pl
from jax.experimental.pallas import tpu as pltpu
from jax.sharding import PartitionSpec as P

HEADS = 6
WZ = 2
WLAT = 6
WLON = 12

HALF_LAT = WLAT // 2
HALF_LON = WLON // 2
GROUP = WZ * WLAT
COUNT = GROUP * WLON
DIFFS = 2 * WLON - 1
SIDE = WLAT * DIFFS
LANES = 128
SPREAD = 3 * LANES

mask_fill = -10000.0
epsilon = 1e-05
bias_factor = 8.0

f32 = jnp.float32
bf16 = jnp.bfloat16


def matmul(a, b, dims=((1,), (0,)), precision=None):
    return lax.dot_general(a, b, (dims, ((), ())), preferred_element_type=f32, precision=precision)


def order_of_skew(z):
    row = lax.broadcasted_iota(jnp.int32, (SIDE, 1), 0)
    lat = sum((row >= k * DIFFS).astype(jnp.int32) for k in range(1, WLAT))
    diff = row - DIFFS * lat
    target = (DIFFS - 1 - diff) * GROUP + z * WLAT + lat
    return (lax.broadcasted_iota(jnp.int32, (SIDE, SPREAD), 1) == target).astype(f32)


def to_tiles(tiles_ref, value):
    for t in range(tiles_ref.shape[0]):
        part = value[:, t * LANES : (t + 1) * LANES]
        tiles_ref[t, :, : part.shape[1]] = part


def strided_rows(tiles_ref, start, count, stride):
    tiles = [tiles_ref[t, pl.ds(start, count, stride=stride), :] for t in range(tiles_ref.shape[0])]
    return jnp.concatenate(tiles, axis=1)


def bias_kernel(
    place_ref,
    valid_ref,
    table_ref,
    *rest,
):
    params, add_ref, params_out, (sides_ref, skewed_ref) = rest[:6], rest[6], rest[7:13], rest[13:]
    for ref, to in zip(params, params_out):
        to[...] = ref[...].reshape(to.shape)
    for zn in range(WZ):
        for zm in range(WZ):
            for ln in range(WLAT):
                at = ((zn * WZ + zm) * WLAT + ln) * SIDE
                row = (zn * WLAT + ln) * HEADS
                for h in range(HEADS):
                    sides_ref[zm, row + h : row + h + 1, :] = table_ref[0, h, :, at : at + SIDE]
    skewed = 0.0
    for z in range(WZ):
        left = sides_ref[z]
        parts = []
        for _ in range(3):
            parts.append(left.astype(bf16))
            left = left - parts[-1].astype(f32)
        placed = matmul(jnp.concatenate(parts, axis=0), order_of_skew(z).astype(bf16))
        high, middle, low = [placed[k * HEADS * GROUP : (k + 1) * HEADS * GROUP] for k in range(3)]
        skewed = skewed + ((high + middle) + low)
    to_tiles(skewed_ref, skewed)
    skewed = jnp.concatenate(
        [strided_rows(skewed_ref, h, GROUP, HEADS) for h in range(HEADS)], axis=0
    )
    masked = mask_of_windows(place_ref[0], valid_ref)
    for i in range(WLON):
        shift = (GROUP * (i - WLON + 1)) % SPREAD
        rolled = skewed if shift == 0 else pltpu.roll(skewed, shift, 1)
        for h in range(HEADS):
            add_ref[h * COUNT + i * GROUP : h * COUNT + (i + 1) * GROUP, :] = (
                rolled[h * GROUP : (h + 1) * GROUP, :COUNT] + masked
            )


def mask_of_windows(band, valid_ref):
    total_rows = valid_ref.shape[0]

    def place_of(shape, axis):
        position = lax.broadcasted_iota(jnp.int32, shape, axis)
        group = position - GROUP * sum(
            (position >= GROUP * k).astype(jnp.int32) for k in range(1, shape[axis] // GROUP)
        )
        level = (group >= WLAT).astype(jnp.int32)
        row_in = group - WLAT * level
        row = band * WLAT + row_in
        region = (row >= total_rows - WLAT).astype(jnp.int32) + (
            row >= total_rows - HALF_LAT
        ).astype(jnp.int32)
        return level, row_in, region

    level_n, _, region_n = place_of((GROUP, COUNT), 0)
    level_m, row_m, region_m = place_of((GROUP, COUNT), 1)
    key_ok = jnp.zeros((GROUP, COUNT), jnp.int32)
    for r in range(WLAT):
        at = lax.rem(band * WLAT + r + HALF_LAT, total_rows)
        key_ok = jnp.where(row_m == r, valid_ref[at], key_ok)
    allowed = (level_n == level_m) & (region_n == region_m) & (key_ok == 1)
    return jnp.where(allowed, f32(0.0), f32(mask_fill))


def head_lanes(width, h):
    lane = lax.broadcasted_iota(jnp.int32, (1, width), 1)
    return (lane // 32 == h).astype(f32)


def unpacked(packed_ref, at, kind):
    low = packed_ref[(*at, kind)].astype(f32)
    high = packed_ref[(*at, 2)].astype(f32)
    return [low, high if kind == 0 else pltpu.roll(high, LANES // 2, 1)]


def gather_window(kind, first, own_ref, lat_ref, ends_refs, tiles_ref):
    levels, rows, cols, width = own_ref.shape
    inner = rows - HALF_LAT
    for z in range(levels):
        src = (z + WZ // 2) % levels
        for r in range(rows):
            if r < inner:
                line = own_ref[src, HALF_LAT + r].astype(f32)
                high = jnp.concatenate(
                    [line[:, LANES:], jnp.zeros((cols, -width % LANES), f32)], axis=1
                )
                line = [part[first:] for part in (line[:, :LANES], high)]
            else:
                line = unpacked(lat_ref, (src, r - inner), kind)
                line = [part[first - HALF_LON :] for part in line]
            if not ends_refs:
                line = [part[:WLON] for part in line]
            else:
                ends = unpacked(ends_refs[r // inner], (src, r % inner), kind)
                line = [jnp.concatenate([p, e], axis=0) for p, e in zip(line, ends)]
            for t, part in enumerate(line):
                tiles_ref[t, pl.ds(z * rows + r, WLON, stride=GROUP), :] = part
    return jnp.concatenate([tiles_ref[0], tiles_ref[1]], axis=1)[:, :width]


def pack_line(packed_ref, at, kind, low, high):
    packed_ref[(*at, kind)] = low.astype(bf16)
    half = LANES // 2
    if kind == 0:
        packed_ref[(*at, 2, slice(None), slice(0, half))] = high[:, :half].astype(bf16)
    else:
        moved = pltpu.roll(high, half, 1)
        packed_ref[(*at, 2, slice(None), slice(half, LANES))] = moved[:, half:].astype(bf16)


def scatter_window(kind, result, tiles_ref, upper_ref, bottom_ref, side_ref):
    levels, inner = upper_ref.shape[1:3]
    width = result.shape[1]
    to_tiles(tiles_ref, result)
    for z in range(levels):
        to = (z + WZ // 2) % levels
        for r in range(WLAT):
            low, high = [
                tiles_ref[t, pl.ds(z * WLAT + r, WLON, stride=GROUP), :] for t in range(2)
            ]
            if side_ref is not None:
                pack_line(side_ref, (to, r), kind, low[HALF_LON:], high[HALF_LON:])
            if r < inner:
                upper_ref[kind, to, r] = jnp.concatenate([low, high], axis=1)[:, :width]
            else:
                pack_line(bottom_ref, (to, r - inner), kind, low, high)


def packed_lines(tokens, cotangent):
    high = jnp.concatenate([tokens[..., LANES:], cotangent[..., LANES:]], axis=-1)
    return jnp.stack([tokens[..., :LANES], cotangent[..., :LANES], high], axis=2)


def cut_kernel(tokens_ref, cot_ref, near_ref, rest_ref):
    for z in range(near_ref.shape[0]):
        for r in range(near_ref.shape[1]):
            lines = [ref[z, r].astype(f32) for ref in (tokens_ref, cot_ref)]
            high = jnp.concatenate([line[:, LANES:] for line in lines], axis=1)
            for k, part in enumerate([line[:, :LANES] for line in lines] + [high]):
                near_ref[z, r, k] = part[:HALF_LON].astype(bf16)
                rest_ref[z, r, k] = part[HALF_LON:].astype(bf16)


def owned_kernel(top_ref, left_ref, upper_a_ref, upper_b_ref, out_ref, grad_ref):
    levels, rows, cols, width = out_ref.shape
    for kind, ref in enumerate((out_ref, grad_ref)):
        for z in range(levels):
            for r in range(rows):
                if r < HALF_LAT:
                    ref[z, r] = jnp.concatenate(unpacked(top_ref, (z, r), kind), axis=1)[:, :width]
                else:
                    line = unpacked(left_ref, (z, r - HALF_LAT), kind)
                    own = [u[kind, z, r - HALF_LAT] for u in (upper_a_ref, upper_b_ref)]
                    parts = [jnp.concatenate(line, axis=1)[:, :width], own[0], own[1][:HALF_LON]]
                    ref[z, r] = jnp.concatenate(parts, axis=0)


def pair_kernel(mine_ref, other_ref, sum_ref):
    sum_ref[...] = (mine_ref[...] + other_ref[...].astype(f32)).astype(bf16)


def spread(piece_ref, out_ref, sem):
    copies = [pltpu.make_async_copy(piece_ref, out_ref.at[d], sem.at[d]) for d in range(out_ref.shape[0])]
    for copy in copies:
        copy.start()
    for copy in copies:
        copy.wait()


def sum_pieces(pieces_ref):
    total = pieces_ref[0].astype(f32)
    for d in range(1, pieces_ref.shape[0]):
        total = total + pieces_ref[d].astype(f32)
    return total


def lon_kernel(pieces_ref, piece_ref, out_ref, sem):
    piece_ref[...] = sum_pieces(pieces_ref).astype(bf16)
    spread(piece_ref, out_ref, sem)


def lat_kernel(rows, pieces_ref, by_lon_ref, out_ref, piece_ref, sem):
    shape = piece_ref.shape
    row = lax.broadcasted_iota(jnp.int32, shape, 0)
    column = lax.broadcasted_iota(jnp.int32, shape, 1)
    is_table = (row >= rows) & (column < 5 * LANES)
    total = jnp.where(is_table, by_lon_ref[...].astype(f32), sum_pieces(pieces_ref))
    piece_ref[...] = total.astype(bf16)
    spread(piece_ref, out_ref, sem)


def attend(
    x_tiles, dy_tiles, own, cot, lat, ends, first, params, add_ref, d_bias_ref, prior, *grids
):
    gain_ref, shift_ref, qkv_weight_ref, qkv_bias_ref, proj_weight_ref, proj_bias_ref = params
    width = own.shape[-1]
    head_dim = width // HEADS
    scale = 1.0 / math.sqrt(head_dim)
    xf = gather_window(0, first, own, lat, ends, x_tiles)
    dyf = gather_window(1, first, cot, lat, ends, dy_tiles)
    dy = dyf.astype(bf16)
    mean_value = jnp.mean(xf, axis=-1, keepdims=True)
    centered = xf - mean_value
    inverse = lax.rsqrt(jnp.mean(centered * centered, axis=-1, keepdims=True) + epsilon)
    xhat = centered * inverse
    gain = gain_ref[...]
    normed = (xhat * gain + shift_ref[...]).astype(bf16)
    weights = [qkv_weight_ref[:, k * width : (k + 1) * width] for k in range(3)]
    q, k, v = [
        (matmul(normed, weights[i]) + qkv_bias_ref[:, i * width : (i + 1) * width]).astype(bf16)
        for i in range(3)
    ]
    proj_weight = proj_weight_ref[...]
    d_attn = matmul(dy, proj_weight, ((1,), (1,))).astype(bf16)
    per_tile = []
    for head, heads in ((0, 4), (4, 2)):
        lanes = slice(head * head_dim, (head + heads) * head_dim)
        masks = [head_lanes(heads * head_dim, h) for h in range(heads)]
        masks_b = [m.astype(bf16) for m in masks]
        qt, kt, vt, at = q[:, lanes], k[:, lanes], v[:, lanes], d_attn[:, lanes]
        q_stack = jnp.concatenate([qt * m for m in masks_b], axis=0)
        a_stack = jnp.concatenate([at * m for m in masks_b], axis=0)

        def by_head(stacked):
            total = stacked[:COUNT] * masks[0]
            for h in range(1, heads):
                total = total + stacked[h * COUNT : (h + 1) * COUNT] * masks[h]
            return total

        rows = slice(head * COUNT, (head + heads) * COUNT)
        scores = matmul(q_stack, kt, ((1,), (1,))) * scale + add_ref[rows, :]
        top = jnp.max(scores, axis=-1, keepdims=True)
        e = jnp.exp(scores - top)
        probs_f = e * (1.0 / jnp.sum(e, axis=-1, keepdims=True))
        probs = probs_f.astype(bf16)
        attn = by_head(matmul(probs, vt)).astype(bf16)
        d_probs = matmul(a_stack, vt, ((1,), (1,)))
        d_scores = probs_f * (d_probs - jnp.sum(probs_f * d_probs, axis=-1, keepdims=True))
        d_bias_ref[rows, :] = d_scores if prior is None else d_scores + prior[rows, :]
        d_scores_b = d_scores.astype(bf16)
        d_v = matmul(probs, a_stack, ((0,), (0,))).astype(bf16)
        d_q = (by_head(matmul(d_scores_b, kt)) * scale).astype(bf16)
        d_k = (matmul(d_scores_b, q_stack, ((0,), (0,))) * scale).astype(bf16)
        per_tile.append((attn, d_q, d_k, d_v))
    attn, d_q, d_k, d_v = [jnp.concatenate([t[i] for t in per_tile], axis=1) for i in range(4)]
    out = xf + matmul(attn, proj_weight) + proj_bias_ref[...]
    scatter_window(0, out, x_tiles, *grids)
    d_parts = (d_q, d_k, d_v)
    d_normed = sum(matmul(d_parts[i], weights[i], ((1,), (1,))) for i in range(3))
    d_xhat = d_normed * gain
    d_centered = inverse * (
        d_xhat
        - jnp.mean(d_xhat, axis=-1, keepdims=True)
        - xhat * jnp.mean(d_xhat * xhat, axis=-1, keepdims=True)
    )
    scatter_window(1, dyf + d_centered, dy_tiles, *grids)
    d_qkv = jnp.concatenate(d_parts, axis=1)
    qkv_weight_grad = matmul(normed, d_qkv, ((0,), (0,)))
    proj_weight_grad = matmul(attn, dy, ((0,), (0,)))
    matrix = jnp.concatenate([qkv_weight_grad, proj_weight_grad], axis=1)
    vector = jnp.concatenate(
        [
            jnp.sum(d_normed * xhat, axis=0, keepdims=True),
            jnp.sum(d_normed, axis=0, keepdims=True),
            jnp.sum(d_qkv.astype(f32), axis=0, keepdims=True),
            jnp.sum(dyf, axis=0, keepdims=True),
        ],
        axis=1,
    )
    return matrix, vector


def first_kernel(own, cot, lat, *rest):
    params, (add, upper, bottom, d_bias, matrix_ref, vector_ref, x_tiles, dy_tiles) = rest[:6], rest[6:]
    matrix_ref[...], vector_ref[...] = attend(
        x_tiles, dy_tiles, own, cot, lat, (), HALF_LON, params, add, d_bias, None, upper, bottom, None
    )


def second_kernel(place_ref, own, cot, lat, corner, lon, *rest):
    params, (add, prior, prior_matrix, prior_vector) = rest[:6], rest[6:10]
    upper, bottom, side, mine_ref, other_ref, x_tiles, dy_tiles, d_bias, parts_ref = rest[10:]
    first = own.shape[2] - HALF_LON
    matrix, vector = attend(
        x_tiles, dy_tiles, own, cot, lat, (lon, corner), first, params, add, d_bias, prior, upper, bottom, side
    )
    skewed = jnp.zeros((HEADS * GROUP, SPREAD), f32)
    for i in range(WLON):
        part = jnp.concatenate(
            [d_bias[h * COUNT + i * GROUP : h * COUNT + (i + 1) * GROUP, :] for h in range(HEADS)],
            axis=0,
        )
        part = jnp.concatenate([part, jnp.zeros((HEADS * GROUP, SPREAD - COUNT), f32)], axis=1)
        shift = GROUP * (WLON - 1 - i)
        skewed = skewed + (part if shift == 0 else pltpu.roll(part, shift, 1))
    pack(parts_ref, matrix + prior_matrix[...], vector + prior_vector[...], skewed)
    core = place_ref[1]
    mine_ref[...] = parts_ref[core]
    other_ref[...] = parts_ref[1 - core].astype(bf16)


def table_slots(pieces, pairs):
    slots = []
    for p in range(pairs):
        if p < pieces:
            slots.append((p, 0, p, 4 * LANES))
        else:
            slots.append((p - pieces, 2 * LANES, p - pieces + (pairs - pieces), 2 * LANES))
    return slots


def pack(parts_ref, matrix, vector, skewed):
    cores, half = parts_ref.shape[:2]
    pieces = cores * half
    rows = matrix.shape[0] // pieces
    for d in range(pieces):
        parts_ref[d % cores, d // cores, 0:rows, :] = matrix[d * rows : (d + 1) * rows, :]
        parts_ref[d % cores, d // cores, rows:8, :] = jnp.zeros((8 - rows, matrix.shape[1]), f32)
    for p, (d, at, d2, at2) in enumerate(table_slots(pieces, skewed.shape[0] // 2)):
        pair = slice(2 * p, 2 * p + 2)
        parts_ref[d % cores, d // cores, rows : rows + 2, at : at + 2 * LANES] = skewed[pair, : 2 * LANES]
        parts_ref[d2 % cores, d2 // cores, rows : rows + 2, at2 : at2 + LANES] = skewed[pair, 2 * LANES :]
    for d in range(vector.shape[1] // LANES):
        parts_ref[d % cores, d // cores, rows : rows + 1, 5 * LANES :] = vector[
            :, d * LANES : (d + 1) * LANES
        ]


def unpack_kernel(
    norm_by,
    place_ref,
    mine_ref,
    other_ref,
    qkv_ref,
    proj_ref,
    table_ref,
    gain_ref,
    shift_ref,
    qkv_bias_ref,
    proj_bias_ref,
    wide_ref,
    skewed_ref,
):
    core = place_ref[1]
    wide_ref[core] = mine_ref[...].astype(f32)
    wide_ref[1 - core] = other_ref[...].astype(f32)
    cores, half = wide_ref.shape[:2]
    pieces = cores * half
    width, wide = qkv_ref.shape
    rows = width // pieces
    for d in range(pieces):
        piece = wide_ref[d % cores, d // cores, 0:rows, :] * norm_by
        qkv_ref[d * rows : (d + 1) * rows, :] = piece[:, :wide]
        proj_ref[d * rows : (d + 1) * rows, :] = piece[:, wide:]
    for p, (d, at, d2, at2) in enumerate(table_slots(pieces, skewed_ref.shape[1] // 2)):
        for t in range(2):
            lanes = slice(at + t * LANES, at + (t + 1) * LANES)
            skewed_ref[t, 2 * p : 2 * p + 2, :] = wide_ref[
                d % cores, d // cores, rows : rows + 2, lanes
            ]
        skewed_ref[2, 2 * p : 2 * p + 2, :] = wide_ref[
            d2 % cores, d2 // cores, rows : rows + 2, at2 : at2 + LANES
        ]
    skewed = jnp.concatenate(
        [strided_rows(skewed_ref, a, HEADS, GROUP) for a in range(GROUP)], axis=0
    )
    skewed = (skewed * bias_factor).astype(bf16)
    sides = [matmul(skewed, order_of_skew(z).astype(bf16), ((1,), (1,))) for z in range(WZ)]
    table = jnp.concatenate(
        [
            sides[zm][(zn * WLAT + ln) * HEADS : (zn * WLAT + ln + 1) * HEADS]
            for zn in range(WZ)
            for zm in range(WZ)
            for ln in range(WLAT)
        ],
        axis=1,
    )
    for h in range(HEADS):
        table_ref[0, h] = table[h : h + 1]
    count = (3 * width + wide) // LANES
    vector = jnp.concatenate(
        [wide_ref[d % cores, d // cores, rows : rows + 1, 5 * LANES :] for d in range(count)], axis=1
    )
    vector = vector * norm_by
    gain_ref[...] = vector[:, :width]
    shift_ref[...] = vector[:, width : 2 * width]
    qkv_bias_ref[...] = vector[0, 2 * width : 2 * width + wide]
    proj_bias_ref[...] = vector[:, 2 * width + wide :]


VMEM_LIMIT = 48 * 1024 * 1024


def call(kernel, out_shape, name, scalars, arrays, scratch=(), in_space=pltpu.VMEM, out_spaces=None, cost=None):
    smem = pl.BlockSpec(memory_space=pltpu.SMEM)
    vmem = pl.BlockSpec(memory_space=in_space)
    if out_spaces is None:
        out_specs = jax.tree.map(lambda _: pl.BlockSpec(memory_space=pltpu.VMEM), out_shape)
    else:
        out_specs = jax.tree.map(lambda space: pl.BlockSpec(memory_space=space), out_spaces)
    return pl.pallas_call(
        kernel,
        out_shape=out_shape,
        in_specs=[smem] * len(scalars) + [vmem] * len(arrays),
        out_specs=out_specs,
        scratch_shapes=scratch,
        compiler_params=pltpu.CompilerParams(vmem_limit_bytes=VMEM_LIMIT),
        cost_estimate=cost,
        name=name,
    )(*scalars, *arrays)


def struct(shape, dtype=f32):
    return jax.ShapeDtypeStruct(shape, dtype)


CORES = 2


def swap_cores(value):
    count = lax.axis_size("lon")
    return lax.ppermute(value, "lon", [(i, i ^ 1) for i in range(count)])


def same_core():
    count = lax.axis_size("lon")
    return [list(range(c, count, CORES)) for c in range(CORES)]


def to_neighbour(value, axes, steps):
    counts = [lax.axis_size(a) for a in axes]
    if len(axes) == 1:
        n = counts[0]
        return lax.ppermute(value, axes[0], [(i, (i + steps[0]) % n) for i in range(n)])
    na, nb = counts
    pairs = [
        (a * nb + b, (a + steps[0]) % na * nb + (b + steps[1]) % nb)
        for a in range(na)
        for b in range(nb)
    ]
    return lax.ppermute(value, axes, pairs)


def local(
    tokens,
    cotangent,
    norm_gain_vector,
    norm_bias_vector,
    qkv_weight,
    qkv_bias,
    proj_weight,
    proj_bias,
    earth_bias,
    lat_valid,
):
    levels, rows, cols, width = tokens.shape
    wide = qkv_weight.shape[1]
    lat_count = lax.axis_size("lat")
    lon_count = lax.axis_size("lon")
    total = levels * rows * cols
    place = jnp.stack([lax.axis_index("lat"), lax.axis_index("lon") % CORES]).astype(jnp.int32)
    def packed(count, columns):
        return struct((levels, count, 3, columns, LANES), bf16)

    cuts = lax.optimization_barrier(tuple(a[:, :HALF_LAT] for a in (tokens, cotangent)))
    near, rest = call(
        cut_kernel,
        (packed(HALF_LAT, HALF_LON), packed(HALF_LAT, cols - HALF_LON)),
        "cut",
        [],
        list(cuts),
        cost=pl.CostEstimate(flops=5_000_000_000, bytes_accessed=2_000_000, transcendentals=0),
    )
    side = packed_lines(*[a[:, HALF_LAT:, :HALF_LON] for a in (tokens, cotangent)])
    lat_halo = to_neighbour(rest, ("lat",), (-1,))
    table = earth_bias.transpose(0, 2, 1, 3)
    params = [norm_gain_vector, norm_bias_vector, qkv_weight, qkv_bias, proj_weight, proj_bias]
    rows_of = [(1, p.size) if p.ndim == 1 else p.shape for p in params]
    add, *params = call(
        bias_kernel,
        (struct((HEADS * COUNT, COUNT)), *[struct(r, p.dtype) for r, p in zip(rows_of, params)]),
        "bias",
        [place, lat_valid],
        [table, *params],
        [
            pltpu.VMEM((WZ, HEADS * GROUP, SIDE), f32),
            pltpu.VMEM((SPREAD // LANES, HEADS * GROUP, LANES), f32),
        ],
    )
    near, side, add = lax.optimization_barrier((near, side, add))
    corner = to_neighbour(near, ("lat", "lon"), (-1, -1))
    lon_halo = to_neighbour(side, ("lon",), (-1,))

    half = lon_count // CORES
    across = wide + width
    upper = struct((2, levels, rows - HALF_LAT, WLON, width))
    bottom = packed(HALF_LAT, WLON)
    side = packed(rows, WLON - HALF_LON)
    tiles = pltpu.VMEM((pl.cdiv(width, LANES), COUNT, LANES), f32)
    d_bias = (HEADS * COUNT, COUNT)
    upper_a, bottom_a, *prior = call(
        first_kernel,
        (upper, bottom, struct(d_bias), struct((width, across)), struct((1, 3 * width + wide))),
        "first",
        [],
        [tokens, cotangent, lat_halo, *params, add],
        [tiles, tiles],
    )
    upper_b, bottom_b, side_b, mine, other = call(
        second_kernel,
        (upper, bottom, side, struct((half, 8, across)), struct((half, 8, across), bf16)),
        "second",
        [place],
        [tokens, cotangent, lat_halo, corner, lon_halo, *params, add, *prior],
        [tiles, tiles, pltpu.VMEM(d_bias, f32), pltpu.VMEM((CORES, half, 8, across), f32)],
    )

    pieces = struct((half, 8, across), bf16)
    piece = struct((8, across), bf16)
    pair = call(pair_kernel, pieces, "pair", [], [mine, swap_cores(other)])
    pair = lax.all_to_all(pair, "lon", 0, 0, axis_index_groups=same_core())
    left = to_neighbour(side_b, ("lon",), (1,))
    pair, left = lax.optimization_barrier((pair, left))
    by_lon, pair = call(
        lon_kernel,
        (piece, struct((lat_count, 8, across), bf16)),
        "lon",
        [],
        [pair],
        [pltpu.SemaphoreType.DMA((lat_count,))],
        out_spaces=(pltpu.VMEM, pl.ANY),
    )
    by_lat = lax.all_to_all(pair, "lat", 0, 0)
    inner = rows - HALF_LAT
    bottom = [left[:, inner:], bottom_a, bottom_b[:, :, :, :HALF_LON]]
    top = to_neighbour(jnp.concatenate(bottom, axis=3), ("lat",), (1,))
    by_lat, top = lax.optimization_barrier((by_lat, top))

    def lat_sum(*refs):
        lat_kernel(width // lon_count, *refs)

    mine = call(
        lat_sum,
        pieces,
        "lat",
        [],
        [by_lat, by_lon],
        [pltpu.VMEM((8, across), bf16), pltpu.SemaphoreType.DMA((half,))],
        out_spaces=pl.ANY,
    )
    mine = lax.all_to_all(mine, "lon", 0, 0, axis_index_groups=same_core())
    block_out, token_grad = call(
        owned_kernel,
        (struct(tokens.shape), struct(tokens.shape)),
        "owned",
        [],
        [top, left, upper_a, upper_b],
    )
    mine, block_out, token_grad = lax.optimization_barrier((mine, block_out, token_grad))
    other = swap_cores(mine)

    norm_by = 1.0 / math.sqrt(total * lat_count * lon_count)

    def unpack(*refs):
        unpack_kernel(norm_by, *refs)

    qkv_weight_grad, proj_weight_grad, table, gain, shift, qkv_bias_grad, proj_bias_grad = call(
        unpack,
        (
            struct((width, wide)),
            struct((width, width)),
            struct(table.shape),
            struct((1, width)),
            struct((1, width)),
            struct((wide,)),
            struct((1, width)),
        ),
        "unpack",
        [place],
        [mine, other],
        [pltpu.VMEM((CORES, half, 8, across), f32), pltpu.VMEM((SPREAD // LANES, HEADS * GROUP, LANES), f32)],
    )
    return (
        block_out,
        token_grad,
        gain[0],
        shift[0],
        qkv_weight_grad,
        qkv_bias_grad,
        proj_weight_grad,
        proj_bias_grad[0],
        table.transpose(0, 2, 1, 3),
    )


def solution(mesh):
    placed = (
        P(None, "lat", "lon", None),
        P(None, "lat", "lon", None),
        P(),
        P(),
        P(),
        P(),
        P(),
        P(),
        P(None, "lat", None, None),
        P(),
    )
    return jax.shard_map(
        local,
        mesh=mesh,
        in_specs=placed,
        out_specs=(
            P(None, "lat", "lon", None),
            P(None, "lat", "lon", None),
            P(),
            P(),
            P(),
            P(),
            P(),
            P(),
            P(None, "lat", None, None),
        ),
        check_vma=False,
    )
```

```python
import math

import jax
import jax.numpy as jnp
from jax import lax
from jax.experimental import pallas as pl
from jax.experimental.pallas import tpu as pltpu
from jax.sharding import PartitionSpec as P

HEADS = 6
WZ = 2
WLAT = 6
WLON = 12

HALF_LAT = WLAT // 2
HALF_LON = WLON // 2
GROUP = WZ * WLAT
COUNT = GROUP * WLON
DIFFS = 2 * WLON - 1
SIDE = WLAT * DIFFS
LANES = 128
SPREAD = 3 * LANES

mask_fill = -10000.0
epsilon = 1e-05
bias_factor = 8.0

f32 = jnp.float32
bf16 = jnp.bfloat16


def matmul(a, b, dims=((1,), (0,)), precision=None):
    return lax.dot_general(a, b, (dims, ((), ())), preferred_element_type=f32, precision=precision)


def order_of_skew(z):
    row = lax.broadcasted_iota(jnp.int32, (SIDE, 1), 0)
    lat = sum((row >= k * DIFFS).astype(jnp.int32) for k in range(1, WLAT))
    diff = row - DIFFS * lat
    target = (DIFFS - 1 - diff) * GROUP + z * WLAT + lat
    return (lax.broadcasted_iota(jnp.int32, (SIDE, SPREAD), 1) == target).astype(f32)


def to_tiles(tiles_ref, value):
    for t in range(tiles_ref.shape[0]):
        part = value[:, t * LANES : (t + 1) * LANES]
        tiles_ref[t, :, : part.shape[1]] = part


def strided_rows(tiles_ref, start, count, stride):
    tiles = [tiles_ref[t, pl.ds(start, count, stride=stride), :] for t in range(tiles_ref.shape[0])]
    return jnp.concatenate(tiles, axis=1)


def bias_kernel(
    place_ref,
    valid_ref,
    table_ref,
    *rest,
):
    params, add_ref, params_out, (sides_ref, skewed_ref) = rest[:6], rest[6], rest[7:13], rest[13:]
    for ref, to in zip(params, params_out):
        to[...] = ref[...].reshape(to.shape)
    for zn in range(WZ):
        for zm in range(WZ):
            for ln in range(WLAT):
                at = ((zn * WZ + zm) * WLAT + ln) * SIDE
                row = (zn * WLAT + ln) * HEADS
                for h in range(HEADS):
                    sides_ref[zm, row + h : row + h + 1, :] = table_ref[0, h, :, at : at + SIDE]
    skewed = 0.0
    for z in range(WZ):
        left = sides_ref[z]
        parts = []
        for _ in range(3):
            parts.append(left.astype(bf16))
            left = left - parts[-1].astype(f32)
        placed = matmul(jnp.concatenate(parts, axis=0), order_of_skew(z).astype(bf16))
        high, middle, low = [placed[k * HEADS * GROUP : (k + 1) * HEADS * GROUP] for k in range(3)]
        skewed = skewed + ((high + middle) + low)
    to_tiles(skewed_ref, skewed)
    skewed = jnp.concatenate(
        [strided_rows(skewed_ref, h, GROUP, HEADS) for h in range(HEADS)], axis=0
    )
    masked = mask_of_windows(place_ref[0], valid_ref)
    for i in range(WLON):
        shift = (GROUP * (i - WLON + 1)) % SPREAD
        rolled = skewed if shift == 0 else pltpu.roll(skewed, shift, 1)
        for h in range(HEADS):
            add_ref[h * COUNT + i * GROUP : h * COUNT + (i + 1) * GROUP, :] = (
                rolled[h * GROUP : (h + 1) * GROUP, :COUNT] + masked
            )


def mask_of_windows(band, valid_ref):
    total_rows = valid_ref.shape[0]

    def place_of(shape, axis):
        position = lax.broadcasted_iota(jnp.int32, shape, axis)
        group = position - GROUP * sum(
            (position >= GROUP * k).astype(jnp.int32) for k in range(1, shape[axis] // GROUP)
        )
        level = (group >= WLAT).astype(jnp.int32)
        row_in = group - WLAT * level
        row = band * WLAT + row_in
        region = (row >= total_rows - WLAT).astype(jnp.int32) + (
            row >= total_rows - HALF_LAT
        ).astype(jnp.int32)
        return level, row_in, region

    level_n, _, region_n = place_of((GROUP, COUNT), 0)
    level_m, row_m, region_m = place_of((GROUP, COUNT), 1)
    key_ok = jnp.zeros((GROUP, COUNT), jnp.int32)
    for r in range(WLAT):
        at = lax.rem(band * WLAT + r + HALF_LAT, total_rows)
        key_ok = jnp.where(row_m == r, valid_ref[at], key_ok)
    allowed = (level_n == level_m) & (region_n == region_m) & (key_ok == 1)
    return jnp.where(allowed, f32(0.0), f32(mask_fill))


def head_lanes(width, h):
    lane = lax.broadcasted_iota(jnp.int32, (1, width), 1)
    return (lane // 32 == h).astype(f32)


def unpacked(packed_ref, at, kind):
    low = packed_ref[(*at, kind)].astype(f32)
    high = packed_ref[(*at, 2)].astype(f32)
    return [low, high if kind == 0 else pltpu.roll(high, LANES // 2, 1)]


def gather_window(kind, first, own_ref, lat_ref, ends_refs, tiles_ref):
    levels, rows, cols, width = own_ref.shape
    inner = rows - HALF_LAT
    for z in range(levels):
        src = (z + WZ // 2) % levels
        for r in range(rows):
            if r < inner:
                line = own_ref[src, HALF_LAT + r].astype(f32)
                high = jnp.concatenate(
                    [line[:, LANES:], jnp.zeros((cols, -width % LANES), f32)], axis=1
                )
                line = [part[first:] for part in (line[:, :LANES], high)]
            else:
                line = unpacked(lat_ref, (src, r - inner), kind)
                line = [part[first - HALF_LON :] for part in line]
            if not ends_refs:
                line = [part[:WLON] for part in line]
            else:
                ends = unpacked(ends_refs[r // inner], (src, r % inner), kind)
                line = [jnp.concatenate([p, e], axis=0) for p, e in zip(line, ends)]
            for t, part in enumerate(line):
                tiles_ref[t, pl.ds(z * rows + r, WLON, stride=GROUP), :] = part
    return jnp.concatenate([tiles_ref[0], tiles_ref[1]], axis=1)[:, :width]


def pack_line(packed_ref, at, kind, low, high):
    packed_ref[(*at, kind)] = low.astype(bf16)
    half = LANES // 2
    if kind == 0:
        packed_ref[(*at, 2, slice(None), slice(0, half))] = high[:, :half].astype(bf16)
    else:
        moved = pltpu.roll(high, half, 1)
        packed_ref[(*at, 2, slice(None), slice(half, LANES))] = moved[:, half:].astype(bf16)


def scatter_window(kind, result, tiles_ref, upper_ref, bottom_ref, side_ref):
    levels, inner = upper_ref.shape[1:3]
    width = result.shape[1]
    to_tiles(tiles_ref, result)
    for z in range(levels):
        to = (z + WZ // 2) % levels
        for r in range(WLAT):
            low, high = [
                tiles_ref[t, pl.ds(z * WLAT + r, WLON, stride=GROUP), :] for t in range(2)
            ]
            if side_ref is not None:
                pack_line(side_ref, (to, r), kind, low[HALF_LON:], high[HALF_LON:])
            if r < inner:
                upper_ref[kind, to, r] = jnp.concatenate([low, high], axis=1)[:, :width]
            else:
                pack_line(bottom_ref, (to, r - inner), kind, low, high)


def packed_lines(tokens, cotangent):
    high = jnp.concatenate([tokens[..., LANES:], cotangent[..., LANES:]], axis=-1)
    return jnp.stack([tokens[..., :LANES], cotangent[..., :LANES], high], axis=2)


def cut_kernel(tokens_ref, cot_ref, near_ref, rest_ref):
    for z in range(near_ref.shape[0]):
        for r in range(near_ref.shape[1]):
            lines = [ref[z, r].astype(f32) for ref in (tokens_ref, cot_ref)]
            high = jnp.concatenate([line[:, LANES:] for line in lines], axis=1)
            for k, part in enumerate([line[:, :LANES] for line in lines] + [high]):
                near_ref[z, r, k] = part[:HALF_LON].astype(bf16)
                rest_ref[z, r, k] = part[HALF_LON:].astype(bf16)


def owned_kernel(top_ref, left_ref, upper_a_ref, upper_b_ref, out_ref, grad_ref):
    levels, rows, cols, width = out_ref.shape
    for kind, ref in enumerate((out_ref, grad_ref)):
        for z in range(levels):
            for r in range(rows):
                if r < HALF_LAT:
                    ref[z, r] = jnp.concatenate(unpacked(top_ref, (z, r), kind), axis=1)[:, :width]
                else:
                    line = unpacked(left_ref, (z, r - HALF_LAT), kind)
                    own = [u[kind, z, r - HALF_LAT] for u in (upper_a_ref, upper_b_ref)]
                    parts = [jnp.concatenate(line, axis=1)[:, :width], own[0], own[1][:HALF_LON]]
                    ref[z, r] = jnp.concatenate(parts, axis=0)


def pair_kernel(mine_ref, other_ref, sum_ref):
    sum_ref[...] = (mine_ref[...] + other_ref[...].astype(f32)).astype(bf16)


def spread(piece, out_ref):
    for d in range(out_ref.shape[0]):
        out_ref[d] = piece


def sum_pieces(pieces_ref):
    total = pieces_ref[0].astype(f32)
    for d in range(1, pieces_ref.shape[0]):
        total = total + pieces_ref[d].astype(f32)
    return total


def lon_kernel(pieces_ref, piece_ref, out_ref):
    piece = sum_pieces(pieces_ref).astype(bf16)
    piece_ref[...] = piece
    spread(piece, out_ref)


def lat_kernel(rows, pieces_ref, by_lon_ref, out_ref):
    shape = by_lon_ref.shape
    row = lax.broadcasted_iota(jnp.int32, shape, 0)
    column = lax.broadcasted_iota(jnp.int32, shape, 1)
    is_table = (row >= rows) & (column < 5 * LANES)
    total = jnp.where(is_table, by_lon_ref[...].astype(f32), sum_pieces(pieces_ref))
    spread(total.astype(bf16), out_ref)


def attend(
    x_tiles, dy_tiles, own, cot, lat, ends, first, params, add_ref, d_bias_ref, prior, *grids
):
    gain_ref, shift_ref, qkv_weight_ref, qkv_bias_ref, proj_weight_ref, proj_bias_ref = params
    width = own.shape[-1]
    head_dim = width // HEADS
    scale = 1.0 / math.sqrt(head_dim)
    xf = gather_window(0, first, own, lat, ends, x_tiles)
    dyf = gather_window(1, first, cot, lat, ends, dy_tiles)
    dy = dyf.astype(bf16)
    mean_value = jnp.mean(xf, axis=-1, keepdims=True)
    centered = xf - mean_value
    inverse = lax.rsqrt(jnp.mean(centered * centered, axis=-1, keepdims=True) + epsilon)
    xhat = centered * inverse
    gain = gain_ref[...]
    normed = (xhat * gain + shift_ref[...]).astype(bf16)
    weights = [qkv_weight_ref[:, k * width : (k + 1) * width] for k in range(3)]
    q, k, v = [
        (matmul(normed, weights[i]) + qkv_bias_ref[:, i * width : (i + 1) * width]).astype(bf16)
        for i in range(3)
    ]
    proj_weight = proj_weight_ref[...]
    d_attn = matmul(dy, proj_weight, ((1,), (1,))).astype(bf16)
    per_tile = []
    for head, heads in ((0, 4), (4, 2)):
        lanes = slice(head * head_dim, (head + heads) * head_dim)
        masks = [head_lanes(heads * head_dim, h) for h in range(heads)]
        masks_b = [m.astype(bf16) for m in masks]
        qt, kt, vt, at = q[:, lanes], k[:, lanes], v[:, lanes], d_attn[:, lanes]
        q_stack = jnp.concatenate([qt * m for m in masks_b], axis=0)
        a_stack = jnp.concatenate([at * m for m in masks_b], axis=0)

        def by_head(stacked):
            total = stacked[:COUNT] * masks[0]
            for h in range(1, heads):
                total = total + stacked[h * COUNT : (h + 1) * COUNT] * masks[h]
            return total

        rows = slice(head * COUNT, (head + heads) * COUNT)
        scores = matmul(q_stack, kt, ((1,), (1,))) * scale + add_ref[rows, :]
        top = jnp.max(scores, axis=-1, keepdims=True)
        e = jnp.exp(scores - top)
        probs_f = e * (1.0 / jnp.sum(e, axis=-1, keepdims=True))
        probs = probs_f.astype(bf16)
        attn = by_head(matmul(probs, vt)).astype(bf16)
        d_probs = matmul(a_stack, vt, ((1,), (1,)))
        d_scores = probs_f * (d_probs - jnp.sum(probs_f * d_probs, axis=-1, keepdims=True))
        d_bias_ref[rows, :] = d_scores if prior is None else d_scores + prior[rows, :]
        d_scores_b = d_scores.astype(bf16)
        d_v = matmul(probs, a_stack, ((0,), (0,))).astype(bf16)
        d_q = (by_head(matmul(d_scores_b, kt)) * scale).astype(bf16)
        d_k = (matmul(d_scores_b, q_stack, ((0,), (0,))) * scale).astype(bf16)
        per_tile.append((attn, d_q, d_k, d_v))
    attn, d_q, d_k, d_v = [jnp.concatenate([t[i] for t in per_tile], axis=1) for i in range(4)]
    out = xf + matmul(attn, proj_weight) + proj_bias_ref[...]
    scatter_window(0, out, x_tiles, *grids)
    d_parts = (d_q, d_k, d_v)
    d_normed = sum(matmul(d_parts[i], weights[i], ((1,), (1,))) for i in range(3))
    d_xhat = d_normed * gain
    d_centered = inverse * (
        d_xhat
        - jnp.mean(d_xhat, axis=-1, keepdims=True)
        - xhat * jnp.mean(d_xhat * xhat, axis=-1, keepdims=True)
    )
    scatter_window(1, dyf + d_centered, dy_tiles, *grids)
    d_qkv = jnp.concatenate(d_parts, axis=1)
    qkv_weight_grad = matmul(normed, d_qkv, ((0,), (0,)))
    proj_weight_grad = matmul(attn, dy, ((0,), (0,)))
    matrix = jnp.concatenate([qkv_weight_grad, proj_weight_grad], axis=1)
    vector = jnp.concatenate(
        [
            jnp.sum(d_normed * xhat, axis=0, keepdims=True),
            jnp.sum(d_normed, axis=0, keepdims=True),
            jnp.sum(d_qkv.astype(f32), axis=0, keepdims=True),
            jnp.sum(dyf, axis=0, keepdims=True),
        ],
        axis=1,
    )
    return matrix, vector


def first_kernel(own, cot, lat, *rest):
    params, (add, upper, bottom, d_bias, matrix_ref, vector_ref, x_tiles, dy_tiles) = rest[:6], rest[6:]
    matrix_ref[...], vector_ref[...] = attend(
        x_tiles, dy_tiles, own, cot, lat, (), HALF_LON, params, add, d_bias, None, upper, bottom, None
    )


def second_kernel(place_ref, own, cot, lat, corner, lon, *rest):
    params, (add, prior, prior_matrix, prior_vector) = rest[:6], rest[6:10]
    upper, bottom, side, mine_ref, other_ref, x_tiles, dy_tiles, d_bias, parts_ref = rest[10:]
    first = own.shape[2] - HALF_LON
    matrix, vector = attend(
        x_tiles, dy_tiles, own, cot, lat, (lon, corner), first, params, add, d_bias, prior, upper, bottom, side
    )
    skewed = jnp.zeros((HEADS * GROUP, SPREAD), f32)
    for i in range(WLON):
        part = jnp.concatenate(
            [d_bias[h * COUNT + i * GROUP : h * COUNT + (i + 1) * GROUP, :] for h in range(HEADS)],
            axis=0,
        )
        part = jnp.concatenate([part, jnp.zeros((HEADS * GROUP, SPREAD - COUNT), f32)], axis=1)
        shift = GROUP * (WLON - 1 - i)
        skewed = skewed + (part if shift == 0 else pltpu.roll(part, shift, 1))
    pack(parts_ref, matrix + prior_matrix[...], vector + prior_vector[...], skewed)
    core = place_ref[1]
    mine_ref[...] = parts_ref[core]
    other_ref[...] = parts_ref[1 - core].astype(bf16)


def table_slots(pieces, pairs):
    slots = []
    for p in range(pairs):
        if p < pieces:
            slots.append((p, 0, p, 4 * LANES))
        else:
            slots.append((p - pieces, 2 * LANES, p - pieces + (pairs - pieces), 2 * LANES))
    return slots


def pack(parts_ref, matrix, vector, skewed):
    cores, half = parts_ref.shape[:2]
    pieces = cores * half
    rows = matrix.shape[0] // pieces
    for d in range(pieces):
        parts_ref[d % cores, d // cores, 0:rows, :] = matrix[d * rows : (d + 1) * rows, :]
        parts_ref[d % cores, d // cores, rows:8, :] = jnp.zeros((8 - rows, matrix.shape[1]), f32)
    for p, (d, at, d2, at2) in enumerate(table_slots(pieces, skewed.shape[0] // 2)):
        pair = slice(2 * p, 2 * p + 2)
        parts_ref[d % cores, d // cores, rows : rows + 2, at : at + 2 * LANES] = skewed[pair, : 2 * LANES]
        parts_ref[d2 % cores, d2 // cores, rows : rows + 2, at2 : at2 + LANES] = skewed[pair, 2 * LANES :]
    for d in range(vector.shape[1] // LANES):
        parts_ref[d % cores, d // cores, rows : rows + 1, 5 * LANES :] = vector[
            :, d * LANES : (d + 1) * LANES
        ]


def unpack_kernel(
    norm_by,
    place_ref,
    mine_ref,
    other_ref,
    qkv_ref,
    proj_ref,
    table_ref,
    gain_ref,
    shift_ref,
    qkv_bias_ref,
    proj_bias_ref,
    wide_ref,
    skewed_ref,
):
    core = place_ref[1]
    wide_ref[core] = mine_ref[...].astype(f32)
    wide_ref[1 - core] = other_ref[...].astype(f32)
    cores, half = wide_ref.shape[:2]
    pieces = cores * half
    width, wide = qkv_ref.shape
    rows = width // pieces
    for d in range(pieces):
        piece = wide_ref[d % cores, d // cores, 0:rows, :] * norm_by
        qkv_ref[d * rows : (d + 1) * rows, :] = piece[:, :wide]
        proj_ref[d * rows : (d + 1) * rows, :] = piece[:, wide:]
    for p, (d, at, d2, at2) in enumerate(table_slots(pieces, skewed_ref.shape[1] // 2)):
        for t in range(2):
            lanes = slice(at + t * LANES, at + (t + 1) * LANES)
            skewed_ref[t, 2 * p : 2 * p + 2, :] = wide_ref[
                d % cores, d // cores, rows : rows + 2, lanes
            ]
        skewed_ref[2, 2 * p : 2 * p + 2, :] = wide_ref[
            d2 % cores, d2 // cores, rows : rows + 2, at2 : at2 + LANES
        ]
    skewed = jnp.concatenate(
        [strided_rows(skewed_ref, a, HEADS, GROUP) for a in range(GROUP)], axis=0
    )
    skewed = (skewed * bias_factor).astype(bf16)
    sides = [matmul(skewed, order_of_skew(z).astype(bf16), ((1,), (1,))) for z in range(WZ)]
    table = jnp.concatenate(
        [
            sides[zm][(zn * WLAT + ln) * HEADS : (zn * WLAT + ln + 1) * HEADS]
            for zn in range(WZ)
            for zm in range(WZ)
            for ln in range(WLAT)
        ],
        axis=1,
    )
    for h in range(HEADS):
        table_ref[0, h] = table[h : h + 1]
    count = (3 * width + wide) // LANES
    vector = jnp.concatenate(
        [wide_ref[d % cores, d // cores, rows : rows + 1, 5 * LANES :] for d in range(count)], axis=1
    )
    vector = vector * norm_by
    gain_ref[...] = vector[:, :width]
    shift_ref[...] = vector[:, width : 2 * width]
    qkv_bias_ref[...] = vector[0, 2 * width : 2 * width + wide]
    proj_bias_ref[...] = vector[:, 2 * width + wide :]


VMEM_LIMIT = 48 * 1024 * 1024


def call(kernel, out_shape, name, scalars, arrays, scratch=(), in_space=pltpu.VMEM, out_spaces=None, cost=None):
    smem = pl.BlockSpec(memory_space=pltpu.SMEM)
    vmem = pl.BlockSpec(memory_space=in_space)
    if out_spaces is None:
        out_specs = jax.tree.map(lambda _: pl.BlockSpec(memory_space=pltpu.VMEM), out_shape)
    else:
        out_specs = jax.tree.map(lambda space: pl.BlockSpec(memory_space=space), out_spaces)
    return pl.pallas_call(
        kernel,
        out_shape=out_shape,
        in_specs=[smem] * len(scalars) + [vmem] * len(arrays),
        out_specs=out_specs,
        scratch_shapes=scratch,
        compiler_params=pltpu.CompilerParams(vmem_limit_bytes=VMEM_LIMIT),
        cost_estimate=cost,
        name=name,
    )(*scalars, *arrays)


def struct(shape, dtype=f32):
    return jax.ShapeDtypeStruct(shape, dtype)


CORES = 2


def swap_cores(value):
    count = lax.axis_size("lon")
    return lax.ppermute(value, "lon", [(i, i ^ 1) for i in range(count)])


def same_core():
    count = lax.axis_size("lon")
    return [list(range(c, count, CORES)) for c in range(CORES)]


def to_neighbour(value, axes, steps):
    counts = [lax.axis_size(a) for a in axes]
    if len(axes) == 1:
        n = counts[0]
        return lax.ppermute(value, axes[0], [(i, (i + steps[0]) % n) for i in range(n)])
    na, nb = counts
    pairs = [
        (a * nb + b, (a + steps[0]) % na * nb + (b + steps[1]) % nb)
        for a in range(na)
        for b in range(nb)
    ]
    return lax.ppermute(value, axes, pairs)


def local(
    tokens,
    cotangent,
    norm_gain_vector,
    norm_bias_vector,
    qkv_weight,
    qkv_bias,
    proj_weight,
    proj_bias,
    earth_bias,
    lat_valid,
):
    levels, rows, cols, width = tokens.shape
    wide = qkv_weight.shape[1]
    lat_count = lax.axis_size("lat")
    lon_count = lax.axis_size("lon")
    total = levels * rows * cols
    place = jnp.stack([lax.axis_index("lat"), lax.axis_index("lon") % CORES]).astype(jnp.int32)
    def packed(count, columns):
        return struct((levels, count, 3, columns, LANES), bf16)

    cuts = lax.optimization_barrier(tuple(a[:, :HALF_LAT] for a in (tokens, cotangent)))
    near, rest = call(
        cut_kernel,
        (packed(HALF_LAT, HALF_LON), packed(HALF_LAT, cols - HALF_LON)),
        "cut",
        [],
        list(cuts),
        cost=pl.CostEstimate(flops=5_000_000_000, bytes_accessed=2_000_000, transcendentals=0),
    )
    side = packed_lines(*[a[:, HALF_LAT:, :HALF_LON] for a in (tokens, cotangent)])
    lat_halo = to_neighbour(rest, ("lat",), (-1,))
    table = earth_bias.transpose(0, 2, 1, 3)
    params = [norm_gain_vector, norm_bias_vector, qkv_weight, qkv_bias, proj_weight, proj_bias]
    rows_of = [(1, p.size) if p.ndim == 1 else p.shape for p in params]
    add, *params = call(
        bias_kernel,
        (struct((HEADS * COUNT, COUNT)), *[struct(r, p.dtype) for r, p in zip(rows_of, params)]),
        "bias",
        [place, lat_valid],
        [table, *params],
        [
            pltpu.VMEM((WZ, HEADS * GROUP, SIDE), f32),
            pltpu.VMEM((SPREAD // LANES, HEADS * GROUP, LANES), f32),
        ],
    )
    near, side, add = lax.optimization_barrier((near, side, add))
    corner = to_neighbour(near, ("lat", "lon"), (-1, -1))
    lon_halo = to_neighbour(side, ("lon",), (-1,))

    half = lon_count // CORES
    across = wide + width
    upper = struct((2, levels, rows - HALF_LAT, WLON, width))
    bottom = packed(HALF_LAT, WLON)
    side = packed(rows, WLON - HALF_LON)
    tiles = pltpu.VMEM((pl.cdiv(width, LANES), COUNT, LANES), f32)
    d_bias = (HEADS * COUNT, COUNT)
    upper_a, bottom_a, *prior = call(
        first_kernel,
        (upper, bottom, struct(d_bias), struct((width, across)), struct((1, 3 * width + wide))),
        "first",
        [],
        [tokens, cotangent, lat_halo, *params, add],
        [tiles, tiles],
    )
    upper_b, bottom_b, side_b, mine, other = call(
        second_kernel,
        (upper, bottom, side, struct((half, 8, across)), struct((half, 8, across), bf16)),
        "second",
        [place],
        [tokens, cotangent, lat_halo, corner, lon_halo, *params, add, *prior],
        [tiles, tiles, pltpu.VMEM(d_bias, f32), pltpu.VMEM((CORES, half, 8, across), f32)],
    )

    pieces = struct((half, 8, across), bf16)
    piece = struct((8, across), bf16)
    pair = call(pair_kernel, pieces, "pair", [], [mine, swap_cores(other)])
    pair = lax.all_to_all(pair, "lon", 0, 0, axis_index_groups=same_core())
    left = to_neighbour(side_b, ("lon",), (1,))
    pair, left = lax.optimization_barrier((pair, left))
    by_lon, pair = call(
        lon_kernel,
        (piece, struct((lat_count, 8, across), bf16)),
        "lon",
        [],
        [pair],
    )
    by_lat = lax.all_to_all(pair, "lat", 0, 0)
    inner = rows - HALF_LAT
    bottom = [left[:, inner:], bottom_a, bottom_b[:, :, :, :HALF_LON]]
    top = to_neighbour(jnp.concatenate(bottom, axis=3), ("lat",), (1,))

    def lat_sum(*refs):
        lat_kernel(width // lon_count, *refs)

    mine = call(
        lat_sum,
        pieces,
        "lat",
        [],
        [by_lat, by_lon],
    )
    mine = lax.all_to_all(mine, "lon", 0, 0, axis_index_groups=same_core())
    block_out, token_grad = call(
        owned_kernel,
        (struct(tokens.shape), struct(tokens.shape)),
        "owned",
        [],
        [top, left, upper_a, upper_b],
        cost=pl.CostEstimate(flops=5000000000, bytes_accessed=2_000_000, transcendentals=0),
    )
    mine, block_out, token_grad = lax.optimization_barrier((mine, block_out, token_grad))
    other = swap_cores(mine)

    norm_by = 1.0 / math.sqrt(total * lat_count * lon_count)

    def unpack(*refs):
        unpack_kernel(norm_by, *refs)

    qkv_weight_grad, proj_weight_grad, table, gain, shift, qkv_bias_grad, proj_bias_grad = call(
        unpack,
        (
            struct((width, wide)),
            struct((width, width)),
            struct(table.shape),
            struct((1, width)),
            struct((1, width)),
            struct((wide,)),
            struct((1, width)),
        ),
        "unpack",
        [place],
        [mine, other],
        [pltpu.VMEM((CORES, half, 8, across), f32), pltpu.VMEM((SPREAD // LANES, HEADS * GROUP, LANES), f32)],
    )
    return (
        block_out,
        token_grad,
        gain[0],
        shift[0],
        qkv_weight_grad,
        qkv_bias_grad,
        proj_weight_grad,
        proj_bias_grad[0],
        table.transpose(0, 2, 1, 3),
    )


def solution(mesh):
    placed = (
        P(None, "lat", "lon", None),
        P(None, "lat", "lon", None),
        P(),
        P(),
        P(),
        P(),
        P(),
        P(),
        P(None, "lat", None, None),
        P(),
    )
    return jax.shard_map(
        local,
        mesh=mesh,
        in_specs=placed,
        out_specs=(
            P(None, "lat", "lon", None),
            P(None, "lat", "lon", None),
            P(),
            P(),
            P(),
            P(),
            P(),
            P(),
            P(None, "lat", None, None),
        ),
        check_vma=False,
    )
```

```python
import math

import jax
import jax.numpy as jnp
from jax import lax
from jax.experimental import pallas as pl
from jax.experimental.pallas import tpu as pltpu
from jax.sharding import PartitionSpec as P

HEADS = 6
WZ = 2
WLAT = 6
WLON = 12

HALF_LAT = WLAT // 2
HALF_LON = WLON // 2
GROUP = WZ * WLAT
COUNT = GROUP * WLON
DIFFS = 2 * WLON - 1
SIDE = WLAT * DIFFS
LANES = 128
SPREAD = 3 * LANES

mask_fill = -10000.0
epsilon = 1e-05
bias_factor = 8.0

f32 = jnp.float32
bf16 = jnp.bfloat16


def matmul(a, b, dims=((1,), (0,)), precision=None):
    return lax.dot_general(a, b, (dims, ((), ())), preferred_element_type=f32, precision=precision)


def order_of_skew(z):
    row = lax.broadcasted_iota(jnp.int32, (SIDE, 1), 0)
    lat = sum((row >= k * DIFFS).astype(jnp.int32) for k in range(1, WLAT))
    diff = row - DIFFS * lat
    target = (DIFFS - 1 - diff) * GROUP + z * WLAT + lat
    return (lax.broadcasted_iota(jnp.int32, (SIDE, SPREAD), 1) == target).astype(f32)


def to_tiles(tiles_ref, value):
    for t in range(tiles_ref.shape[0]):
        part = value[:, t * LANES : (t + 1) * LANES]
        tiles_ref[t, : part.shape[0], : part.shape[1]] = part


def strided_rows(tiles_ref, start, count, stride):
    tiles = [tiles_ref[t, pl.ds(start, count, stride=stride), :] for t in range(tiles_ref.shape[0])]
    return jnp.concatenate(tiles, axis=1)


def bias_kernel(
    place_ref,
    valid_ref,
    table_ref,
    *rest,
):
    params, add_ref, params_out, (sides_ref, skewed_ref) = rest[:6], rest[6], rest[7:13], rest[13:]
    for ref, to in zip(params, params_out):
        to[...] = ref[...].reshape(to.shape)
    for zn in range(WZ):
        for zm in range(WZ):
            for ln in range(WLAT):
                at = ((zn * WZ + zm) * WLAT + ln) * SIDE
                row = (zn * WLAT + ln) * HEADS
                for h in range(HEADS):
                    sides_ref[zm, row + h : row + h + 1, :] = table_ref[0, h, :, at : at + SIDE]
    skewed = 0.0
    for z in range(WZ):
        left = sides_ref[z]
        parts = []
        for _ in range(3):
            parts.append(left.astype(bf16))
            left = left - parts[-1].astype(f32)
        placed = matmul(jnp.concatenate(parts, axis=0), order_of_skew(z).astype(bf16))
        high, middle, low = [placed[k * HEADS * GROUP : (k + 1) * HEADS * GROUP] for k in range(3)]
        skewed = skewed + ((high + middle) + low)
    to_tiles(skewed_ref, skewed)
    skewed = jnp.concatenate(
        [strided_rows(skewed_ref, h, GROUP, HEADS) for h in range(HEADS)], axis=0
    )
    masked = mask_of_windows(place_ref[0], valid_ref)
    for i in range(WLON):
        shift = (GROUP * (i - WLON + 1)) % SPREAD
        rolled = skewed if shift == 0 else pltpu.roll(skewed, shift, 1)
        for h in range(HEADS):
            add_ref[h * COUNT + i * GROUP : h * COUNT + (i + 1) * GROUP, :] = (
                rolled[h * GROUP : (h + 1) * GROUP, :COUNT] + masked
            )


def mask_of_windows(band, valid_ref):
    total_rows = valid_ref.shape[0]

    def place_of(shape, axis):
        position = lax.broadcasted_iota(jnp.int32, shape, axis)
        group = position - GROUP * sum(
            (position >= GROUP * k).astype(jnp.int32) for k in range(1, shape[axis] // GROUP)
        )
        level = (group >= WLAT).astype(jnp.int32)
        row_in = group - WLAT * level
        row = band * WLAT + row_in
        region = (row >= total_rows - WLAT).astype(jnp.int32) + (
            row >= total_rows - HALF_LAT
        ).astype(jnp.int32)
        return level, row_in, region

    level_n, _, region_n = place_of((GROUP, COUNT), 0)
    level_m, row_m, region_m = place_of((GROUP, COUNT), 1)
    key_ok = jnp.zeros((GROUP, COUNT), jnp.int32)
    for r in range(WLAT):
        at = lax.rem(band * WLAT + r + HALF_LAT, total_rows)
        key_ok = jnp.where(row_m == r, valid_ref[at], key_ok)
    allowed = (level_n == level_m) & (region_n == region_m) & (key_ok == 1)
    return jnp.where(allowed, f32(0.0), f32(mask_fill))


def head_lanes(width, h):
    lane = lax.broadcasted_iota(jnp.int32, (1, width), 1)
    return (lane // 32 == h).astype(f32)


def unpacked(packed_ref, at, kind):
    low = packed_ref[(*at, kind)].astype(f32)
    high = packed_ref[(*at, 2)].astype(f32)
    return [low, high if kind == 0 else pltpu.roll(high, LANES // 2, 1)]


def gather_window(kind, first, own_ref, lat_ref, ends_refs, tiles_ref):
    levels, rows, cols, width = own_ref.shape
    inner = rows - HALF_LAT
    for z in range(levels):
        src = (z + WZ // 2) % levels
        for r in range(rows):
            if r < inner:
                line = own_ref[src, HALF_LAT + r].astype(f32)
                high = jnp.concatenate(
                    [line[:, LANES:], jnp.zeros((cols, -width % LANES), f32)], axis=1
                )
                line = [part[first:] for part in (line[:, :LANES], high)]
            else:
                line = unpacked(lat_ref, (src, r - inner), kind)
                line = [part[first - HALF_LON :] for part in line]
            if not ends_refs:
                line = [part[:WLON] for part in line]
            else:
                ends = unpacked(ends_refs[r // inner], (src, r % inner), kind)
                line = [jnp.concatenate([p, e], axis=0) for p, e in zip(line, ends)]
            for t, part in enumerate(line):
                tiles_ref[t, pl.ds(z * rows + r, WLON, stride=GROUP), :] = part
    return jnp.concatenate([tiles_ref[t, :COUNT, :] for t in range(2)], axis=1)[:, :width]


def pack_line(packed_ref, at, kind, low, high):
    packed_ref[(*at, kind)] = low.astype(bf16)
    half = LANES // 2
    if kind == 0:
        packed_ref[(*at, 2, slice(None), slice(0, half))] = high[:, :half].astype(bf16)
    else:
        moved = pltpu.roll(high, half, 1)
        packed_ref[(*at, 2, slice(None), slice(half, LANES))] = moved[:, half:].astype(bf16)


def scatter_window(kind, result, tiles_ref, upper_ref, bottom_ref, side_ref):
    levels, inner = upper_ref.shape[1:3]
    width = result.shape[1]
    to_tiles(tiles_ref, result)
    for z in range(levels):
        to = (z + WZ // 2) % levels
        for r in range(WLAT):
            low, high = [
                tiles_ref[t, pl.ds(z * WLAT + r, WLON, stride=GROUP), :] for t in range(2)
            ]
            if side_ref is not None:
                pack_line(side_ref, (to, r), kind, low[HALF_LON:], high[HALF_LON:])
            if r < inner:
                upper_ref[kind, to, r] = jnp.concatenate([low, high], axis=1)[:, :width]
            else:
                pack_line(bottom_ref, (to, r - inner), kind, low, high)


def packed_lines(tokens, cotangent):
    high = jnp.concatenate([tokens[..., LANES:], cotangent[..., LANES:]], axis=-1)
    return jnp.stack([tokens[..., :LANES], cotangent[..., :LANES], high], axis=2)


def cut_kernel(tokens_ref, cot_ref, near_ref, rest_ref):
    for z in range(near_ref.shape[0]):
        for r in range(near_ref.shape[1]):
            lines = [ref[z, r].astype(f32) for ref in (tokens_ref, cot_ref)]
            high = jnp.concatenate([line[:, LANES:] for line in lines], axis=1)
            for k, part in enumerate([line[:, :LANES] for line in lines] + [high]):
                near_ref[z, r, k] = part[:HALF_LON].astype(bf16)
                rest_ref[z, r, k] = part[HALF_LON:].astype(bf16)


def owned_kernel(top_ref, left_ref, upper_a_ref, upper_b_ref, out_ref, grad_ref):
    levels, rows, cols, width = out_ref.shape
    for kind, ref in enumerate((out_ref, grad_ref)):
        for z in range(levels):
            for r in range(rows):
                if r < HALF_LAT:
                    ref[z, r] = jnp.concatenate(unpacked(top_ref, (z, r), kind), axis=1)[:, :width]
                else:
                    line = unpacked(left_ref, (z, r - HALF_LAT), kind)
                    own = [u[kind, z, r - HALF_LAT] for u in (upper_a_ref, upper_b_ref)]
                    parts = [jnp.concatenate(line, axis=1)[:, :width], own[0], own[1][:HALF_LON]]
                    ref[z, r] = jnp.concatenate(parts, axis=0)


def pair_kernel(mine_ref, other_ref, sum_ref):
    sum_ref[...] = (mine_ref[...] + other_ref[...].astype(f32)).astype(bf16)


def spread(piece, out_ref):
    for d in range(out_ref.shape[0]):
        out_ref[d] = piece


def sum_pieces(pieces_ref):
    total = pieces_ref[0].astype(f32)
    for d in range(1, pieces_ref.shape[0]):
        total = total + pieces_ref[d].astype(f32)
    return total


def lon_kernel(pieces_ref, piece_ref, out_ref):
    piece = sum_pieces(pieces_ref).astype(bf16)
    piece_ref[...] = piece
    spread(piece, out_ref)


def lat_kernel(rows, pieces_ref, by_lon_ref, out_ref):
    shape = by_lon_ref.shape
    row = lax.broadcasted_iota(jnp.int32, shape, 0)
    column = lax.broadcasted_iota(jnp.int32, shape, 1)
    is_table = (row >= rows) & (column < 5 * LANES)
    total = jnp.where(is_table, by_lon_ref[...].astype(f32), sum_pieces(pieces_ref))
    spread(total.astype(bf16), out_ref)


def attend(
    x_tiles, dy_tiles, own, cot, lat, ends, first, params, add_ref, d_bias_ref, prior, *grids
):
    gain_ref, shift_ref, qkv_weight_ref, qkv_bias_ref, proj_weight_ref, proj_bias_ref = params
    width = own.shape[-1]
    head_dim = width // HEADS
    scale = 1.0 / math.sqrt(head_dim)
    xf = gather_window(0, first, own, lat, ends, x_tiles)
    dyf = gather_window(1, first, cot, lat, ends, dy_tiles)
    dy = dyf.astype(bf16)
    mean_value = jnp.mean(xf, axis=-1, keepdims=True)
    centered = xf - mean_value
    inverse = lax.rsqrt(jnp.mean(centered * centered, axis=-1, keepdims=True) + epsilon)
    xhat = centered * inverse
    gain = gain_ref[...]
    normed = (xhat * gain + shift_ref[...]).astype(bf16)
    weights = [qkv_weight_ref[:, k * width : (k + 1) * width] for k in range(3)]
    q, k, v = [
        (matmul(normed, weights[i]) + qkv_bias_ref[:, i * width : (i + 1) * width]).astype(bf16)
        for i in range(3)
    ]
    proj_weight = proj_weight_ref[...]
    d_attn = matmul(dy, proj_weight, ((1,), (1,))).astype(bf16)
    per_tile = []
    for head, heads in ((0, 4), (4, 2)):
        lanes = slice(head * head_dim, (head + heads) * head_dim)
        masks = [head_lanes(heads * head_dim, h) for h in range(heads)]
        masks_b = [m.astype(bf16) for m in masks]
        qt, kt, vt, at = q[:, lanes], k[:, lanes], v[:, lanes], d_attn[:, lanes]
        q_stack = jnp.concatenate([qt * m for m in masks_b], axis=0)
        a_stack = jnp.concatenate([at * m for m in masks_b], axis=0)

        def by_head(stacked):
            total = stacked[:COUNT] * masks[0]
            for h in range(1, heads):
                total = total + stacked[h * COUNT : (h + 1) * COUNT] * masks[h]
            return total

        rows = slice(head * COUNT, (head + heads) * COUNT)
        scores = matmul(q_stack, kt, ((1,), (1,))) * scale + add_ref[rows, :]
        top = jnp.max(scores, axis=-1, keepdims=True)
        e = jnp.exp(scores - top)
        probs_f = e * (1.0 / jnp.sum(e, axis=-1, keepdims=True))
        probs = probs_f.astype(bf16)
        attn = by_head(matmul(probs, vt)).astype(bf16)
        d_probs = matmul(a_stack, vt, ((1,), (1,)))
        d_scores = probs_f * (d_probs - jnp.sum(probs_f * d_probs, axis=-1, keepdims=True))
        d_bias_ref[rows, :] = d_scores if prior is None else d_scores + prior[rows, :]
        d_scores_b = d_scores.astype(bf16)
        d_v = matmul(probs, a_stack, ((0,), (0,))).astype(bf16)
        d_q = (by_head(matmul(d_scores_b, kt)) * scale).astype(bf16)
        d_k = (matmul(d_scores_b, q_stack, ((0,), (0,))) * scale).astype(bf16)
        per_tile.append((attn, d_q, d_k, d_v))
    attn, d_q, d_k, d_v = [jnp.concatenate([t[i] for t in per_tile], axis=1) for i in range(4)]
    out = xf + matmul(attn, proj_weight) + proj_bias_ref[...]
    scatter_window(0, out, x_tiles, *grids)
    d_parts = (d_q, d_k, d_v)
    d_normed = sum(matmul(d_parts[i], weights[i], ((1,), (1,))) for i in range(3))
    d_xhat = d_normed * gain
    d_centered = inverse * (
        d_xhat
        - jnp.mean(d_xhat, axis=-1, keepdims=True)
        - xhat * jnp.mean(d_xhat * xhat, axis=-1, keepdims=True)
    )
    scatter_window(1, dyf + d_centered, dy_tiles, *grids)
    d_qkv = jnp.concatenate(d_parts, axis=1)
    qkv_weight_grad = matmul(normed, d_qkv, ((0,), (0,)))
    proj_weight_grad = matmul(attn, dy, ((0,), (0,)))
    matrix = jnp.concatenate([qkv_weight_grad, proj_weight_grad], axis=1)
    vector = jnp.concatenate(
        [
            jnp.sum(d_normed * xhat, axis=0, keepdims=True),
            jnp.sum(d_normed, axis=0, keepdims=True),
            jnp.sum(d_qkv.astype(f32), axis=0, keepdims=True),
            jnp.sum(dyf, axis=0, keepdims=True),
        ],
        axis=1,
    )
    return matrix, vector


def first_kernel(own, cot, lat, *rest):
    params, (add, upper, bottom, d_bias, matrix_ref, vector_ref, x_tiles, dy_tiles) = rest[:6], rest[6:]
    matrix_ref[...], vector_ref[...] = attend(
        x_tiles, dy_tiles, own, cot, lat, (), HALF_LON, params, add, d_bias, None, upper, bottom, None
    )


def second_kernel(place_ref, own, cot, lat, corner, lon, *rest):
    params, (add, prior, prior_matrix, prior_vector) = rest[:6], rest[6:10]
    upper, bottom, side, mine_ref, other_ref, x_tiles, dy_tiles, d_bias, parts_ref = rest[10:]
    first = own.shape[2] - HALF_LON
    matrix, vector = attend(
        x_tiles, dy_tiles, own, cot, lat, (lon, corner), first, params, add, d_bias, prior, upper, bottom, side
    )
    skewed = jnp.zeros((HEADS * GROUP, SPREAD), f32)
    for i in range(WLON):
        part = jnp.concatenate(
            [d_bias[h * COUNT + i * GROUP : h * COUNT + (i + 1) * GROUP, :] for h in range(HEADS)],
            axis=0,
        )
        part = jnp.concatenate([part, jnp.zeros((HEADS * GROUP, SPREAD - COUNT), f32)], axis=1)
        shift = GROUP * (WLON - 1 - i)
        skewed = skewed + (part if shift == 0 else pltpu.roll(part, shift, 1))
    pack(parts_ref, matrix + prior_matrix[...], vector + prior_vector[...], skewed)
    core = place_ref[1]
    mine_ref[...] = parts_ref[core]
    other_ref[...] = parts_ref[1 - core].astype(bf16)


def table_slots(pieces, pairs):
    slots = []
    for p in range(pairs):
        if p < pieces:
            slots.append((p, 0, p, 4 * LANES))
        else:
            slots.append((p - pieces, 2 * LANES, p - pieces + (pairs - pieces), 2 * LANES))
    return slots


def pack(parts_ref, matrix, vector, skewed):
    cores, half = parts_ref.shape[:2]
    pieces = cores * half
    rows = matrix.shape[0] // pieces
    for d in range(pieces):
        parts_ref[d % cores, d // cores, 0:rows, :] = matrix[d * rows : (d + 1) * rows, :]
        parts_ref[d % cores, d // cores, rows:8, :] = jnp.zeros((8 - rows, matrix.shape[1]), f32)
    for p, (d, at, d2, at2) in enumerate(table_slots(pieces, skewed.shape[0] // 2)):
        pair = slice(2 * p, 2 * p + 2)
        parts_ref[d % cores, d // cores, rows : rows + 2, at : at + 2 * LANES] = skewed[pair, : 2 * LANES]
        parts_ref[d2 % cores, d2 // cores, rows : rows + 2, at2 : at2 + LANES] = skewed[pair, 2 * LANES :]
    for d in range(vector.shape[1] // LANES):
        parts_ref[d % cores, d // cores, rows : rows + 1, 5 * LANES :] = vector[
            :, d * LANES : (d + 1) * LANES
        ]


def unpack_kernel(
    norm_by,
    place_ref,
    mine_ref,
    other_ref,
    qkv_ref,
    proj_ref,
    table_ref,
    gain_ref,
    shift_ref,
    qkv_bias_ref,
    proj_bias_ref,
    wide_ref,
    skewed_ref,
):
    core = place_ref[1]
    wide_ref[core] = mine_ref[...].astype(f32)
    wide_ref[1 - core] = other_ref[...].astype(f32)
    cores, half = wide_ref.shape[:2]
    pieces = cores * half
    width, wide = qkv_ref.shape
    rows = width // pieces
    for d in range(pieces):
        piece = wide_ref[d % cores, d // cores, 0:rows, :] * norm_by
        qkv_ref[d * rows : (d + 1) * rows, :] = piece[:, :wide]
        proj_ref[d * rows : (d + 1) * rows, :] = piece[:, wide:]
    for p, (d, at, d2, at2) in enumerate(table_slots(pieces, HEADS * GROUP // 2)):
        for t in range(2):
            lanes = slice(at + t * LANES, at + (t + 1) * LANES)
            skewed_ref[t, 2 * p : 2 * p + 2, :] = wide_ref[
                d % cores, d // cores, rows : rows + 2, lanes
            ]
        skewed_ref[2, 2 * p : 2 * p + 2, :] = wide_ref[
            d2 % cores, d2 // cores, rows : rows + 2, at2 : at2 + LANES
        ]
    skewed = jnp.concatenate(
        [strided_rows(skewed_ref, a, HEADS, GROUP) for a in range(GROUP)], axis=0
    )
    skewed = (skewed * bias_factor).astype(bf16)
    sides = [matmul(skewed, order_of_skew(z).astype(bf16), ((1,), (1,))) for z in range(WZ)]
    table = jnp.concatenate(
        [
            sides[zm][(zn * WLAT + ln) * HEADS : (zn * WLAT + ln + 1) * HEADS]
            for zn in range(WZ)
            for zm in range(WZ)
            for ln in range(WLAT)
        ],
        axis=1,
    )
    for h in range(HEADS):
        table_ref[0, h] = table[h : h + 1]
    count = (3 * width + wide) // LANES
    vector = jnp.concatenate(
        [wide_ref[d % cores, d // cores, rows : rows + 1, 5 * LANES :] for d in range(count)], axis=1
    )
    vector = vector * norm_by
    gain_ref[...] = vector[:, :width]
    shift_ref[...] = vector[:, width : 2 * width]
    qkv_bias_ref[...] = vector[0, 2 * width : 2 * width + wide]
    proj_bias_ref[...] = vector[:, 2 * width + wide :]


VMEM_LIMIT = 48 * 1024 * 1024


def call(kernel, out_shape, name, scalars, arrays, scratch=(), in_space=pltpu.VMEM, out_spaces=None, cost=None):
    smem = pl.BlockSpec(memory_space=pltpu.SMEM)
    vmem = pl.BlockSpec(memory_space=in_space)
    if out_spaces is None:
        out_specs = jax.tree.map(lambda _: pl.BlockSpec(memory_space=pltpu.VMEM), out_shape)
    else:
        out_specs = jax.tree.map(lambda space: pl.BlockSpec(memory_space=space), out_spaces)
    return pl.pallas_call(
        kernel,
        out_shape=out_shape,
        in_specs=[smem] * len(scalars) + [vmem] * len(arrays),
        out_specs=out_specs,
        scratch_shapes=scratch,
        compiler_params=pltpu.CompilerParams(vmem_limit_bytes=VMEM_LIMIT),
        cost_estimate=cost,
        name=name,
    )(*scalars, *arrays)


def struct(shape, dtype=f32):
    return jax.ShapeDtypeStruct(shape, dtype)


CORES = 2


def swap_cores(value):
    count = lax.axis_size("lon")
    return lax.ppermute(value, "lon", [(i, i ^ 1) for i in range(count)])


def same_core():
    count = lax.axis_size("lon")
    return [list(range(c, count, CORES)) for c in range(CORES)]


def to_neighbour(value, axes, steps):
    counts = [lax.axis_size(a) for a in axes]
    if len(axes) == 1:
        n = counts[0]
        return lax.ppermute(value, axes[0], [(i, (i + steps[0]) % n) for i in range(n)])
    na, nb = counts
    pairs = [
        (a * nb + b, (a + steps[0]) % na * nb + (b + steps[1]) % nb)
        for a in range(na)
        for b in range(nb)
    ]
    return lax.ppermute(value, axes, pairs)


def local(
    tokens,
    cotangent,
    norm_gain_vector,
    norm_bias_vector,
    qkv_weight,
    qkv_bias,
    proj_weight,
    proj_bias,
    earth_bias,
    lat_valid,
):
    levels, rows, cols, width = tokens.shape
    wide = qkv_weight.shape[1]
    lat_count = lax.axis_size("lat")
    lon_count = lax.axis_size("lon")
    total = levels * rows * cols
    place = jnp.stack([lax.axis_index("lat"), lax.axis_index("lon") % CORES]).astype(jnp.int32)
    def packed(count, columns):
        return struct((levels, count, 3, columns, LANES), bf16)

    cuts = lax.optimization_barrier(tuple(a[:, :HALF_LAT] for a in (tokens, cotangent)))
    near, rest = call(
        cut_kernel,
        (packed(HALF_LAT, HALF_LON), packed(HALF_LAT, cols - HALF_LON)),
        "cut",
        [],
        list(cuts),
        cost=pl.CostEstimate(flops=5_000_000_000, bytes_accessed=2_000_000, transcendentals=0),
    )
    side = packed_lines(*[a[:, HALF_LAT:, :HALF_LON] for a in (tokens, cotangent)])
    lat_halo = to_neighbour(rest, ("lat",), (-1,))
    table = earth_bias.transpose(0, 2, 1, 3)
    params = [norm_gain_vector, norm_bias_vector, qkv_weight, qkv_bias, proj_weight, proj_bias]
    rows_of = [(1, p.size) if p.ndim == 1 else p.shape for p in params]
    add, *params = call(
        bias_kernel,
        (struct((HEADS * COUNT + 8, COUNT)), *[struct(r, p.dtype) for r, p in zip(rows_of, params)]),
        "bias",
        [place, lat_valid],
        [table, *params],
        [
            pltpu.VMEM((WZ, HEADS * GROUP, SIDE), f32),
            pltpu.VMEM((SPREAD // LANES, 8 * GROUP, LANES), f32),
        ],
    )
    near, side, add = lax.optimization_barrier((near, side, add))
    corner = to_neighbour(near, ("lat", "lon"), (-1, -1))
    lon_halo = to_neighbour(side, ("lon",), (-1,))

    half = lon_count // CORES
    across = wide + width
    upper = struct((2, levels, rows - HALF_LAT, WLON, width))
    bottom = packed(HALF_LAT, WLON)
    side = packed(rows, WLON - HALF_LON)
    tiles = pltpu.VMEM((pl.cdiv(width, LANES), 16 * GROUP, LANES), f32)
    d_bias = (HEADS * COUNT, COUNT)
    upper_a, bottom_a, *prior = call(
        first_kernel,
        (upper, bottom, struct(d_bias), struct((width, across)), struct((1, 3 * width + wide))),
        "first",
        [],
        [tokens, cotangent, lat_halo, *params, add],
        [tiles, tiles],
    )
    upper_b, bottom_b, side_b, mine, other = call(
        second_kernel,
        (upper, bottom, side, struct((half, 8, across)), struct((half, 8, across), bf16)),
        "second",
        [place],
        [tokens, cotangent, lat_halo, corner, lon_halo, *params, add, *prior],
        [tiles, tiles, pltpu.VMEM((HEADS * COUNT + 8, COUNT), f32), pltpu.VMEM((CORES, half, 8, across), f32)],
    )

    pieces = struct((half, 8, across), bf16)
    piece = struct((8, across), bf16)
    pair = call(pair_kernel, pieces, "pair", [], [mine, swap_cores(other)])
    pair = lax.all_to_all(pair, "lon", 0, 0, axis_index_groups=same_core())
    left = to_neighbour(side_b, ("lon",), (1,))
    pair, left = lax.optimization_barrier((pair, left))
    by_lon, pair = call(
        lon_kernel,
        (piece, struct((lat_count, 8, across), bf16)),
        "lon",
        [],
        [pair],
    )
    by_lat = lax.all_to_all(pair, "lat", 0, 0)
    inner = rows - HALF_LAT
    bottom = [left[:, inner:], bottom_a, bottom_b[:, :, :, :HALF_LON]]
    top = to_neighbour(jnp.concatenate(bottom, axis=3), ("lat",), (1,))

    def lat_sum(*refs):
        lat_kernel(width // lon_count, *refs)

    mine = call(
        lat_sum,
        pieces,
        "lat",
        [],
        [by_lat, by_lon],
    )
    mine = lax.all_to_all(mine, "lon", 0, 0, axis_index_groups=same_core())
    block_out, token_grad = call(
        owned_kernel,
        (struct(tokens.shape), struct(tokens.shape)),
        "owned",
        [],
        [top, left, upper_a, upper_b],
        cost=pl.CostEstimate(flops=5000000000, bytes_accessed=2_000_000, transcendentals=0),
    )
    mine, block_out, token_grad = lax.optimization_barrier((mine, block_out, token_grad))
    other = swap_cores(mine)

    norm_by = 1.0 / math.sqrt(total * lat_count * lon_count)

    def unpack(*refs):
        unpack_kernel(norm_by, *refs)

    qkv_weight_grad, proj_weight_grad, table, gain, shift, qkv_bias_grad, proj_bias_grad = call(
        unpack,
        (
            struct((width, wide)),
            struct((width, width)),
            struct(table.shape),
            struct((1, width)),
            struct((1, width)),
            struct((wide,)),
            struct((1, width)),
        ),
        "unpack",
        [place],
        [mine, other],
        [pltpu.VMEM((CORES, half, 8, across), f32), pltpu.VMEM((SPREAD // LANES, 8 * GROUP, LANES), f32)],
    )
    return (
        block_out,
        token_grad,
        gain[0],
        shift[0],
        qkv_weight_grad,
        qkv_bias_grad,
        proj_weight_grad,
        proj_bias_grad[0],
        table.transpose(0, 2, 1, 3),
    )


def solution(mesh):
    placed = (
        P(None, "lat", "lon", None),
        P(None, "lat", "lon", None),
        P(),
        P(),
        P(),
        P(),
        P(),
        P(),
        P(None, "lat", None, None),
        P(),
    )
    return jax.shard_map(
        local,
        mesh=mesh,
        in_specs=placed,
        out_specs=(
            P(None, "lat", "lon", None),
            P(None, "lat", "lon", None),
            P(),
            P(),
            P(),
            P(),
            P(),
            P(),
            P(None, "lat", None, None),
        ),
        check_vma=False,
    )
```

```python
import math

import jax
import jax.numpy as jnp
from jax import lax
from jax.experimental import pallas as pl
from jax.experimental.pallas import tpu as pltpu
from jax.sharding import PartitionSpec as P

HEADS = 6
WZ = 2
WLAT = 6
WLON = 12

HALF_LAT = WLAT // 2
HALF_LON = WLON // 2
GROUP = WZ * WLAT
COUNT = GROUP * WLON
DIFFS = 2 * WLON - 1
SIDE = WLAT * DIFFS
LANES = 128
SPREAD = 3 * LANES

mask_fill = -10000.0
epsilon = 1e-05
bias_factor = 8.0

f32 = jnp.float32
bf16 = jnp.bfloat16


def matmul(a, b, dims=((1,), (0,)), precision=None):
    return lax.dot_general(a, b, (dims, ((), ())), preferred_element_type=f32, precision=precision)


def order_of_skew(z):
    row = lax.broadcasted_iota(jnp.int32, (SIDE, 1), 0)
    lat = sum((row >= k * DIFFS).astype(jnp.int32) for k in range(1, WLAT))
    diff = row - DIFFS * lat
    target = (DIFFS - 1 - diff) * GROUP + z * WLAT + lat
    return (lax.broadcasted_iota(jnp.int32, (SIDE, SPREAD), 1) == target).astype(f32)


def to_tiles(tiles_ref, value):
    for t in range(tiles_ref.shape[0]):
        part = value[:, t * LANES : (t + 1) * LANES]
        tiles_ref[t, : part.shape[0], : part.shape[1]] = part


def strided_rows(tiles_ref, start, count, stride):
    tiles = [tiles_ref[t, pl.ds(start, count, stride=stride), :] for t in range(tiles_ref.shape[0])]
    return jnp.concatenate(tiles, axis=1)


def bias_kernel(
    place_ref,
    valid_ref,
    table_ref,
    *rest,
):
    params, add_ref, params_out, (sides_ref, skewed_ref) = rest[:6], rest[6], rest[7:13], rest[13:]
    for ref, to in zip(params, params_out):
        to[...] = ref[...].reshape(to.shape)
    for zn in range(WZ):
        for zm in range(WZ):
            for ln in range(WLAT):
                at = ((zn * WZ + zm) * WLAT + ln) * SIDE
                row = (zn * WLAT + ln) * HEADS
                for h in range(HEADS):
                    sides_ref[zm, row + h : row + h + 1, :] = table_ref[0, h, :, at : at + SIDE]
    skewed = 0.0
    for z in range(WZ):
        left = sides_ref[z]
        parts = []
        for _ in range(3):
            parts.append(left.astype(bf16))
            left = left - parts[-1].astype(f32)
        placed = matmul(jnp.concatenate(parts, axis=0), order_of_skew(z).astype(bf16))
        high, middle, low = [placed[k * HEADS * GROUP : (k + 1) * HEADS * GROUP] for k in range(3)]
        skewed = skewed + ((high + middle) + low)
    to_tiles(skewed_ref, skewed)
    skewed = jnp.concatenate(
        [strided_rows(skewed_ref, h, GROUP, HEADS) for h in range(HEADS)], axis=0
    )
    masked = mask_of_windows(place_ref[0], valid_ref)
    for i in range(WLON):
        shift = (GROUP * (i - WLON + 1)) % SPREAD
        rolled = skewed if shift == 0 else pltpu.roll(skewed, shift, 1)
        for h in range(HEADS):
            add_ref[h * COUNT + i * GROUP : h * COUNT + (i + 1) * GROUP, :] = (
                rolled[h * GROUP : (h + 1) * GROUP, :COUNT] + masked
            )


def mask_of_windows(band, valid_ref):
    total_rows = valid_ref.shape[0]

    def place_of(shape, axis):
        position = lax.broadcasted_iota(jnp.int32, shape, axis)
        group = position - GROUP * sum(
            (position >= GROUP * k).astype(jnp.int32) for k in range(1, shape[axis] // GROUP)
        )
        level = (group >= WLAT).astype(jnp.int32)
        row_in = group - WLAT * level
        row = band * WLAT + row_in
        region = (row >= total_rows - WLAT).astype(jnp.int32) + (
            row >= total_rows - HALF_LAT
        ).astype(jnp.int32)
        return level, row_in, region

    level_n, _, region_n = place_of((GROUP, COUNT), 0)
    level_m, row_m, region_m = place_of((GROUP, COUNT), 1)
    key_ok = jnp.zeros((GROUP, COUNT), jnp.int32)
    for r in range(WLAT):
        at = lax.rem(band * WLAT + r + HALF_LAT, total_rows)
        key_ok = jnp.where(row_m == r, valid_ref[at], key_ok)
    allowed = (level_n == level_m) & (region_n == region_m) & (key_ok == 1)
    return jnp.where(allowed, f32(0.0), f32(mask_fill))


def head_lanes(width, h):
    lane = lax.broadcasted_iota(jnp.int32, (1, width), 1)
    return (lane // 32 == h).astype(f32)


def unpacked(packed_ref, at, kind):
    low = packed_ref[(*at, kind)].astype(f32)
    high = packed_ref[(*at, 2)].astype(f32)
    return [low, high if kind == 0 else pltpu.roll(high, LANES // 2, 1)]


def gather_window(kind, first, own_ref, lat_ref, ends_refs, tiles_ref):
    levels, rows, cols, width = own_ref.shape
    inner = rows - HALF_LAT
    for z in range(levels):
        src = (z + WZ // 2) % levels
        for r in range(rows):
            if r < inner:
                line = own_ref[src, HALF_LAT + r].astype(f32)
                high = jnp.concatenate(
                    [line[:, LANES:], jnp.zeros((cols, -width % LANES), f32)], axis=1
                )
                line = [part[first:] for part in (line[:, :LANES], high)]
            else:
                line = unpacked(lat_ref, (src, r - inner), kind)
                line = [part[first - HALF_LON :] for part in line]
            if not ends_refs:
                line = [part[:WLON] for part in line]
            else:
                ends = unpacked(ends_refs[r // inner], (src, r % inner), kind)
                line = [jnp.concatenate([p, e], axis=0) for p, e in zip(line, ends)]
            for t, part in enumerate(line):
                tiles_ref[t, pl.ds(z * rows + r, WLON, stride=GROUP), :] = part
    return jnp.concatenate([tiles_ref[t, :COUNT, :] for t in range(2)], axis=1)[:, :width]


def pack_line(packed_ref, at, kind, low, high):
    packed_ref[(*at, kind)] = low.astype(bf16)
    half = LANES // 2
    if kind == 0:
        packed_ref[(*at, 2, slice(None), slice(0, half))] = high[:, :half].astype(bf16)
    else:
        moved = pltpu.roll(high, half, 1)
        packed_ref[(*at, 2, slice(None), slice(half, LANES))] = moved[:, half:].astype(bf16)


def scatter_window(kind, result, tiles_ref, upper_ref, bottom_ref, side_ref):
    levels, inner = upper_ref.shape[1:3]
    width = result.shape[1]
    to_tiles(tiles_ref, result)
    for z in range(levels):
        to = (z + WZ // 2) % levels
        for r in range(WLAT):
            low, high = [
                tiles_ref[t, pl.ds(z * WLAT + r, WLON, stride=GROUP), :] for t in range(2)
            ]
            if side_ref is not None:
                pack_line(side_ref, (to, r), kind, low[HALF_LON:], high[HALF_LON:])
            if r < inner:
                upper_ref[kind, to, r] = jnp.concatenate([low, high], axis=1)[:, :width]
            else:
                pack_line(bottom_ref, (to, r - inner), kind, low, high)


def packed_lines(tokens, cotangent):
    high = jnp.concatenate([tokens[..., LANES:], cotangent[..., LANES:]], axis=-1)
    return jnp.stack([tokens[..., :LANES], cotangent[..., :LANES], high], axis=2)


def cut_kernel(tokens_ref, cot_ref, near_ref, rest_ref):
    for z in range(near_ref.shape[0]):
        for r in range(near_ref.shape[1]):
            lines = [ref[z, r].astype(f32) for ref in (tokens_ref, cot_ref)]
            high = jnp.concatenate([line[:, LANES:] for line in lines], axis=1)
            for k, part in enumerate([line[:, :LANES] for line in lines] + [high]):
                near_ref[z, r, k] = part[:HALF_LON].astype(bf16)
                rest_ref[z, r, k] = part[HALF_LON:].astype(bf16)


def owned_kernel(top_ref, left_ref, upper_a_ref, upper_b_ref, out_ref, grad_ref):
    levels, rows, cols, width = out_ref.shape
    for kind, ref in enumerate((out_ref, grad_ref)):
        for z in range(levels):
            for r in range(rows):
                if r < HALF_LAT:
                    ref[z, r] = jnp.concatenate(unpacked(top_ref, (z, r), kind), axis=1)[:, :width]
                else:
                    line = unpacked(left_ref, (z, r - HALF_LAT), kind)
                    own = [u[kind, z, r - HALF_LAT] for u in (upper_a_ref, upper_b_ref)]
                    parts = [jnp.concatenate(line, axis=1)[:, :width], own[0], own[1][:HALF_LON]]
                    ref[z, r] = jnp.concatenate(parts, axis=0)


def pair_kernel(mine_ref, other_ref, sum_ref):
    sum_ref[...] = (mine_ref[...] + other_ref[...].astype(f32)).astype(bf16)


def spread(piece, out_ref):
    for d in range(out_ref.shape[0]):
        out_ref[d] = piece


def sum_pieces(pieces_ref):
    total = pieces_ref[0].astype(f32)
    for d in range(1, pieces_ref.shape[0]):
        total = total + pieces_ref[d].astype(f32)
    return total


def lon_kernel(pieces_ref, piece_ref, out_ref):
    total = sum_pieces(pieces_ref)
    piece_ref[...] = total.astype(bf16)
    keep = out_ref.shape[2]
    ends = [total[r : r + 1, keep:] for r in range(7)] + [jnp.zeros((1, LANES), f32)] * 3
    last = [jnp.concatenate(ends[k : k + 5], axis=1) for k in (0, 5)]
    spread(jnp.concatenate([total[:6, :keep], *last], axis=0).astype(bf16), out_ref)


def lat_kernel(rows, pieces_ref, by_lon_ref, out_ref):
    total = sum_pieces(pieces_ref)
    keep = total.shape[1]
    ends = [
        total[6 + k // 5 : 7 + k // 5, k % 5 * LANES : (k % 5 + 1) * LANES] for k in range(8)
    ]
    start = jnp.concatenate([total[:6], jnp.zeros((2, keep), f32)], axis=0)
    total = jnp.concatenate([start, jnp.concatenate(ends, axis=0)], axis=1)
    shape = by_lon_ref.shape
    row = lax.broadcasted_iota(jnp.int32, shape, 0)
    column = lax.broadcasted_iota(jnp.int32, shape, 1)
    is_table = (row >= rows) & (column < keep)
    total = jnp.where(is_table, by_lon_ref[...].astype(f32), total)
    spread(total.astype(bf16), out_ref)


def attend(
    x_tiles, dy_tiles, own, cot, lat, ends, first, params, add_ref, d_bias_ref, prior, *grids
):
    gain_ref, shift_ref, qkv_weight_ref, qkv_bias_ref, proj_weight_ref, proj_bias_ref = params
    width = own.shape[-1]
    head_dim = width // HEADS
    scale = 1.0 / math.sqrt(head_dim)
    xf = gather_window(0, first, own, lat, ends, x_tiles)
    dyf = gather_window(1, first, cot, lat, ends, dy_tiles)
    dy = dyf.astype(bf16)
    mean_value = jnp.mean(xf, axis=-1, keepdims=True)
    centered = xf - mean_value
    inverse = lax.rsqrt(jnp.mean(centered * centered, axis=-1, keepdims=True) + epsilon)
    xhat = centered * inverse
    gain = gain_ref[...]
    normed = (xhat * gain + shift_ref[...]).astype(bf16)
    weights = [qkv_weight_ref[:, k * width : (k + 1) * width] for k in range(3)]
    q, k, v = [
        (matmul(normed, weights[i]) + qkv_bias_ref[:, i * width : (i + 1) * width]).astype(bf16)
        for i in range(3)
    ]
    proj_weight = proj_weight_ref[...]
    d_attn = matmul(dy, proj_weight, ((1,), (1,))).astype(bf16)
    per_tile = []
    for head, heads in ((0, 4), (4, 2)):
        lanes = slice(head * head_dim, (head + heads) * head_dim)
        masks = [head_lanes(heads * head_dim, h) for h in range(heads)]
        masks_b = [m.astype(bf16) for m in masks]
        qt, kt, vt, at = q[:, lanes], k[:, lanes], v[:, lanes], d_attn[:, lanes]
        q_stack = jnp.concatenate([qt * m for m in masks_b], axis=0)
        a_stack = jnp.concatenate([at * m for m in masks_b], axis=0)

        def by_head(stacked):
            total = stacked[:COUNT] * masks[0]
            for h in range(1, heads):
                total = total + stacked[h * COUNT : (h + 1) * COUNT] * masks[h]
            return total

        rows = slice(head * COUNT, (head + heads) * COUNT)
        scores = matmul(q_stack, kt, ((1,), (1,))) * scale + add_ref[rows, :]
        top = jnp.max(scores, axis=-1, keepdims=True)
        e = jnp.exp(scores - top)
        probs_f = e * (1.0 / jnp.sum(e, axis=-1, keepdims=True))
        probs = probs_f.astype(bf16)
        attn = by_head(matmul(probs, vt)).astype(bf16)
        d_probs = matmul(a_stack, vt, ((1,), (1,)))
        d_scores = probs_f * (d_probs - jnp.sum(probs_f * d_probs, axis=-1, keepdims=True))
        d_bias_ref[rows, :] = d_scores if prior is None else d_scores + prior[rows, :]
        d_scores_b = d_scores.astype(bf16)
        d_v = matmul(probs, a_stack, ((0,), (0,))).astype(bf16)
        d_q = (by_head(matmul(d_scores_b, kt)) * scale).astype(bf16)
        d_k = (matmul(d_scores_b, q_stack, ((0,), (0,))) * scale).astype(bf16)
        per_tile.append((attn, d_q, d_k, d_v))
    attn, d_q, d_k, d_v = [jnp.concatenate([t[i] for t in per_tile], axis=1) for i in range(4)]
    out = xf + matmul(attn, proj_weight) + proj_bias_ref[...]
    scatter_window(0, out, x_tiles, *grids)
    d_parts = (d_q, d_k, d_v)
    d_normed = sum(matmul(d_parts[i], weights[i], ((1,), (1,))) for i in range(3))
    d_xhat = d_normed * gain
    d_centered = inverse * (
        d_xhat
        - jnp.mean(d_xhat, axis=-1, keepdims=True)
        - xhat * jnp.mean(d_xhat * xhat, axis=-1, keepdims=True)
    )
    scatter_window(1, dyf + d_centered, dy_tiles, *grids)
    d_qkv = jnp.concatenate(d_parts, axis=1)
    qkv_weight_grad = matmul(normed, d_qkv, ((0,), (0,)))
    proj_weight_grad = matmul(attn, dy, ((0,), (0,)))
    matrix = jnp.concatenate([qkv_weight_grad, proj_weight_grad], axis=1)
    vector = jnp.concatenate(
        [
            jnp.sum(d_normed * xhat, axis=0, keepdims=True),
            jnp.sum(d_normed, axis=0, keepdims=True),
            jnp.sum(d_qkv.astype(f32), axis=0, keepdims=True),
            jnp.sum(dyf, axis=0, keepdims=True),
        ],
        axis=1,
    )
    return matrix, vector


def first_kernel(own, cot, lat, *rest):
    params, (add, upper, bottom, d_bias, matrix_ref, vector_ref, x_tiles, dy_tiles) = rest[:6], rest[6:]
    matrix_ref[...], vector_ref[...] = attend(
        x_tiles, dy_tiles, own, cot, lat, (), HALF_LON, params, add, d_bias, None, upper, bottom, None
    )


def second_kernel(place_ref, own, cot, lat, corner, lon, *rest):
    params, (add, prior, prior_matrix, prior_vector) = rest[:6], rest[6:10]
    upper, bottom, side, mine_ref, other_ref, x_tiles, dy_tiles, d_bias, parts_ref = rest[10:]
    first = own.shape[2] - HALF_LON
    matrix, vector = attend(
        x_tiles, dy_tiles, own, cot, lat, (lon, corner), first, params, add, d_bias, prior, upper, bottom, side
    )
    skewed = jnp.zeros((HEADS * GROUP, SPREAD), f32)
    for i in range(WLON):
        part = jnp.concatenate(
            [d_bias[h * COUNT + i * GROUP : h * COUNT + (i + 1) * GROUP, :] for h in range(HEADS)],
            axis=0,
        )
        part = jnp.concatenate([part, jnp.zeros((HEADS * GROUP, SPREAD - COUNT), f32)], axis=1)
        shift = GROUP * (WLON - 1 - i)
        skewed = skewed + (part if shift == 0 else pltpu.roll(part, shift, 1))
    pack(parts_ref, matrix + prior_matrix[...], vector + prior_vector[...], skewed)
    core = place_ref[1]
    mine_ref[...] = parts_ref[core]
    other_ref[...] = parts_ref[1 - core].astype(bf16)


def table_slots(pieces, pairs):
    slots = []
    for p in range(pairs):
        if p < pieces:
            slots.append((p, 0, p, 4 * LANES))
        else:
            slots.append((p - pieces, 2 * LANES, p - pieces + (pairs - pieces), 2 * LANES))
    return slots


def pack(parts_ref, matrix, vector, skewed):
    cores, half = parts_ref.shape[:2]
    pieces = cores * half
    rows = matrix.shape[0] // pieces
    for d in range(pieces):
        parts_ref[d % cores, d // cores, 0:rows, :] = matrix[d * rows : (d + 1) * rows, :]
        parts_ref[d % cores, d // cores, rows:8, :] = jnp.zeros((8 - rows, matrix.shape[1]), f32)
    for p, (d, at, d2, at2) in enumerate(table_slots(pieces, skewed.shape[0] // 2)):
        pair = slice(2 * p, 2 * p + 2)
        parts_ref[d % cores, d // cores, rows : rows + 2, at : at + 2 * LANES] = skewed[pair, : 2 * LANES]
        parts_ref[d2 % cores, d2 // cores, rows : rows + 2, at2 : at2 + LANES] = skewed[pair, 2 * LANES :]
    for d in range(vector.shape[1] // LANES):
        parts_ref[d % cores, d // cores, rows : rows + 1, 5 * LANES :] = vector[
            :, d * LANES : (d + 1) * LANES
        ]


def unpack_kernel(
    norm_by,
    place_ref,
    mine_ref,
    other_ref,
    qkv_ref,
    proj_ref,
    table_ref,
    gain_ref,
    shift_ref,
    qkv_bias_ref,
    proj_bias_ref,
    wide_ref,
    skewed_ref,
):
    core = place_ref[1]
    wide_ref[core] = mine_ref[...].astype(f32)
    wide_ref[1 - core] = other_ref[...].astype(f32)
    cores, half = wide_ref.shape[:2]
    pieces = cores * half
    width, wide = qkv_ref.shape
    rows = width // pieces
    for d in range(pieces):
        piece = wide_ref[d % cores, d // cores, 0:rows, :] * norm_by
        qkv_ref[d * rows : (d + 1) * rows, :] = piece[:, :wide]
        proj_ref[d * rows : (d + 1) * rows, :] = piece[:, wide:]
    for p, (d, at, d2, at2) in enumerate(table_slots(pieces, HEADS * GROUP // 2)):
        for t in range(2):
            lanes = slice(at + t * LANES, at + (t + 1) * LANES)
            skewed_ref[t, 2 * p : 2 * p + 2, :] = wide_ref[
                d % cores, d // cores, rows : rows + 2, lanes
            ]
        skewed_ref[2, 2 * p : 2 * p + 2, :] = wide_ref[
            d2 % cores, d2 // cores, rows : rows + 2, at2 : at2 + LANES
        ]
    skewed = jnp.concatenate(
        [strided_rows(skewed_ref, a, HEADS, GROUP) for a in range(GROUP)], axis=0
    )
    skewed = (skewed * bias_factor).astype(bf16)
    sides = [matmul(skewed, order_of_skew(z).astype(bf16), ((1,), (1,))) for z in range(WZ)]
    table = jnp.concatenate(
        [
            sides[zm][(zn * WLAT + ln) * HEADS : (zn * WLAT + ln + 1) * HEADS]
            for zn in range(WZ)
            for zm in range(WZ)
            for ln in range(WLAT)
        ],
        axis=1,
    )
    for h in range(HEADS):
        table_ref[0, h] = table[h : h + 1]
    count = (3 * width + wide) // LANES
    vector = jnp.concatenate(
        [wide_ref[d % cores, d // cores, rows : rows + 1, 5 * LANES :] for d in range(count)], axis=1
    )
    vector = vector * norm_by
    gain_ref[...] = vector[:, :width]
    shift_ref[...] = vector[:, width : 2 * width]
    qkv_bias_ref[...] = vector[0, 2 * width : 2 * width + wide]
    proj_bias_ref[...] = vector[:, 2 * width + wide :]


VMEM_LIMIT = 48 * 1024 * 1024


def call(kernel, out_shape, name, scalars, arrays, scratch=(), in_space=pltpu.VMEM, out_spaces=None, cost=None):
    smem = pl.BlockSpec(memory_space=pltpu.SMEM)
    vmem = pl.BlockSpec(memory_space=in_space)
    if out_spaces is None:
        out_specs = jax.tree.map(lambda _: pl.BlockSpec(memory_space=pltpu.VMEM), out_shape)
    else:
        out_specs = jax.tree.map(lambda space: pl.BlockSpec(memory_space=space), out_spaces)
    return pl.pallas_call(
        kernel,
        out_shape=out_shape,
        in_specs=[smem] * len(scalars) + [vmem] * len(arrays),
        out_specs=out_specs,
        scratch_shapes=scratch,
        compiler_params=pltpu.CompilerParams(vmem_limit_bytes=VMEM_LIMIT),
        cost_estimate=cost,
        name=name,
    )(*scalars, *arrays)


def struct(shape, dtype=f32):
    return jax.ShapeDtypeStruct(shape, dtype)


CORES = 2


def swap_cores(value):
    count = lax.axis_size("lon")
    return lax.ppermute(value, "lon", [(i, i ^ 1) for i in range(count)])


def same_core():
    count = lax.axis_size("lon")
    return [list(range(c, count, CORES)) for c in range(CORES)]


def to_neighbour(value, axes, steps):
    counts = [lax.axis_size(a) for a in axes]
    if len(axes) == 1:
        n = counts[0]
        return lax.ppermute(value, axes[0], [(i, (i + steps[0]) % n) for i in range(n)])
    na, nb = counts
    pairs = [
        (a * nb + b, (a + steps[0]) % na * nb + (b + steps[1]) % nb)
        for a in range(na)
        for b in range(nb)
    ]
    return lax.ppermute(value, axes, pairs)


def local(
    tokens,
    cotangent,
    norm_gain_vector,
    norm_bias_vector,
    qkv_weight,
    qkv_bias,
    proj_weight,
    proj_bias,
    earth_bias,
    lat_valid,
):
    levels, rows, cols, width = tokens.shape
    wide = qkv_weight.shape[1]
    lat_count = lax.axis_size("lat")
    lon_count = lax.axis_size("lon")
    total = levels * rows * cols
    place = jnp.stack([lax.axis_index("lat"), lax.axis_index("lon") % CORES]).astype(jnp.int32)
    def packed(count, columns):
        return struct((levels, count, 3, columns, LANES), bf16)

    cuts = lax.optimization_barrier(tuple(a[:, :HALF_LAT] for a in (tokens, cotangent)))
    near, rest = call(
        cut_kernel,
        (packed(HALF_LAT, HALF_LON), packed(HALF_LAT, cols - HALF_LON)),
        "cut",
        [],
        list(cuts),
        cost=pl.CostEstimate(flops=5_000_000_000, bytes_accessed=2_000_000, transcendentals=0),
    )
    side = packed_lines(*[a[:, HALF_LAT:, :HALF_LON] for a in (tokens, cotangent)])
    lat_halo = to_neighbour(rest, ("lat",), (-1,))
    table = earth_bias.transpose(0, 2, 1, 3)
    params = [norm_gain_vector, norm_bias_vector, qkv_weight, qkv_bias, proj_weight, proj_bias]
    rows_of = [(1, p.size) if p.ndim == 1 else p.shape for p in params]
    add, *params = call(
        bias_kernel,
        (struct((HEADS * COUNT + 8, COUNT)), *[struct(r, p.dtype) for r, p in zip(rows_of, params)]),
        "bias",
        [place, lat_valid],
        [table, *params],
        [
            pltpu.VMEM((WZ, HEADS * GROUP, SIDE), f32),
            pltpu.VMEM((SPREAD // LANES, 8 * GROUP, LANES), f32),
        ],
    )
    near, side, add = lax.optimization_barrier((near, side, add))
    corner = to_neighbour(near, ("lat", "lon"), (-1, -1))
    lon_halo = to_neighbour(side, ("lon",), (-1,))

    half = lon_count // CORES
    across = wide + width
    upper = struct((2, levels, rows - HALF_LAT, WLON, width))
    bottom = packed(HALF_LAT, WLON)
    side = packed(rows, WLON - HALF_LON)
    tiles = pltpu.VMEM((pl.cdiv(width, LANES), 16 * GROUP, LANES), f32)
    d_bias = (HEADS * COUNT, COUNT)
    upper_a, bottom_a, *prior = call(
        first_kernel,
        (upper, bottom, struct(d_bias), struct((width, across)), struct((1, 3 * width + wide))),
        "first",
        [],
        [tokens, cotangent, lat_halo, *params, add],
        [tiles, tiles],
    )
    upper_b, bottom_b, side_b, mine, other = call(
        second_kernel,
        (upper, bottom, side, struct((half, 8, across)), struct((half, 8, across), bf16)),
        "second",
        [place],
        [tokens, cotangent, lat_halo, corner, lon_halo, *params, add, *prior],
        [tiles, tiles, pltpu.VMEM((HEADS * COUNT + 8, COUNT), f32), pltpu.VMEM((CORES, half, 8, across), f32)],
    )

    pieces = struct((half, 8, across), bf16)
    piece = struct((8, across), bf16)
    pair = call(pair_kernel, pieces, "pair", [], [mine, swap_cores(other)])
    pair = lax.all_to_all(pair, "lon", 0, 0, axis_index_groups=same_core())
    left = to_neighbour(side_b, ("lon",), (1,))
    pair, left = lax.optimization_barrier((pair, left))
    by_lon, pair = call(
        lon_kernel,
        (piece, struct((lat_count, 8, across - LANES), bf16)),
        "lon",
        [],
        [pair],
    )
    by_lat = lax.all_to_all(pair, "lat", 0, 0)
    inner = rows - HALF_LAT
    bottom = [left[:, inner:], bottom_a, bottom_b[:, :, :, :HALF_LON]]
    top = to_neighbour(jnp.concatenate(bottom, axis=3), ("lat",), (1,))

    def lat_sum(*refs):
        lat_kernel(width // lon_count, *refs)

    mine = call(
        lat_sum,
        pieces,
        "lat",
        [],
        [by_lat, by_lon],
    )
    mine = lax.all_to_all(mine, "lon", 0, 0, axis_index_groups=same_core())
    block_out, token_grad = call(
        owned_kernel,
        (struct(tokens.shape), struct(tokens.shape)),
        "owned",
        [],
        [top, left, upper_a, upper_b],
        cost=pl.CostEstimate(flops=5000000000, bytes_accessed=2_000_000, transcendentals=0),
    )
    mine, block_out, token_grad = lax.optimization_barrier((mine, block_out, token_grad))
    other = swap_cores(mine)

    norm_by = 1.0 / math.sqrt(total * lat_count * lon_count)

    def unpack(*refs):
        unpack_kernel(norm_by, *refs)

    qkv_weight_grad, proj_weight_grad, table, gain, shift, qkv_bias_grad, proj_bias_grad = call(
        unpack,
        (
            struct((width, wide)),
            struct((width, width)),
            struct(table.shape),
            struct((1, width)),
            struct((1, width)),
            struct((wide,)),
            struct((1, width)),
        ),
        "unpack",
        [place],
        [mine, other],
        [pltpu.VMEM((CORES, half, 8, across), f32), pltpu.VMEM((SPREAD // LANES, 8 * GROUP, LANES), f32)],
    )
    return (
        block_out,
        token_grad,
        gain[0],
        shift[0],
        qkv_weight_grad,
        qkv_bias_grad,
        proj_weight_grad,
        proj_bias_grad[0],
        table.transpose(0, 2, 1, 3),
    )


def solution(mesh):
    placed = (
        P(None, "lat", "lon", None),
        P(None, "lat", "lon", None),
        P(),
        P(),
        P(),
        P(),
        P(),
        P(),
        P(None, "lat", None, None),
        P(),
    )
    return jax.shard_map(
        local,
        mesh=mesh,
        in_specs=placed,
        out_specs=(
            P(None, "lat", "lon", None),
            P(None, "lat", "lon", None),
            P(),
            P(),
            P(),
            P(),
            P(),
            P(),
            P(None, "lat", None, None),
        ),
        check_vma=False,
    )
```
